32 devices in a mesh: batch: 2 (over x), blk: 16 (over z, y, core).
Axes of the slice: x: 2, y: 2, z: 4, core: 2. Of those that a mesh axis runs over, the one named last changes fastest.
Arguments:
- layer_input: bfloat16 [2, 4, 1024, 768], P('batch', None, 'blk'), may hold values from -6 to 6
- cotangent: bfloat16 [2, 4, 1024, 768], P('batch', None, 'blk'), may hold values from -6 to 6
- doc_lengths: int32 [2, 4, 8], P('batch'), may hold values from 0 to 1024, as said below
- joined_weight: bfloat16 [768, 2304], replicated, may hold values from -0.21875 to 0.21875
- merge_weight: bfloat16 [768, 768], replicated, may hold values from -0.21875 to 0.21875
- expand_weight: bfloat16 [768, 3072], replicated, may hold values from -0.21875 to 0.21875
- shrink_weight: bfloat16 [3072, 768], replicated, may hold values from -0.109375 to 0.109375
- first_gain: float32 [768], replicated, may hold values from 0.1 to 1.9
- mixed_gain: float32 [768], replicated, may hold values from 0.1 to 1.9
- second_gain: float32 [768], replicated, may hold values from 0.1 to 1.9
- hidden_gain: float32 [3072], replicated, may hold values from 0.1 to 1.9
Outputs:
- layer_result: bfloat16 [2, 4, 1024, 768], P('batch', None, 'blk')
- input_grad: bfloat16 [2, 4, 1024, 768], P('batch', None, 'blk')
- joined_grad: float32 [768, 2304], P('blk')
- merge_grad: float32 [768, 768], P('blk')
- expand_grad: float32 [768, 3072], P('blk')
- shrink_grad: float32 [3072, 768], P('blk')
- first_grad: float32 [768], replicated
- mixed_grad: float32 [768], replicated
- second_grad: float32 [768], replicated
- hidden_grad: float32 [3072], replicated
The draws below stay inside these ranges and needn't reach their ends.
Inputs may be any that keep to these rules, and one draw needn't show every extreme that they name: `doc_lengths`: each stream's lengths sum to at most 1024; tokens after that sum are padding. In every group one stream holds a single document of 1024 tokens.
All inputs are finite; a program needn't handle non-finite values.
Results may differ from the reference program's by a relative error of at most 0.02.
Values may be sent and summed in bfloat16 or wider, within the bound.
No kernel may reach another device: no remote copies, remote signals or barrier semaphores. Data moves between devices by JAX's collectives and lax.ppermute only.
A program may use at most 192 MiB of HBM per device.

```python
import jax
import jax.numpy as jnp
from jax import lax

D = 768
FF = 3072
HEAD = 64
STREAMS = 4
DOCS = 8
MIN_DOC = 64
GROUPS = 2
STREAM_LEN = 1024


def draw_doc_lengths(key, part):
    key = jax.random.fold_in(key, 11)
    key_sizes, key_padding, key_chosen = jax.random.split(key, 3)
    upper_size = 2 * STREAM_LEN // DOCS - MIN_DOC
    drawn_sizes = jax.random.randint(key_sizes, (GROUPS, STREAMS, DOCS), MIN_DOC, upper_size + 1, dtype=jnp.int32)
    padding = jax.random.randint(key_padding, (GROUPS, STREAMS, 1), 0, MIN_DOC, dtype=jnp.int32)
    boundaries = jnp.minimum(jnp.cumsum(drawn_sizes, axis=-1), STREAM_LEN - padding)
    earlier = jnp.concatenate([jnp.zeros((GROUPS, STREAMS, 1), jnp.int32), boundaries[..., :-1]], axis=-1)
    lengths = boundaries - earlier
    chosen = jax.random.randint(key_chosen, (GROUPS, 1, 1), 0, STREAMS, dtype=jnp.int32)
    slot_index = jnp.arange(DOCS, dtype=jnp.int32)[None, None, :]
    stream_index = jnp.arange(STREAMS, dtype=jnp.int32)[None, :, None]
    whole_doc = jnp.where(slot_index == 0, STREAM_LEN, 0).astype(jnp.int32)
    return jnp.where(stream_index == chosen, whole_doc, lengths).astype(jnp.int32)


def levels(stream_key, shape, cuts, low, largest):
    level = 1.0
    for dim, parts in cuts:
        heights = jax.random.uniform(jax.random.fold_in(jax.random.fold_in(stream_key, 6), dim), (parts,), jnp.float32, low / len(cuts), largest / len(cuts))
        level = level * jnp.repeat(jnp.exp(heights), shape[dim] // parts).reshape((-1,) + (1,) * (len(shape) - 1 - dim))
    return level


def bell_draw(own_key, extent, scale, limit, cuts=(), held_as=jnp.bfloat16):
    values = jax.random.normal(own_key, extent, jnp.float32) * scale
    if len(cuts) > 0:
        values = levels(own_key, extent, cuts, -0.22, 0.18) * values
    return jnp.clip(values, min=-limit, max=limit).astype(held_as)


def setup_inputs(seed: int = 0) -> dict:
    key_list = jax.random.split(jax.random.key(seed), 12)
    layer_input = bell_draw(key_list[0], (GROUPS, STREAMS, STREAM_LEN, D), 1.0, 6.0, ((0, 2), (2, 16)))
    cotangent = bell_draw(key_list[1], (GROUPS, STREAMS, STREAM_LEN, D), 1.0, 6.0, ((0, 2), (2, 16)))
    doc_lengths = draw_doc_lengths(jax.random.fold_in(key_list[11], 71), 0)
    joined_weight = bell_draw(key_list[3], (D, 3 * D), D ** -0.5, 0.21875)
    merge_weight = bell_draw(key_list[4], (D, D), D ** -0.5, 0.21875)
    expand_weight = bell_draw(key_list[5], (D, FF), D ** -0.5, 0.21875)
    shrink_weight = bell_draw(key_list[6], (FF, D), FF ** -0.5, 0.109375)
    first_gain = jnp.clip(1.0 + 0.18 * jax.random.normal(key_list[7], (D,), jnp.float32), 0.1, 1.9)
    mixed_gain = jnp.clip(1.0 + 0.18 * jax.random.normal(key_list[8], (D,), jnp.float32), 0.1, 1.9)
    second_gain = jnp.clip(1.0 + 0.18 * jax.random.normal(key_list[9], (D,), jnp.float32), 0.1, 1.9)
    hidden_gain = jnp.clip(1.0 + 0.18 * jax.random.normal(key_list[10], (FF,), jnp.float32), 0.1, 1.9)
    return dict(layer_input=layer_input, cotangent=cotangent, doc_lengths=doc_lengths, joined_weight=joined_weight, merge_weight=merge_weight, expand_weight=expand_weight, shrink_weight=shrink_weight, first_gain=first_gain, mixed_gain=mixed_gain, second_gain=second_gain, hidden_gain=hidden_gain)


largest_value = lax.Precision.HIGHEST
big_negative = -1e+30

@jax.custom_vjp
def reduced_precision(v):
    return lax.optimization_barrier(v.astype(jnp.bfloat16)).astype(jnp.float32)

@jax.custom_vjp
def reduced_backward(v):
    return v

def low_keep(v):
    return (reduced_precision(v), None)

def low_pass(kept, grad):
    return (grad,)

def back_keep(v):
    return (v, None)

def back_low(kept, grad):
    return (reduced_precision(grad),)
reduced_precision.defvjp(low_keep, low_pass)
reduced_backward.defvjp(back_keep, back_low)

def layer_norm(values, gain):
    centred = values - lax.optimization_barrier(jnp.mean(values, axis=-1, keepdims=True))
    spread = lax.optimization_barrier(jnp.mean(centred * centred, axis=-1, keepdims=True))
    return centred * lax.rsqrt(spread + 1e-05) * gain

def document_ids(doc_lengths, positions):
    doc_ends = jnp.cumsum(doc_lengths, axis=-1)
    return lax.optimization_barrier(jnp.sum((doc_ends[..., None, :] <= positions[:, None]).astype(jnp.int32), axis=-1))

def attend(operands):
    queries, keys_all, values_all, stream_docs = operands
    length = queries.shape[0]
    head_count = queries.shape[1] // HEAD
    query_heads = queries.reshape(length, head_count, HEAD)
    key_heads = keys_all.reshape(length, head_count, HEAD)
    value_heads = values_all.reshape(length, head_count, HEAD)
    scores = reduced_backward(jnp.einsum('qhd,khd->hqk', query_heads, key_heads, precision=largest_value))
    places = jnp.arange(length, dtype=jnp.int32)
    allowed = (stream_docs[:, None] == stream_docs[None, :]) & (places[None, :] <= places[:, None])
    scores = jnp.where(allowed[None], scores, big_negative)
    peak_score = lax.optimization_barrier(jnp.max(scores, axis=-1, keepdims=True))
    weights = jnp.where(allowed[None], jnp.exp(scores - peak_score), 0.0)
    weights = weights / lax.optimization_barrier(jnp.sum(weights, axis=-1, keepdims=True))
    result = jnp.einsum('hqk,khd->qhd', reduced_precision(weights), value_heads, precision=largest_value)
    return result.reshape(length, head_count * HEAD)

def reference(layer_input, cotangent, doc_lengths, joined_weight, merge_weight, expand_weight, shrink_weight, first_gain, mixed_gain, second_gain, hidden_gain):
    positions = jnp.arange(STREAM_LEN, dtype=jnp.int32)
    documents = document_ids(doc_lengths, positions)
    valid_rows = (documents < DOCS).astype(jnp.float32)

    def forward(inputs, combined_matrix, merging_matrix, expansion_matrix, reduction_matrix, gain_first, gain_mixed, gain_second, gain_hidden):

        def group_layer(operands):
            packed_input, group_docs = operands
            leading_norm = reduced_precision(layer_norm(packed_input, gain_first))
            combined_output = reduced_precision(reduced_backward(jnp.einsum('nzc,cg->nzg', leading_norm, combined_matrix, precision=largest_value)))
            queries = combined_output[..., :D] * 0.125
            keys_all = combined_output[..., D:2 * D]
            values_all = combined_output[..., 2 * D:]
            attention = reduced_backward(lax.map(jax.checkpoint(attend), (queries, keys_all, values_all, group_docs)))
            attention_mixed_norm = reduced_precision(layer_norm(attention, gain_mixed))
            intermediate = packed_input + reduced_backward(jnp.einsum('nzc,cg->nzg', attention_mixed_norm, merging_matrix, precision=largest_value))
            trailing_branch = reduced_precision(layer_norm(intermediate, gain_second))
            widened_hidden = reduced_backward(jnp.einsum('iwo,om->iwm', trailing_branch, expansion_matrix, precision=largest_value))
            hidden_state = reduced_precision(layer_norm(jax.nn.gelu(widened_hidden, approximate=False), gain_hidden))
            return intermediate + reduced_backward(jnp.einsum('qbi,iv->qbv', hidden_state, reduction_matrix, precision=largest_value))
        return lax.map(jax.checkpoint(group_layer), (inputs, documents))
    result, pullback = jax.vjp(forward, layer_input.astype(jnp.float32), joined_weight.astype(jnp.float32), merge_weight.astype(jnp.float32), expand_weight.astype(jnp.float32), shrink_weight.astype(jnp.float32), first_gain.astype(jnp.float32), mixed_gain.astype(jnp.float32), second_gain.astype(jnp.float32), hidden_gain.astype(jnp.float32))
    grads = pullback(cotangent.astype(jnp.float32) * valid_rows[..., None])
    return (result.astype(jnp.bfloat16), grads[0].astype(jnp.bfloat16), grads[1], grads[2], grads[3], grads[4], grads[5], grads[6], grads[7], grads[8])
```

```python
import functools

import jax
import jax.numpy as jnp
from jax import lax
from jax.experimental import pallas as pl
from jax.experimental.pallas import tpu as pltpu
from jax.sharding import PartitionSpec as P

HEAD = 64
TILE = 256
WIDE = 512
big_negative = -1e30
norm_epsilon = 1e-05
VMEM_BYTES = 52 * 1024 * 1024

f32 = jnp.float32
bf16 = jnp.bfloat16


def dot(left, right):
    return jnp.dot(left, right, preferred_element_type=f32)


def dot_nt(left, right):
    return lax.dot_general(left, right, (((1,), (1,)), ((), ())), preferred_element_type=f32)


def dot_tn(left, right):
    return lax.dot_general(left, right, (((0,), (0,)), ((), ())), preferred_element_type=f32)


def normalized(values):
    centred = values - jnp.mean(values, axis=-1, keepdims=True)
    rate = lax.rsqrt(jnp.mean(centred * centred, axis=-1, keepdims=True) + norm_epsilon)
    return centred * rate, rate


def norm_back(normal, rate, weighted):
    return rate * (
        weighted
        - jnp.mean(weighted, axis=-1, keepdims=True)
        - normal * jnp.mean(weighted * normal, axis=-1, keepdims=True)
    )


def forward_kernel(
    place_ref, start_ref, gain_ref, weight_ref, pieces_ref,
    first_ref, joined_ref, shares_ref, attention_ref, sent_ref, rows_ref,
    *, planes, slots, seg, heads,
):
    plane, slot = place_ref[0], place_ref[1]
    for u in range(slots):
        for k in range(planes):
            offset = ((plane ^ k) * slots + (slot ^ u)) * seg
            rows_ref[pl.ds(pl.multiple_of(offset, seg), seg), :] = pieces_ref[u, k]
    length = planes * slots * seg
    width = heads * HEAD

    def project(tile, carry):
        rows = pl.ds(pl.multiple_of(tile * TILE, TILE), TILE)
        normal, _ = normalized(rows_ref[rows, :].astype(f32))
        first = (normal * gain_ref[...]).astype(bf16)
        first_ref[rows, :] = first
        joined = dot(first, weight_ref[...]).astype(bf16)
        for part in range(3):
            for h in range(heads):
                column = part * width + h * HEAD
                value = joined[:, column : column + HEAD]
                if part == 0:
                    value = value * jnp.asarray(0.125, bf16)
                joined_ref[part * heads + h, rows, :] = value
        return carry

    lax.fori_loop(0, length // TILE, project, 0)

    for q in range(length // TILE):
        rows = slice(q * TILE, (q + 1) * TILE)
        reach = (q + 1) * TILE
        query_pos = q * TILE + lax.broadcasted_iota(jnp.int32, (TILE, reach), 0)
        key_pos = lax.broadcasted_iota(jnp.int32, (TILE, reach), 1)
        allowed = (key_pos <= query_pos) & (key_pos >= start_ref[rows, :])
        for h in range(heads):
            scores = dot_nt(joined_ref[h, rows, :], joined_ref[heads + h, :reach, :])
            scores = jnp.where(allowed, scores, big_negative)
            peak = jnp.max(scores, axis=-1, keepdims=True)
            raised = jnp.exp(scores - peak)
            total = jnp.sum(raised, axis=-1, keepdims=True)
            shares = (raised * (1.0 / total)).astype(bf16)
            shares_ref[h, rows, :reach] = shares
            mixed = dot(shares, joined_ref[2 * heads + h, :reach, :])
            attention_ref[h, rows, :] = mixed
    block = slots * seg
    for s in range(slots):
        for z in range(planes):
            for h in range(heads):
                part = attention_ref[h, pl.ds(z * block + s * seg, seg), :]
                sent_ref[s, z * seg : (z + 1) * seg, h * HEAD : (h + 1) * HEAD] = part.astype(bf16)


def forward_call(place, start, gain, weight, pieces):
    slots, planes, seg, width = pieces.shape
    length = planes * slots * seg
    heads = weight.shape[1] // (3 * HEAD)
    kernel = functools.partial(forward_kernel, planes=planes, slots=slots, seg=seg, heads=heads)
    vmem = pl.BlockSpec(memory_space=pltpu.VMEM)
    return pl.pallas_call(
        kernel,
        out_shape=(
            jax.ShapeDtypeStruct((length, width), bf16),
            jax.ShapeDtypeStruct((3 * heads, length, HEAD), bf16),
            jax.ShapeDtypeStruct((heads, length, length), bf16),
            jax.ShapeDtypeStruct((heads, length, HEAD), f32),
            jax.ShapeDtypeStruct((slots, planes * seg, heads * HEAD), bf16),
        ),
        in_specs=[pl.BlockSpec(memory_space=pltpu.SMEM)] + [vmem] * 4,
        out_specs=(vmem,) * 5,
        scratch_shapes=[pltpu.VMEM((length, width), bf16)],
        compiler_params=pltpu.CompilerParams(vmem_limit_bytes=VMEM_BYTES),
        name="attention_forward",
    )(place, start, gain, weight, pieces)


def backward_kernel(
    place_ref, joined_ref, shares_ref, attention_ref, weight_ref, pieces_ref,
    grad_ref, branch_ref, arrived_ref, key_ref, value_ref, total_ref,
    *, planes, slots, seg, heads,
):
    slot = place_ref[1]
    block = slots * seg
    length = planes * block
    width = heads * HEAD
    for u in range(slots):
        for z in range(planes):
            offset = z * block + (slot ^ u) * seg
            arrived_ref[pl.ds(pl.multiple_of(offset, seg), seg), :] = pieces_ref[
                u, z * seg : (z + 1) * seg, :
            ]
    tiles = length // TILE
    for h in range(heads):
        for q in reversed(range(tiles)):
            rows = slice(q * TILE, (q + 1) * TILE)
            reach = (q + 1) * TILE
            grad = arrived_ref[rows, h * HEAD : (h + 1) * HEAD]
            inner = jnp.sum(grad.astype(f32) * attention_ref[h, rows, :], axis=-1, keepdims=True)
            shares = shares_ref[h, rows, :reach]
            grad_shares = dot_nt(grad, joined_ref[2 * heads + h, :reach, :])
            grad_scores = (shares.astype(f32) * (grad_shares - inner)).astype(bf16)
            query_grad = dot(grad_scores, joined_ref[heads + h, :reach, :]) * 0.125
            grad_ref[rows, h * HEAD : (h + 1) * HEAD] = query_grad.astype(bf16)
            key_add = dot_tn(joined_ref[h, rows, :], grad_scores)
            value_add = dot_tn(grad, shares)
            if q == tiles - 1:
                key_ref[...] = key_add
                value_ref[...] = value_add
            else:
                key_ref[:, :reach] += key_add
                value_ref[:, :reach] += value_add
        for part, source in ((1, key_ref), (2, value_ref)):
            column = part * width + h * HEAD
            for q in range(tiles):
                rows = slice(q * TILE, (q + 1) * TILE)
                grad_ref[rows, column : column + HEAD] = source[:, rows].T.astype(bf16)

    def back(tile, carry):
        rows = pl.ds(pl.multiple_of(tile * TILE, TILE), TILE)
        total_ref[rows, :] = dot_nt(grad_ref[rows, :], weight_ref[...]).astype(bf16)
        return carry

    lax.fori_loop(0, tiles, back, 0)
    for s in range(slots):
        for z in range(planes):
            branch_ref[s, z * seg : (z + 1) * seg, :] = total_ref[
                z * block + s * seg : z * block + (s + 1) * seg, :
            ]


def backward_call(place, joined, shares, attention, weight, pieces, planes):
    slots, tokens, _ = pieces.shape
    heads, length, _ = shares.shape
    width = weight.shape[0]
    kernel = functools.partial(
        backward_kernel, planes=planes, slots=slots, seg=tokens // planes, heads=heads
    )
    vmem = pl.BlockSpec(memory_space=pltpu.VMEM)
    return pl.pallas_call(
        kernel,
        out_shape=(
            jax.ShapeDtypeStruct((length, 3 * heads * HEAD), bf16),
            jax.ShapeDtypeStruct((slots, tokens, width), bf16),
        ),
        in_specs=[pl.BlockSpec(memory_space=pltpu.SMEM)] + [vmem] * 5,
        out_specs=(vmem,) * 2,
        scratch_shapes=[
            pltpu.VMEM((length, heads * HEAD), bf16),
            pltpu.VMEM((HEAD, length), f32),
            pltpu.VMEM((HEAD, length), f32),
            pltpu.VMEM((length, width), bf16),
        ],
        compiler_params=pltpu.CompilerParams(vmem_limit_bytes=VMEM_BYTES),
        name="attention_backward",
    )(place, joined, shares, attention, weight, pieces)


def middle_kernel(
    place_ref, pieces_ref, input_ref, cotangent_ref, valid_ref,
    merge_ref, expand_ref, shrink_ref, mixed_gain_ref, second_gain_ref, hidden_gain_ref,
    result_ref, mixed_ref, second_ref, hidden_ref, expanded_ref, mix_ref, branch_ref,
    grad_ref, away_ref, mixed_part_ref, second_part_ref, hidden_part_ref,
    held_ref, normal_ref, slope_ref, weighted_ref,
    *, slots, groups, width, spread,
):
    slot = place_ref[1]
    piece = width // groups
    for u in range(slots):
        held_ref[slot ^ u] = pieces_ref[u].astype(f32)
    mean = sum(jnp.sum(held_ref[g], axis=-1, keepdims=True) for g in range(groups)) * (1.0 / width)
    square = 0.0
    for g in range(groups):
        centred = held_ref[g] - mean
        held_ref[g] = centred
        square = square + jnp.sum(centred * centred, axis=-1, keepdims=True)
    mixed_rate = lax.rsqrt(square * (1.0 / width) + norm_epsilon)
    middle = input_ref[...].astype(f32)
    for g in range(groups):
        normal = held_ref[g] * mixed_rate
        held_ref[g] = normal
        mixed = (normal * mixed_gain_ref[g]).astype(bf16)
        mixed_ref[g] = mixed
        middle = middle + dot(mixed, merge_ref[g * piece : (g + 1) * piece, :])
    second_normal, second_rate = normalized(middle)
    second = (second_normal * second_gain_ref[...]).astype(bf16)
    second_ref[...] = second
    grad_out = cotangent_ref[...].astype(f32) * valid_ref[...]
    branch = grad_out.astype(bf16)
    branch_ref[...] = branch
    tokens = middle.shape[0]
    steps = spread // WIDE
    column = jnp.zeros((tokens, 1), f32)

    def columns(step):
        return pl.ds(pl.multiple_of(step * WIDE, WIDE), WIDE)

    def widen(step, total):
        at = columns(step)
        value = dot(second, expand_ref[:, at])
        share = 0.5 * (1.0 + lax.erf(value * 0.7071067811865476))
        gelu = value * share
        normal_ref[:, at] = gelu
        slope_ref[:, at] = share + value * (0.3989422804014327 * jnp.exp(-0.5 * value * value))
        return total + jnp.sum(gelu, axis=-1, keepdims=True)

    hidden_mean = lax.fori_loop(0, steps, widen, column) * (1.0 / spread)

    def deviate(step, total):
        centred = normal_ref[:, columns(step)] - hidden_mean
        return total + jnp.sum(centred * centred, axis=-1, keepdims=True)

    variance = lax.fori_loop(0, steps, deviate, column) * (1.0 / spread)
    hidden_rate = lax.rsqrt(variance + norm_epsilon)

    def narrow(step, carry):
        result, weighted_sum, inner_sum = carry
        at = columns(step)
        normal = (normal_ref[:, at] - hidden_mean) * hidden_rate
        normal_ref[:, at] = normal
        gain = hidden_gain_ref[:, at]
        hidden = (normal * gain).astype(bf16)
        hidden_ref[:, at] = hidden
        result = result + dot(hidden, shrink_ref[at, :])
        grad_hidden = dot_nt(branch, shrink_ref[at, :])
        hidden_part_ref[:, at] = jnp.sum(grad_hidden * normal, axis=0, keepdims=True)
        weighted = grad_hidden * gain
        weighted_ref[:, at] = weighted
        return (
            result,
            weighted_sum + jnp.sum(weighted, axis=-1, keepdims=True),
            inner_sum + jnp.sum(weighted * normal, axis=-1, keepdims=True),
        )

    result, weighted_sum, inner_sum = lax.fori_loop(0, steps, narrow, (middle, column, column))
    result_ref[...] = result.astype(bf16)
    weighted_mean = weighted_sum * (1.0 / spread)
    inner_mean = inner_sum * (1.0 / spread)

    def turn(step, total):
        at = columns(step)
        grad = hidden_rate * (
            weighted_ref[:, at] - weighted_mean - normal_ref[:, at] * inner_mean
        )
        expanded = (grad * slope_ref[:, at]).astype(bf16)
        expanded_ref[:, at] = expanded
        return total + dot_nt(expanded, expand_ref[:, at])

    grad_second = lax.fori_loop(0, steps, turn, jnp.zeros((tokens, width), f32))
    second_part_ref[...] = jnp.sum(grad_second * second_normal, axis=0, keepdims=True)
    grad_middle = grad_out + norm_back(
        second_normal, second_rate, grad_second * second_gain_ref[...]
    )
    grad_ref[...] = grad_middle
    mix = grad_middle.astype(bf16)
    mix_ref[...] = mix
    grads = []
    weighted_sum = 0.0
    inner_sum = 0.0
    for g in range(groups):
        grad_mixed = dot_nt(mix, merge_ref[g * piece : (g + 1) * piece, :])
        mixed_part_ref[g] = jnp.sum(grad_mixed * held_ref[g], axis=0, keepdims=True)
        weighted = grad_mixed * mixed_gain_ref[g]
        grads.append(weighted)
        weighted_sum = weighted_sum + jnp.sum(weighted, axis=-1, keepdims=True)
        inner_sum = inner_sum + jnp.sum(weighted * held_ref[g], axis=-1, keepdims=True)
    weighted_mean = weighted_sum * (1.0 / width)
    inner_mean = inner_sum * (1.0 / width)
    for g in range(slots):
        if g < groups:
            grad = mixed_rate * (grads[g] - weighted_mean - held_ref[g] * inner_mean)
            away_ref[g] = grad.astype(bf16)
        else:
            away_ref[g] = jnp.zeros(away_ref.shape[1:], bf16)


def middle_call(
    place, pieces, inputs, cotangent, valid, merge, expand, shrink,
    mixed_gain, second_gain, hidden_gain,
):
    slots, tokens, piece = pieces.shape
    width, spread = expand.shape
    groups = width // piece
    kernel = functools.partial(
        middle_kernel, slots=slots, groups=groups, width=width, spread=spread
    )
    vmem = pl.BlockSpec(memory_space=pltpu.VMEM)

    def low(*shape):
        return jax.ShapeDtypeStruct(shape, bf16)

    def full(*shape):
        return jax.ShapeDtypeStruct(shape, f32)

    return pl.pallas_call(
        kernel,
        out_shape=(
            low(tokens, width),
            low(groups, tokens, piece),
            low(tokens, width),
            low(tokens, spread),
            low(tokens, spread),
            low(tokens, width),
            low(tokens, width),
            full(tokens, width),
            low(slots, tokens, piece),
            full(groups, 1, piece),
            full(1, width),
            full(1, spread),
        ),
        in_specs=[pl.BlockSpec(memory_space=pltpu.SMEM)] + [vmem] * 10,
        out_specs=(vmem,) * 12,
        scratch_shapes=[
            pltpu.VMEM((slots, tokens, piece), f32),
            pltpu.VMEM((tokens, spread), f32),
            pltpu.VMEM((tokens, spread), f32),
            pltpu.VMEM((tokens, spread), f32),
        ],
        compiler_params=pltpu.CompilerParams(vmem_limit_bytes=VMEM_BYTES),
        name="middle",
    )(
        place, pieces, inputs, cotangent, valid, merge, expand, shrink,
        mixed_gain.reshape(groups, 1, piece), second_gain.reshape(1, width),
        hidden_gain.reshape(1, spread),
    )


def swap(value, axis, bits):
    size = lax.axis_size(axis)
    return lax.ppermute(value, axis, [(i, i ^ bits) for i in range(size)])


def pick(value, index, axis=0):
    return lax.dynamic_index_in_dim(value, index, axis, keepdims=False)


def added(left, right):
    return (left.astype(f32) + right.astype(f32)).astype(bf16)


def bits_of(size):
    return size.bit_length() - 1


def per_device(
    layer_input, cotangent, doc_lengths, joined_weight, merge_weight, expand_weight,
    shrink_weight, first_gain, mixed_gain, second_gain, hidden_gain,
):
    _, planes, seg, width = layer_input.shape
    spread = expand_weight.shape[1]
    size = lax.axis_size("blk")
    slots = size // planes
    batches = lax.axis_size("batch")
    rank = lax.axis_index("blk")
    group_rank = lax.axis_index("batch")
    plane = rank // slots
    slot = rank % slots
    head_count = width // HEAD
    heads = -(-head_count // slots)
    groups = head_count // heads
    piece = heads * HEAD
    tokens = planes * seg
    length = slots * tokens
    place = jnp.stack([plane, slot]).astype(jnp.int32)

    def to_planes(blocks):
        return [pick(blocks, plane)] + [
            swap(pick(blocks, plane ^ k), "blk", k * slots) for k in range(1, planes)
        ]

    def in_order(blocks):
        stacked = jnp.stack(blocks)
        return jnp.stack([pick(stacked, plane ^ k) for k in range(planes)])

    def all_slots(value):
        held = [value]
        for bit in reversed(range(bits_of(slots))):
            held = held + [swap(v, "blk", 1 << bit) for v in held]
        ordered = [None] * slots
        for at, v in enumerate(held):
            code = 0
            for order, bit in enumerate(reversed(range(bits_of(slots)))):
                if at >> order & 1:
                    code |= 1 << bit
            ordered[code] = v
        return ordered

    def over_slots(blocks):
        return jnp.stack(
            [pick(blocks, slot)]
            + [swap(pick(blocks, slot ^ u), "blk", u) for u in range(1, slots)]
        )

    arrived = to_planes(layer_input[0])
    quarter = jnp.stack(arrived)
    pieces = jnp.stack(all_slots(quarter))
    ends = jnp.cumsum(pick(doc_lengths[0], plane), axis=-1)
    positions = jnp.arange(length, dtype=jnp.int32)
    reached = ends[None, :] <= positions[:, None]
    start = jnp.max(jnp.where(reached, ends[None, :], 0), axis=-1, keepdims=True)
    own_start = jnp.clip(jnp.minimum(slot, groups - 1) * piece, 0, width - piece)
    columns = [
        lax.dynamic_slice_in_dim(joined_weight, part * width + own_start, piece, 1)
        for part in range(3)
    ]
    own_weight = jnp.concatenate(columns, axis=1)
    first, joined, shares, attention, sent = forward_call(
        place, start, first_gain.reshape(1, width), own_weight, pieces
    )
    cotangent_rows = in_order(to_planes(cotangent[0])).reshape(tokens, width)
    input_rows = in_order(arrived).reshape(tokens, width)
    own_pos = (
        jnp.arange(planes, dtype=jnp.int32)[:, None] * (slots * seg)
        + slot * seg
        + jnp.arange(seg, dtype=jnp.int32)[None, :]
    ).reshape(tokens, 1)
    valid = (own_pos < ends[-1]).astype(f32)
    (
        result, mixed, second, hidden, expanded, mix, branch, grad_middle, away,
        mixed_part, second_part, hidden_part,
    ) = middle_call(
        place, over_slots(sent), input_rows, cotangent_rows, valid,
        merge_weight, expand_weight, shrink_weight, mixed_gain, second_gain, hidden_gain,
    )

    def to_owners(rows):
        blocks = rows.reshape(planes, seg, width)
        return in_order(to_planes(blocks)).reshape(layer_input.shape)

    layer_result = to_owners(result)
    grad_joined, first_branch = backward_call(
        place, joined, shares, attention, own_weight, over_slots(away), planes
    )

    rows_view = (planes, slots)

    def halve(value, axis, stride, bit_axis):
        rank_bit = (lax.axis_index(axis) // stride) % 2
        keep = pick(value, rank_bit, bit_axis)
        give = pick(value, 1 - rank_bit, bit_axis)
        return added(keep, swap(give, axis, stride))

    def split_bits(value):
        return value.reshape((2,) * bits_of(size) + (value.shape[0] // size,) + value.shape[1:])

    def halve_blk(value, bit, left):
        at = left.index(bit)
        return halve(value, "blk", 1 << bit, at), [b for b in left if b != bit]

    def halve_batch(value):
        half = value.shape[-1] // 2
        bit = group_rank % 2
        keep = lax.dynamic_slice_in_dim(value, bit * half, half, value.ndim - 1)
        give = lax.dynamic_slice_in_dim(value, (1 - bit) * half, half, value.ndim - 1)
        return added(keep, swap(give, "batch", 1))

    def finish(value):
        for bit in range(1, bits_of(batches)):
            value = added(value, swap(value, "batch", 1 << bit))
        other = swap(value, "batch", 1)
        low_first = group_rank % 2 == 0
        return jnp.concatenate(
            [jnp.where(low_first, value, other), jnp.where(low_first, other, value)], axis=-1
        ).astype(f32)

    all_bits = list(reversed(range(bits_of(size))))
    slot_bits = bits_of(slots)
    row_bits = list(range(1, slot_bits))
    plane_bits = list(range(slot_bits, bits_of(size)))

    def reduce_rows(value, order):
        value = split_bits(value.astype(bf16))
        left = all_bits
        for step in order:
            if step == "batch":
                value = halve_batch(value)
            else:
                value, left = halve_blk(value, step, left)
        return finish(value)

    shrink_grad = reduce_rows(dot_tn(hidden, branch), [0, "batch"] + row_bits + plane_bits)
    expand_grad = reduce_rows(dot_tn(second, expanded), [0] + row_bits + ["batch"] + plane_bits)
    merge_part = jnp.concatenate([dot_tn(mixed[g], mix) for g in range(groups)], axis=0)
    merge_grad = reduce_rows(merge_part, [0] + row_bits + ["batch"] + plane_bits)

    joined_part = dot_tn(first, grad_joined).astype(bf16)
    value = joined_part.reshape((2,) * len(plane_bits) + (width // planes, 3 * piece))
    left = list(reversed(plane_bits))
    for bit in plane_bits:
        value, left = halve_blk(value, bit, left)
    for bit in range(bits_of(batches)):
        value = added(value, swap(value, "batch", 1 << bit))
    value = over_slots(value.reshape(slots, width // size, 3 * piece))
    value = jnp.stack([pick(value, slot ^ u) for u in range(groups)])
    value = value.reshape(groups, width // size, 3, piece).transpose(1, 2, 0, 3)
    joined_grad = value.reshape(width // size, 3 * width).astype(f32)

    branch_sum = first_branch.reshape((2,) * slot_bits + (tokens, width))
    left = list(reversed(range(slot_bits)))
    for bit in range(slot_bits):
        branch_sum, left = halve_blk(branch_sum, bit, left)
    grad_first = branch_sum.astype(f32)
    first_normal, first_rate = normalized(input_rows.astype(f32))
    first_part = jnp.sum(grad_first * first_normal, axis=0)
    input_grad = to_owners(
        (grad_middle + norm_back(first_normal, first_rate, grad_first * first_gain)).astype(bf16)
    )

    def everywhere(value):
        for bit in range(bits_of(size)):
            value = value + swap(value, "blk", 1 << bit)
        for bit in range(bits_of(batches)):
            value = value + swap(value, "batch", 1 << bit)
        return value

    early = everywhere(
        jnp.concatenate([mixed_part.reshape(1, width), second_part, hidden_part], axis=1)
    )[0]
    first_total = everywhere(first_part.reshape(1, width))[0]
    return (
        layer_result, input_grad, joined_grad, merge_grad, expand_grad, shrink_grad,
        first_total, early[:width], early[width : 2 * width], early[2 * width :],
    )


def solution(mesh):
    rows = P("batch", None, "blk", None)
    return jax.shard_map(
        per_device,
        mesh=mesh,
        in_specs=(rows, rows, P("batch", None, None)) + (P(),) * 8,
        out_specs=(rows, rows) + (P("blk", None),) * 4 + (P(),) * 4,
        check_vma=False,
    )
```

```python
import functools

import jax
import jax.numpy as jnp
from jax import lax
from jax.experimental import pallas as pl
from jax.experimental.pallas import tpu as pltpu
from jax.sharding import PartitionSpec as P

HEAD = 64
TILE = 256
WIDE = 512
FORWARD_MIB = 24
BACKWARD_MIB = 24
WIDEN_MIB = 16
TURN_MIB = 20
OUTER_MIB = 16
big_negative = -1e30
norm_epsilon = 1e-05

f32 = jnp.float32
bf16 = jnp.bfloat16


def dot(left, right):
    return jnp.dot(left, right, preferred_element_type=f32)


def dot_nt(left, right):
    return lax.dot_general(left, right, (((1,), (1,)), ((), ())), preferred_element_type=f32)


def dot_tn(left, right):
    return lax.dot_general(left, right, (((0,), (0,)), ((), ())), preferred_element_type=f32)


def normalized(values):
    centred = values - jnp.mean(values, axis=-1, keepdims=True)
    rate = lax.rsqrt(jnp.mean(centred * centred, axis=-1, keepdims=True) + norm_epsilon)
    return centred * rate, rate


def norm_back(normal, rate, weighted):
    return rate * (
        weighted
        - jnp.mean(weighted, axis=-1, keepdims=True)
        - normal * jnp.mean(weighted * normal, axis=-1, keepdims=True)
    )


def vmem_spec():
    return pl.BlockSpec(memory_space=pltpu.VMEM)


def hbm_spec():
    return pl.BlockSpec(memory_space=pltpu.HBM)


def params(mebibytes):
    return pltpu.CompilerParams(vmem_limit_bytes=mebibytes * 1024 * 1024)


def cost(flops, moved):
    return pl.CostEstimate(flops=flops, bytes_accessed=moved, transcendentals=0)


def codes(steps):
    listed = [((), 0)]
    for bit in steps:
        listed = [(at + (b,), code | (b << bit)) for at, code in listed for b in (0, 1)]
    return listed


def forward_kernel(*refs, planes, slots, seg, heads):
    place_ref, start_ref, gain_ref, weight_ref = refs[:4]
    pieces = refs[4 : 4 + slots]
    refs = refs[4 + slots :]
    length = planes * slots * seg
    tiles = length // TILE
    first_to, joined_to = refs[:2]
    sent = refs[2 : 2 + slots]
    shares_to = refs[2 + slots : 2 + slots + tiles]
    rows_ref, first_ref, joined_ref, attention_ref = refs[2 + slots + tiles : 6 + slots + tiles]
    shares = refs[6 + slots + tiles : 6 + slots + 2 * tiles]
    ready = refs[-1]
    copies = [
        pltpu.make_async_copy(source, target, ready.at[at])
        for at, (source, target) in enumerate(
            zip((first_ref, joined_ref) + shares, (first_to, joined_to) + shares_to)
        )
    ]
    plane, slot = place_ref[0], place_ref[1]
    for u in range(slots):
        for k in range(planes):
            offset = ((plane ^ k) * slots + (slot ^ u)) * seg
            rows_ref[pl.ds(pl.multiple_of(offset, seg), seg), :] = pieces[u][k]
    width = heads * HEAD

    def project(tile, carry):
        rows = pl.ds(pl.multiple_of(tile * TILE, TILE), TILE)
        normal, _ = normalized(rows_ref[rows, :].astype(f32))
        first = (normal * gain_ref[...]).astype(bf16)
        first_ref[rows, :] = first
        joined = dot(first, weight_ref[...]).astype(bf16)
        for part in range(3):
            for h in range(heads):
                column = part * width + h * HEAD
                value = joined[:, column : column + HEAD]
                if part == 0:
                    value = value * jnp.asarray(0.125, bf16)
                joined_ref[part * heads + h, rows, :] = value
        return carry

    lax.fori_loop(0, tiles, project, 0)
    copies[0].start()
    copies[1].start()
    for q in reversed(range(tiles)):
        rows = slice(q * TILE, (q + 1) * TILE)
        reach = (q + 1) * TILE
        query_pos = q * TILE + lax.broadcasted_iota(jnp.int32, (TILE, reach), 0)
        key_pos = lax.broadcasted_iota(jnp.int32, (TILE, reach), 1)
        allowed = (key_pos <= query_pos) & (key_pos >= start_ref[rows, :])
        for h in range(heads):
            scores = dot_nt(joined_ref[h, rows, :], joined_ref[heads + h, :reach, :])
            scores = jnp.where(allowed, scores, big_negative)
            peak = jnp.max(scores, axis=-1, keepdims=True)
            raised = jnp.exp(scores - peak)
            total = jnp.sum(raised, axis=-1, keepdims=True)
            share = (raised * (1.0 / total)).astype(bf16)
            shares[q][h] = share
            attention_ref[h, rows, :] = dot(share, joined_ref[2 * heads + h, :reach, :])
        copies[2 + q].start()
    half = planes // 2
    for u in range(slots):
        for k in range(planes):
            offset = ((plane ^ k) * slots + (slot ^ u)) * seg
            rows = slice(k % half * seg, (k % half + 1) * seg)
            for h in range(heads):
                part = attention_ref[h, pl.ds(pl.multiple_of(offset, seg), seg), :]
                column = k // half * width + h * HEAD
                sent[u][rows, column : column + HEAD] = part.astype(bf16)
    for copy in copies:
        copy.wait()


def forward_call(place, start, gain, weight, pieces):
    slots = len(pieces)
    planes, seg, width = pieces[0].shape
    length = planes * slots * seg
    heads = weight.shape[1] // (3 * HEAD)
    kernel = functools.partial(forward_kernel, planes=planes, slots=slots, seg=seg, heads=heads)
    packed = jax.ShapeDtypeStruct((planes * seg // 2, 2 * heads * HEAD), bf16)
    tiled = [(heads, TILE, reach) for reach in range(TILE, length + 1, TILE)]
    outs = pl.pallas_call(
        kernel,
        out_shape=(
            pltpu.HBM((length, width), bf16),
            pltpu.HBM((3 * heads, length, HEAD), bf16),
        )
        + (packed,) * slots
        + tuple(pltpu.HBM(shape, bf16) for shape in tiled),
        in_specs=[pl.BlockSpec(memory_space=pltpu.SMEM)] + [vmem_spec()] * (3 + slots),
        out_specs=(hbm_spec(),) * 2 + (vmem_spec(),) * slots + (hbm_spec(),) * len(tiled),
        scratch_shapes=[
            pltpu.VMEM((length, width), bf16),
            pltpu.VMEM((length, width), bf16),
            pltpu.VMEM((3 * heads, length, HEAD), bf16),
            pltpu.VMEM((heads, length, HEAD), f32),
        ]
        + [pltpu.VMEM(shape, bf16) for shape in tiled]
        + [pltpu.SemaphoreType.DMA((2 + len(tiled),))],
        compiler_params=params(FORWARD_MIB * length // 1024),
        cost_estimate=cost(8 << 30, 8 << 20),
        name="attention_forward",
    )(place, start, gain, weight, *pieces)
    return outs[:2], outs[2 : 2 + slots], outs[2 + slots :]


def backward_kernel(*refs, planes, slots, seg, heads, rows_each, sides):
    place_ref, first_from, joined_from, weight_ref, gain_ref, parts_ref = refs[:6]
    pieces = refs[6 : 6 + slots]
    length = planes * slots * seg
    tiles = length // TILE
    refs = refs[6 + slots :]
    shares_from = refs[:tiles]
    joined_keep, joined_give, branch_keep, branch_give = refs[tiles : tiles + 4]
    (
        grad_ref, arrived_ref, key_ref, value_ref, total_ref, outer_ref, row_ref,
        first_ref, joined_ref,
    ) = refs[tiles + 4 : tiles + 13]
    shares = refs[tiles + 13 : 2 * tiles + 13]
    ready = refs[-1]
    copies = [
        pltpu.make_async_copy(source, target, ready.at[at])
        for at, (source, target) in enumerate(
            zip((joined_from, first_from) + shares_from, (joined_ref, first_ref) + shares)
        )
    ]
    copies[0].start()
    for q in reversed(range(tiles)):
        copies[2 + q].start()
    copies[1].start()
    plane, slot, side = place_ref[0], place_ref[1], place_ref[3]
    width = heads * HEAD
    half = planes // 2
    for u in range(slots):
        for k in range(planes):
            offset = ((plane ^ k) * slots + (slot ^ u)) * seg
            column = k // half * width
            arrived_ref[pl.ds(pl.multiple_of(offset, seg), seg), :] = pieces[u][
                k % half * seg : (k % half + 1) * seg, column : column + width
            ]
    copies[0].wait()
    for h in range(heads):
        for q in reversed(range(tiles)):
            rows = slice(q * TILE, (q + 1) * TILE)
            reach = (q + 1) * TILE
            grad = arrived_ref[rows, h * HEAD : (h + 1) * HEAD]
            if h == 0:
                copies[2 + q].wait()
            share = shares[q][h]
            product = share.astype(f32) * dot_nt(grad, joined_ref[2 * heads + h, :reach, :])
            inner = jnp.sum(product, axis=-1, keepdims=True)
            grad_scores = (product - share.astype(f32) * inner).astype(bf16)
            query_grad = dot(grad_scores, joined_ref[heads + h, :reach, :]) * 0.125
            grad_ref[rows, h * HEAD : (h + 1) * HEAD] = query_grad.astype(bf16)
            key_add = dot_tn(joined_ref[h, rows, :], grad_scores)
            value_add = dot_tn(grad, share)
            if q == tiles - 1:
                key_ref[...] = key_add
                value_ref[...] = value_add
            else:
                key_ref[:, :reach] += key_add
                value_ref[:, :reach] += value_add
        for part, source in ((1, key_ref), (2, value_ref)):
            column = part * width + h * HEAD
            for q in range(tiles):
                rows = slice(q * TILE, (q + 1) * TILE)
                grad_ref[rows, column : column + HEAD] = source[:, rows].T.astype(bf16)

    def back(tile, carry):
        rows = pl.ds(pl.multiple_of(tile * TILE, TILE), TILE)
        total_ref[rows, :] = dot_nt(grad_ref[rows, :], weight_ref[...])
        return carry

    lax.fori_loop(0, tiles, back, 0)
    for at, code in codes(range(1, bits_of(slots))):
        for out, u in ((branch_keep, code), (branch_give, code | 1)):
            for k in range(planes):
                offset = ((plane ^ k) * slots + (slot ^ u)) * seg
                out[at + (slice(k * seg, (k + 1) * seg),)] = total_ref[
                    pl.ds(pl.multiple_of(offset, seg), seg), :
                ].astype(bf16)
    model = first_ref.shape[1]
    copies[1].wait()
    for d in range(0, model, TILE):
        outer = dot_tn(first_ref[:, d : d + TILE], grad_ref[...])
        outer_ref[d : d + TILE, :] = outer
        scaled = jnp.sum(outer * weight_ref[d : d + TILE, :].astype(f32), axis=-1, keepdims=True)
        scaled = jnp.broadcast_to(scaled / gain_ref[d : d + TILE, :], (TILE, 128)).T
        row_ref[:, d : d + TILE] = scaled[:1]
    wide = 3 * width
    row_ref[:, model : model + parts_ref.shape[1]] = parts_ref[...]
    gains = model + parts_ref.shape[1]
    rows = rows_each // sides
    outs = [joined_keep, joined_give][:sides] if sides > 1 else [joined_keep]
    for other, out in enumerate(outs):
        at = 0
        for _, code in codes(range(bits_of(planes))):
            for u in range(slots):
                offset = ((plane ^ code) * slots + (slot ^ u)) * rows_each + (side ^ other) * rows
                if sides == 1:
                    offset = ((plane ^ code) * slots + (slot ^ u)) * rows_each
                out[at] = outer_ref[pl.ds(pl.multiple_of(offset, rows), rows), :].astype(bf16)
                at += 1
        out[at] = jnp.zeros((rows, wide), bf16)
        for r in range(-(-gains // wide)):
            end = min((r + 1) * wide, gains)
            out[at, r : r + 1, : end - r * wide] = row_ref[:, r * wide : end].astype(bf16)


def backward_call(
    place, first, joined, weight, gain, parts, pieces, shares, planes, sides
):
    slots = len(pieces)
    tokens = pieces[0].shape[0] * 2
    heads, length = joined.shape[0] // 3, joined.shape[1]
    width = weight.shape[0]
    rows_each = width // (planes * slots)
    kernel = functools.partial(
        backward_kernel, planes=planes, slots=slots, seg=tokens // planes, heads=heads,
        rows_each=rows_each, sides=sides,
    )
    pairs = (2,) * (bits_of(slots) - 1)
    wide = 3 * heads * HEAD
    row = -(-(width + parts.shape[1]) // 128) * 128
    blocks = jax.ShapeDtypeStruct((planes * slots + 1, rows_each // sides, wide), bf16)
    return pl.pallas_call(
        kernel,
        out_shape=(
            blocks,
            blocks,
            jax.ShapeDtypeStruct(pairs + (tokens, width), bf16),
            jax.ShapeDtypeStruct(pairs + (tokens, width), bf16),
        ),
        in_specs=[pl.BlockSpec(memory_space=pltpu.SMEM)]
        + [hbm_spec()] * 2
        + [vmem_spec()] * (3 + slots)
        + [hbm_spec()] * len(shares),
        out_specs=(vmem_spec(),) * 4,
        scratch_shapes=[
            pltpu.VMEM((length, wide), bf16),
            pltpu.VMEM((length, heads * HEAD), bf16),
            pltpu.VMEM((HEAD, length), f32),
            pltpu.VMEM((HEAD, length), f32),
            pltpu.VMEM((length, width), f32),
            pltpu.VMEM((width, wide), f32),
            pltpu.VMEM((1, row), f32),
            pltpu.VMEM(first.shape, bf16),
            pltpu.VMEM(joined.shape, bf16),
        ]
        + [pltpu.VMEM(share.shape, bf16) for share in shares]
        + [pltpu.SemaphoreType.DMA((2 + len(shares),))],
        compiler_params=params(BACKWARD_MIB * length // 1024),
        cost_estimate=cost(10 << 30, 10 << 20),
        name="attention_backward",
    )(place, first, joined, weight, gain, parts, *pieces, *shares)


def widen_kernel(*refs, slots, planes, groups, width, spread):
    place_ref = refs[0]
    pieces = refs[1 : 1 + slots]
    blocks = refs[1 + slots : 1 + slots + planes]
    refs = refs[1 + slots + planes :]
    (
        valid_ref, input_ref, mixed_gain_ref, second_gain_ref, hidden_gain_ref, merge_ref, expand_from,
    ) = refs[:7]
    (
        mixed_ref, middle_ref, second_ref, hidden_ref, normal_ref, slope_ref, held_ref,
        mixed_rate_ref, hidden_rate_ref, branch_ref,
    ) = refs[7:17]
    expand_ref, gelu_ref, ready = refs[17:]
    steps = spread // WIDE

    def copy(step):
        at = pl.ds(step * WIDE, WIDE)
        return pltpu.make_async_copy(
            expand_from.at[:, at], expand_ref.at[:, at], ready.at[step]
        )

    for step in range(steps):
        copy(step).start()
    slot = place_ref[1]
    piece = width // groups
    tokens = input_ref.shape[0]
    half = tokens // 2
    for u in range(slots):
        for side in range(2):
            held_ref[slot ^ u, side * half : (side + 1) * half, :] = pieces[u][
                :, side * piece : (side + 1) * piece
            ].astype(f32)
    mean = sum(jnp.sum(held_ref[g], axis=-1, keepdims=True) for g in range(groups)) * (1.0 / width)
    square = 0.0
    for g in range(groups):
        centred = held_ref[g] - mean
        held_ref[g] = centred
        square = square + jnp.sum(centred * centred, axis=-1, keepdims=True)
    mixed_rate = lax.rsqrt(square * (1.0 / width) + norm_epsilon)
    mixed_rate_ref[...] = mixed_rate
    middle = input_ref[...].astype(f32)
    for g in range(groups):
        normal = held_ref[g] * mixed_rate
        held_ref[g] = normal
        mixed = (normal * mixed_gain_ref[g]).astype(bf16)
        mixed_ref[:, g * piece : (g + 1) * piece] = mixed
        middle = middle + dot(mixed, merge_ref[g * piece : (g + 1) * piece, :])
    middle_ref[...] = middle
    seg = tokens // planes
    for k in range(planes):
        at = slice(k * seg, (k + 1) * seg)
        branch_ref[at, :] = (blocks[k][...].astype(f32) * valid_ref[at, :]).astype(bf16)
    second_normal, _ = normalized(middle)
    second = (second_normal * second_gain_ref[...]).astype(bf16)
    second_ref[...] = second
    total = jnp.zeros((tokens, 1), f32)
    for step in range(steps):
        copy(step).wait()
        at = slice(step * WIDE, (step + 1) * WIDE)
        value = dot(second, expand_ref[:, at])
        share = 0.5 * (1.0 + lax.erf(value * 0.7071067811865476))
        gelu = value * share
        gelu_ref[:, at] = gelu
        slope = share + value * (0.3989422804014327 * jnp.exp(-0.5 * value * value))
        slope_ref[:, at] = slope.astype(bf16)
        total = total + jnp.sum(gelu, axis=-1, keepdims=True)
    mean = total * (1.0 / spread)
    total = jnp.zeros((tokens, 1), f32)
    for step in range(steps):
        centred = gelu_ref[:, step * WIDE : (step + 1) * WIDE] - mean
        total = total + jnp.sum(centred * centred, axis=-1, keepdims=True)
    rate = lax.rsqrt(total * (1.0 / spread) + norm_epsilon)
    hidden_rate_ref[...] = rate
    for step in range(steps):
        at = slice(step * WIDE, (step + 1) * WIDE)
        normal = (gelu_ref[:, at] - mean) * rate
        normal_ref[:, at] = normal.astype(bf16)
        hidden_ref[:, at] = (normal * hidden_gain_ref[:, at]).astype(bf16)


def widen_call(
    place, pieces, blocks, valid, inputs, mixed_gain, second_gain, hidden_gain, merge, expand
):
    slots = len(pieces)
    tokens = inputs.shape[0]
    piece = pieces[0].shape[1] // 2
    width, spread = expand.shape
    groups = width // piece

    def low(*shape):
        return jax.ShapeDtypeStruct(shape, bf16)

    def full(*shape):
        return jax.ShapeDtypeStruct(shape, f32)

    return pl.pallas_call(
        functools.partial(
            widen_kernel, slots=slots, planes=len(blocks), groups=groups, width=width,
            spread=spread,
        ),
        out_shape=(
            low(tokens, width),
            full(tokens, width),
            low(tokens, width),
            low(tokens, spread),
            low(tokens, spread),
            low(tokens, spread),
            full(slots, tokens, piece),
            full(tokens, 1),
            full(tokens, 1),
            low(tokens, width),
        ),
        in_specs=[pl.BlockSpec(memory_space=pltpu.SMEM)]
        + [vmem_spec()] * (6 + slots + len(blocks))
        + [hbm_spec()],
        out_specs=(vmem_spec(),) * 10,
        scratch_shapes=[
            pltpu.VMEM((width, spread), bf16),
            pltpu.VMEM((tokens, spread), f32),
            pltpu.SemaphoreType.DMA((spread // WIDE,)),
        ],
        compiler_params=params(WIDEN_MIB),
        cost_estimate=cost(6 << 30, 6 << 20),
        name="widen",
    )(
        place, *pieces, *blocks, valid, inputs, mixed_gain.reshape(groups, 1, piece),
        second_gain.reshape(1, width), hidden_gain.reshape(1, spread), merge, expand,
    )


def turn_kernel(*refs, slots, planes, groups, width, spread):
    (
        place_ref, branch_ref, hidden_ref, normal_ref, slope_ref, middle_ref, held_ref,
        mixed_rate_ref, hidden_rate_ref,
        mixed_gain_ref, second_gain_ref, hidden_gain_ref, merge_ref, shrink_from, expand_from,
    ) = refs[:15]
    expanded_ref, mix_ref, grad_ref, parts_ref = refs[15:19]
    away = refs[19 : 19 + slots]
    results = refs[19 + slots : 19 + slots + planes]
    shrink_ref, expand_ref, weighted_ref, sent_ref, ready = refs[19 + slots + planes :]
    steps = spread // WIDE

    def copy_shrink(step):
        at = pl.ds(step * WIDE, WIDE)
        return pltpu.make_async_copy(shrink_from.at[at], shrink_ref.at[at], ready.at[step])

    def copy_expand(step):
        at = pl.ds(step * WIDE, WIDE)
        return pltpu.make_async_copy(
            expand_from.at[:, at], expand_ref.at[:, at], ready.at[steps + step]
        )

    for step in range(steps):
        copy_shrink(step).start()
    for step in range(steps):
        copy_expand(step).start()
    slot = place_ref[1]
    piece = width // groups
    tokens = middle_ref.shape[0]
    half = tokens // 2
    branch = branch_ref[...]
    result = middle_ref[...]
    weighted_sum = jnp.zeros((tokens, 1), f32)
    inner_sum = jnp.zeros((tokens, 1), f32)
    for step in range(steps):
        copy_shrink(step).wait()
        at = slice(step * WIDE, (step + 1) * WIDE)
        result = result + dot(hidden_ref[:, at], shrink_ref[at, :])
        grad_hidden = dot_nt(branch, shrink_ref[at, :])
        normal = normal_ref[:, at].astype(f32)
        start = 2 * width + step * WIDE
        parts_ref[:, start : start + WIDE] = jnp.sum(grad_hidden * normal, axis=0, keepdims=True)
        weighted = grad_hidden * hidden_gain_ref[:, at]
        weighted_ref[:, at] = weighted
        weighted_sum = weighted_sum + jnp.sum(weighted, axis=-1, keepdims=True)
        inner_sum = inner_sum + jnp.sum(weighted * normal, axis=-1, keepdims=True)
    seg = tokens // planes
    for k in range(planes):
        results[k][...] = result[k * seg : (k + 1) * seg, :].astype(bf16)
    weighted_mean = weighted_sum * (1.0 / spread)
    inner_mean = inner_sum * (1.0 / spread)
    rate = hidden_rate_ref[...]
    grad_second = jnp.zeros((tokens, width), f32)
    for step in range(steps):
        copy_expand(step).wait()
        at = slice(step * WIDE, (step + 1) * WIDE)
        grad = rate * (
            weighted_ref[:, at] - weighted_mean - normal_ref[:, at].astype(f32) * inner_mean
        )
        expanded = (grad * slope_ref[:, at].astype(f32)).astype(bf16)
        expanded_ref[:, at] = expanded
        grad_second = grad_second + dot_nt(expanded, expand_ref[:, at])
    second_normal, second_rate = normalized(middle_ref[...])
    parts_ref[:, width : 2 * width] = jnp.sum(grad_second * second_normal, axis=0, keepdims=True)
    grad_middle = branch.astype(f32) + norm_back(
        second_normal, second_rate, grad_second * second_gain_ref[...]
    )
    grad_ref[...] = grad_middle
    mix = grad_middle.astype(bf16)
    mix_ref[...] = mix
    grads = []
    weighted_sum = 0.0
    inner_sum = 0.0
    for g in range(groups):
        grad_mixed = dot_nt(mix, merge_ref[g * piece : (g + 1) * piece, :])
        parts_ref[:, g * piece : (g + 1) * piece] = jnp.sum(
            grad_mixed * held_ref[g], axis=0, keepdims=True
        )
        weighted = grad_mixed * mixed_gain_ref[g]
        grads.append(weighted)
        weighted_sum = weighted_sum + jnp.sum(weighted, axis=-1, keepdims=True)
        inner_sum = inner_sum + jnp.sum(weighted * held_ref[g], axis=-1, keepdims=True)
    weighted_mean = weighted_sum * (1.0 / width)
    inner_mean = inner_sum * (1.0 / width)
    for g in range(slots):
        if g < groups:
            sent_ref[g] = mixed_rate_ref[...] * (
                grads[g] - weighted_mean - held_ref[g] * inner_mean
            )
        else:
            sent_ref[g] = jnp.zeros(sent_ref.shape[1:], f32)
    for u in range(slots):
        for side in range(2):
            away[u][:, side * piece : (side + 1) * piece] = sent_ref[
                slot ^ u, side * half : (side + 1) * half, :
            ].astype(bf16)


def turn_call(
    place, branch, hidden, normal, slope, middle, held, mixed_rate, hidden_rate,
    mixed_gain, second_gain, hidden_gain, merge, shrink, expand, planes,
):
    slots, tokens, piece = held.shape
    width, spread = expand.shape
    groups = width // piece

    def low(*shape):
        return jax.ShapeDtypeStruct(shape, bf16)

    def full(*shape):
        return jax.ShapeDtypeStruct(shape, f32)

    outs = pl.pallas_call(
        functools.partial(
            turn_kernel, slots=slots, planes=planes, groups=groups, width=width, spread=spread
        ),
        out_shape=(
            low(tokens, spread),
            low(tokens, width),
            full(tokens, width),
            full(1, 2 * width + spread),
        )
        + (low(tokens // 2, 2 * piece),) * slots
        + (low(tokens // planes, width),) * planes,
        in_specs=[pl.BlockSpec(memory_space=pltpu.SMEM)] + [vmem_spec()] * 12 + [hbm_spec()] * 2,
        out_specs=(vmem_spec(),) * (4 + slots + planes),
        scratch_shapes=[
            pltpu.VMEM((spread, width), bf16),
            pltpu.VMEM((width, spread), bf16),
            pltpu.VMEM((tokens, spread), f32),
            pltpu.VMEM((slots, tokens, piece), f32),
            pltpu.SemaphoreType.DMA((2 * spread // WIDE,)),
        ],
        compiler_params=params(TURN_MIB),
        cost_estimate=cost(9 << 30, 8 << 20),
        name="turn",
    )(
        place, branch, hidden, normal, slope, middle, held, mixed_rate, hidden_rate,
        mixed_gain.reshape(groups, 1, piece), second_gain.reshape(1, width),
        hidden_gain.reshape(1, spread), merge, shrink, expand,
    )
    return outs[:4], outs[4 : 4 + slots], outs[4 + slots :]


def cut_out(keep_ref, give_ref, total_ref, place_ref, bands, steps, rows_each):
    rank, side = place_ref[2], place_ref[3]
    for at, code in codes(steps):
        other, far = code & 1, code >> 1
        for out, core in ((keep_ref, 0), (give_ref, 1)):
            offset = pl.multiple_of((rank ^ (far << 1 | core)) * rows_each, rows_each)
            start = 0
            for first, wide in bands:
                column = pl.multiple_of(first + (side ^ other) * wide, 128)
                out[at + (slice(None), slice(start, start + wide))] = total_ref[
                    pl.ds(offset, rows_each), pl.ds(column, wide)
                ].astype(bf16)
                start += wide


def shrink_kernel(
    place_ref, hidden_ref, branch_ref, keep_ref, give_ref, total_ref, *, steps, rows_each
):
    spread, width = total_ref.shape
    for at in range(0, spread, WIDE):
        total_ref[at : at + WIDE, :] = dot_tn(hidden_ref[:, at : at + WIDE], branch_ref[...])
    cut_out(
        keep_ref, give_ref, total_ref, place_ref, ((0, width // 2),), steps, rows_each
    )


def expand_kernel(
    place_ref, second_ref, expanded_ref, mixed_ref, mix_ref, keep_ref, give_ref, total_ref,
    *, steps, rows_each,
):
    width, spread = second_ref.shape[1], expanded_ref.shape[1]
    turned = second_ref[...].T
    for at in range(0, spread, WIDE):
        total_ref[:, at : at + WIDE] = dot(turned, expanded_ref[:, at : at + WIDE])
    total_ref[:, spread:] = dot(mixed_ref[...].T, mix_ref[...])
    cut_out(
        keep_ref, give_ref, total_ref, place_ref,
        ((0, spread // 2), (spread, width // 2)), steps, rows_each,
    )


def outer_call(kernel, place, operands, rows, columns, steps, size, name):
    rows_each = rows // size
    out = jax.ShapeDtypeStruct((2,) * len(steps) + (rows_each, columns // 2), bf16)
    return pl.pallas_call(
        functools.partial(kernel, steps=steps, rows_each=rows_each),
        out_shape=(out, out),
        in_specs=[pl.BlockSpec(memory_space=pltpu.SMEM)] + [vmem_spec()] * len(operands),
        out_specs=(vmem_spec(),) * 2,
        scratch_shapes=[pltpu.VMEM((rows, columns), f32)],
        compiler_params=params(OUTER_MIB),
        cost_estimate=cost(2 << 30, 10 << 20),
        name=name,
    )(place, *operands)


def settle_kernel(place_ref, *refs):
    out = refs[-1]
    for k, ref in enumerate(refs[:-1]):
        out[place_ref[0] ^ k] = ref[...]


def settle_call(place, blocks):
    return pl.pallas_call(
        settle_kernel,
        out_shape=jax.ShapeDtypeStruct((len(blocks),) + blocks[0].shape, blocks[0].dtype),
        in_specs=[pl.BlockSpec(memory_space=pltpu.SMEM)] + [vmem_spec()] * len(blocks),
        out_specs=vmem_spec(),
        compiler_params=params(8),
        name="settle",
    )(place, *blocks)


def heads_kernel(place_ref, *refs, groups, gains):
    joined_out, gains_out, held_ref = refs[-3:]
    pieces = refs[:-3]
    sums = []
    for u, ref in enumerate(pieces):
        held_ref[place_ref[1] ^ u] = ref[0].astype(f32)
        sums.append(ref[1].astype(f32))
    piece = pieces[0].shape[2] // 3
    for part in range(3):
        for g in range(groups):
            start = (part * groups + g) * piece
            joined_out[:, start : start + piece] = held_ref[
                g, :, part * piece : (part + 1) * piece
            ].astype(joined_out.dtype)
    while len(sums) > 1:
        sums = [sums[i] + sums[i + 1] for i in range(0, len(sums), 2)]
    wide = 3 * piece
    for r in range(-(-gains // wide)):
        end = min((r + 1) * wide, gains)
        gains_out[:, r * wide : end] = sums[0][r : r + 1, : end - r * wide]


def heads_call(place, blocks, width, gains, dtype):
    _, rows, wide = blocks[0].shape
    return pl.pallas_call(
        functools.partial(heads_kernel, groups=3 * width // wide, gains=gains),
        out_shape=(
            jax.ShapeDtypeStruct((rows, 3 * width), dtype),
            jax.ShapeDtypeStruct((1, gains), f32),
        ),
        in_specs=[pl.BlockSpec(memory_space=pltpu.SMEM)] + [vmem_spec()] * len(blocks),
        out_specs=(vmem_spec(),) * 2,
        scratch_shapes=[pltpu.VMEM((len(blocks), rows, wide), f32)],
        compiler_params=params(8),
        name="heads_side_by_side",
    )(place, *blocks)


def input_kernel(*refs, planes, parts):
    input_ref, grad_ref, gain_ref = refs[:3]
    grad = sum(ref[at].astype(f32) for ref, at in zip(refs[3 : 3 + len(parts)], parts))
    outs = refs[3 + len(parts) :]
    normal, rate = normalized(input_ref[...].astype(f32))
    value = grad_ref[...] + norm_back(normal, rate, grad * gain_ref[...])
    seg = value.shape[0] // planes
    for k in range(planes):
        outs[k][...] = value[k * seg : (k + 1) * seg, :].astype(bf16)


def input_call(inputs, grad_middle, gain, held, parts, planes):
    tokens, width = inputs.shape
    return pl.pallas_call(
        functools.partial(input_kernel, planes=planes, parts=parts),
        out_shape=(jax.ShapeDtypeStruct((tokens // planes, width), bf16),) * planes,
        in_specs=[vmem_spec()] * (3 + len(held)),
        out_specs=(vmem_spec(),) * planes,
        compiler_params=params(16),
        name="input_back",
    )(inputs, grad_middle, gain.reshape(1, width), *held)


def swap(value, axis, bits):
    size = lax.axis_size(axis)
    return lax.ppermute(value, axis, [(i, i ^ bits) for i in range(size)])


def pick(value, index, axis=0):
    return lax.dynamic_index_in_dim(value, index, axis, keepdims=False)


def in_hbm(*values):
    return [pltpu.with_memory_space_constraint(value, pltpu.HBM) for value in values]


def bits_of(size):
    return size.bit_length() - 1


def total(values):
    return sum(v.astype(f32) for v in values)


class Halves:
    def __init__(self, bands):
        self.entries = []
        self.bands = bands
        self.chosen = {}

    def hold(self, array, names):
        self.entries.append((array, names))

    def summed(self, choice=()):
        chosen = dict(self.chosen)
        chosen.update(choice)
        values = []
        for array, names in self.entries:
            at = tuple(
                chosen[n] if n in chosen
                else self.bands.get(n, slice(None)) if len(names) == len(self.entries[0][1])
                else slice(None)
                for n in names
            )
            values.append(array[at].astype(f32))
        return sum(values)

    def send(self, name):
        return self.summed({name: 1}).astype(bf16)

    def receive(self, name, array):
        self.chosen[name] = 0
        self.hold(array, [n for n in self.entries[0][1] if n not in self.chosen])


def per_device(
    layer_input, cotangent, doc_lengths, joined_weight, merge_weight, expand_weight,
    shrink_weight, first_gain, mixed_gain, second_gain, hidden_gain,
):
    _, planes, seg, width = layer_input.shape
    size = lax.axis_size("blk")
    slots = size // planes
    batches = lax.axis_size("batch")
    rank = lax.axis_index("blk")
    group_rank = lax.axis_index("batch")
    plane = rank // slots
    slot = rank % slots
    head_count = width // HEAD
    heads = -(-head_count // slots)
    groups = head_count // heads
    piece = heads * HEAD
    tokens = planes * seg
    length = slots * tokens
    side = group_rank % 2
    place = jnp.stack([plane, slot, rank, side]).astype(jnp.int32)

    def to_planes(blocks):
        return [pick(blocks, plane)] + [
            swap(pick(blocks, plane ^ k), "blk", k * slots) for k in range(1, planes)
        ]

    def all_slots(value):
        held = {0: value}
        for bit in reversed(range(bits_of(slots))):
            held.update({u | 1 << bit: swap(v, "blk", 1 << bit) for u, v in held.items()})
        return [held[u] for u in range(slots)]

    def over_slots(blocks):
        return [blocks[0]] + [swap(blocks[u], "blk", u) for u in range(1, slots)]

    spread = expand_weight.shape[1]
    expand_weight, shrink_weight = in_hbm(expand_weight, shrink_weight)
    first_arrived = to_planes(layer_input[0])
    ends = jnp.cumsum(pick(doc_lengths[0], plane), axis=-1)
    positions = jnp.arange(length, dtype=jnp.int32)
    reached = ends[None, :] <= positions[:, None]
    start = jnp.max(jnp.where(reached, ends[None, :], 0), axis=-1, keepdims=True)
    own_start = jnp.minimum(slot, groups - 1) * piece
    own_weight = jnp.concatenate(
        [
            lax.dynamic_slice_in_dim(joined_weight, part * width + own_start, piece, 1)
            for part in range(3)
        ],
        axis=1,
    )
    own_pos = (
        (plane ^ jnp.arange(planes, dtype=jnp.int32))[:, None] * (slots * seg)
        + slot * seg
        + jnp.arange(seg, dtype=jnp.int32)[None, :]
    ).reshape(tokens, 1)
    valid = (own_pos < ends[-1]).astype(f32)
    first_arrived, start, own_weight, valid, cotangent = lax.optimization_barrier(
        (first_arrived, start, own_weight, valid, cotangent)
    )
    arrived = jnp.stack(first_arrived)
    cotangent_blocks = to_planes(cotangent[0])
    pieces = all_slots(arrived)
    (first, joined), sent, shares = forward_call(
        place, start, first_gain.reshape(1, width), own_weight, pieces
    )
    sent, cotangent_blocks = lax.optimization_barrier((sent, cotangent_blocks))
    input_rows = arrived.reshape(tokens, width)
    (
        mixed, middle, second, hidden, normal, slope, held, mixed_rate, hidden_rate, branch,
    ) = widen_call(
        place, over_slots(sent), cotangent_blocks, valid, input_rows, mixed_gain, second_gain,
        hidden_gain, merge_weight, expand_weight,
    )

    row_bits = list(range(1, bits_of(slots)))
    plane_bits = list(range(bits_of(slots), bits_of(size)))
    names = ["side"] + row_bits + plane_bits + ["rows", "columns"]
    steps = [0] + row_bits + plane_bits

    def cross(name, value):
        return swap(value, "batch", 1) if name == "side" else swap(value, "blk", 1 << name)

    def chains(axis, cut, keep, arrived):
        both = []
        for band in (slice(0, cut), slice(cut, None)):
            chain = Halves({axis: band})
            chain.hold(keep, names)
            chain.hold(arrived, names)
            both.append(chain)
        return both

    shrink_keep, shrink_give = outer_call(
        shrink_kernel, place, [hidden, branch], spread, width, steps, size, "shrink_outer"
    )
    shrink_got = swap(shrink_give, "blk", 1)
    (expanded, mix, grad_middle, parts), away, results = turn_call(
        place, branch, hidden, normal, slope, middle, held, mixed_rate, hidden_rate,
        mixed_gain, second_gain, hidden_gain, merge_weight, shrink_weight, expand_weight, planes,
    )
    orders = (["side"] + row_bits, row_bits + ["side"])
    stages = len(orders[0])

    def depart(pair, at):
        return [
            cross(order[at], chain.send(order[at])) for chain, order in zip(pair, orders)
        ]

    def arrive(pair, at, values):
        for chain, order, value in zip(pair, orders, values):
            chain.receive(order[at], value)

    def plane_depart(pair, bit, axis):
        return cross(bit, jnp.concatenate([chain.send(bit) for chain in pair], axis=axis))

    def plane_arrive(pair, bit, axis, both):
        if axis == -2:
            cut = pair[0].bands["rows"].stop
            values = both[..., :cut, :], both[..., cut:, :]
        else:
            cut = pair[0].bands["columns"].stop
            values = both[..., :cut], both[..., cut:]
        for chain, value in zip(pair, values):
            chain.receive(bit, value)

    def closed(pair, axis):
        value = jnp.concatenate([chain.summed() for chain in pair], axis=axis).astype(bf16)
        for bit in range(1, bits_of(batches)):
            value = total([value, swap(value, "batch", 1 << bit)]).astype(bf16)
        return value

    def both_sides(value):
        other = swap(value, "batch", 1)
        return jnp.where(side == 0, value, other), jnp.where(side == 0, other, value)

    returned = over_slots(away)
    expand_keep, expand_give = outer_call(
        expand_kernel, place, [second, expanded, mixed, mix], width, spread + width, steps, size,
        "expand_outer",
    )
    returned, expand_give, shrink_got, results = lax.optimization_barrier(
        (returned, expand_give, shrink_got, results)
    )
    shrink_chains = chains("rows", spread // size // 2, shrink_keep, shrink_got)
    expand_got = swap(expand_give, "blk", 1)
    shrink_sent = depart(shrink_chains, 0)
    result_blocks = [results[0]] + [
        swap(results[k], "blk", k * slots) for k in range(1, planes)
    ]
    rows_each = width // size
    joined_sides = 2 if batches > 1 and rows_each % 16 == 0 else 1
    joined_keep, joined_give, branch_keep, branch_give = backward_call(
        place, *in_hbm(first, joined), own_weight, first_gain.reshape(width, 1), parts,
        returned, in_hbm(*shares), planes, joined_sides,
    )
    (
        joined_give, branch_give, shrink_sent, expand_got, result_blocks,
    ) = lax.optimization_barrier(
        (joined_give, branch_give, shrink_sent, expand_got, result_blocks)
    )
    expand_chains = chains(
        "columns", ((spread + width) // 4 + 127) // 128 * 128, expand_keep, expand_got
    )
    arrive(shrink_chains, 0, shrink_sent)

    joined_held, batch_bits = [joined_keep], list(range(bits_of(batches)))
    branch_got = swap(branch_give, "blk", 1)
    for at in range(1, stages):
        shrink_sent = depart(shrink_chains, at)
        if at < stages - 1:
            arrive(shrink_chains, at, shrink_sent)
    expand_sent = depart(expand_chains, 0)
    if joined_sides > 1:
        joined_held.append(swap(joined_give, "batch", 1))
        batch_bits = batch_bits[1:]
    shrink_sent, joined_held, branch_got = lax.optimization_barrier(
        (shrink_sent, joined_held, branch_got)
    )
    arrive(shrink_chains, stages - 1, shrink_sent)

    blocks = planes * slots
    gains = sum(v[blocks].astype(f32) for v in joined_held)
    joined_sum = [v[:blocks] for v in joined_held]

    def joined_depart(bit):
        half = joined_sum[0].shape[0] // 2
        give = sum(v[half:].astype(f32) for v in joined_sum).astype(bf16)
        return swap(jnp.concatenate([give, gains.astype(bf16)[None]]), "blk", 1 << bit)

    def joined_arrive(got):
        half = got.shape[0] - 1
        return (
            [v[:half] for v in joined_sum] + [got[:half]],
            gains.astype(bf16).astype(f32) + got[half].astype(f32),
        )

    joined_got = joined_depart(plane_bits[0])
    shrink_both = plane_depart(shrink_chains, plane_bits[0], -2)
    branch_held, prefixes = [branch_keep, branch_got], [(), ()]
    for bit in row_bits:
        give = sum(v[p + (1,)].astype(f32) for v, p in zip(branch_held, prefixes)).astype(bf16)
        prefixes = [p + (0,) for p in prefixes] + [()]
        branch_held.append(swap(give, "blk", 1 << bit))
    joined_got, shrink_both, expand_sent, branch_held = lax.optimization_barrier(
        (joined_got, shrink_both, expand_sent, branch_held)
    )
    joined_sum, gains = joined_arrive(joined_got)
    plane_arrive(shrink_chains, plane_bits[0], -2, shrink_both)
    arrive(expand_chains, 0, expand_sent)

    for at in range(1, stages):
        expand_sent = depart(expand_chains, at)
        if at < stages - 1:
            arrive(expand_chains, at, expand_sent)
    input_blocks = input_call(
        input_rows, grad_middle, first_gain, branch_held, prefixes, planes
    )
    for bit in plane_bits[1:]:
        joined_sum, gains = joined_arrive(joined_depart(bit))
        plane_arrive(shrink_chains, bit, -2, plane_depart(shrink_chains, bit, -2))
    shrink_last, joined_last = closed(shrink_chains, -2), jnp.concatenate(
        [sum(v.astype(f32) for v in joined_sum), gains[None]]
    ).astype(bf16)
    expand_sent, shrink_last, joined_last = lax.optimization_barrier(
        (expand_sent, shrink_last, joined_last)
    )
    arrive(expand_chains, stages - 1, expand_sent)

    expand_both = plane_depart(expand_chains, plane_bits[0], -1)
    input_blocks = [input_blocks[0]] + [
        swap(input_blocks[k], "blk", k * slots) for k in range(1, planes)
    ]
    for bit in batch_bits:
        joined_last = total([joined_last, swap(joined_last, "batch", 1 << bit)]).astype(bf16)
    shrink_lower, shrink_upper = both_sides(shrink_last)
    shrink_grad = jnp.concatenate([shrink_lower, shrink_upper], axis=1).astype(f32)
    joined_half, gain_row = heads_call(
        place,
        [jnp.stack([joined_last[0], joined_last[slots]])]
        + [
            swap(jnp.stack([joined_last[u], joined_last[slots]]), "blk", u)
            for u in range(1, slots)
        ],
        width, 3 * width + spread, f32 if joined_sides == 1 else bf16,
    )
    expand_both, input_blocks, joined_half, shrink_grad = lax.optimization_barrier(
        (expand_both, input_blocks, joined_half, shrink_grad)
    )
    plane_arrive(expand_chains, plane_bits[0], -1, expand_both)
    for bit in plane_bits[1:]:
        plane_arrive(expand_chains, bit, -1, plane_depart(expand_chains, bit, -1))
    expand_lower, expand_upper = both_sides(closed(expand_chains, -1))
    cut = spread // 2
    expand_grad = jnp.concatenate([expand_lower[:, :cut], expand_upper[:, :cut]], axis=1)
    merge_grad = jnp.concatenate([expand_lower[:, cut:], expand_upper[:, cut:]], axis=1)
    if joined_sides == 1:
        joined_grad = joined_half
    else:
        joined_grad = jnp.concatenate(both_sides(joined_half), axis=0).astype(f32)
    layer_result = settle_call(place, result_blocks).reshape(layer_input.shape)
    input_grad = settle_call(place, input_blocks).reshape(layer_input.shape)
    gain_row = gain_row[0]
    return (
        layer_result, input_grad, joined_grad, merge_grad.astype(f32), expand_grad.astype(f32),
        shrink_grad, gain_row[:width], gain_row[width : 2 * width],
        gain_row[2 * width : 3 * width], gain_row[3 * width :],
    )


def solution(mesh):
    rows = P("batch", None, "blk", None)
    return jax.shard_map(
        per_device,
        mesh=mesh,
        in_specs=(rows, rows, P("batch", None, None)) + (P(),) * 8,
        out_specs=(rows, rows) + (P("blk", None),) * 4 + (P(),) * 4,
        check_vma=False,
    )
```

```python
import functools

import jax
import jax.numpy as jnp
from jax import lax
from jax.experimental import pallas as pl
from jax.experimental.pallas import tpu as pltpu
from jax.sharding import PartitionSpec as P

HEAD = 64
TILE = 256
WIDE = 512
BAND = 384
FORWARD_MIB = 24
BACKWARD_MIB = 24
WIDEN_MIB = 16
TURN_MIB = 20
OUTER_MIB = 16
big_negative = -1e30
norm_epsilon = 1e-05

f32 = jnp.float32
bf16 = jnp.bfloat16


def dot(left, right):
    return jnp.dot(left, right, preferred_element_type=f32)


def dot_nt(left, right):
    return lax.dot_general(left, right, (((1,), (1,)), ((), ())), preferred_element_type=f32)


def dot_tn(left, right):
    return lax.dot_general(left, right, (((0,), (0,)), ((), ())), preferred_element_type=f32)


def normalized(values):
    centred = values - jnp.mean(values, axis=-1, keepdims=True)
    rate = lax.rsqrt(jnp.mean(centred * centred, axis=-1, keepdims=True) + norm_epsilon)
    return centred * rate, rate


def norm_back(normal, rate, weighted):
    return rate * (
        weighted
        - jnp.mean(weighted, axis=-1, keepdims=True)
        - normal * jnp.mean(weighted * normal, axis=-1, keepdims=True)
    )


def vmem_spec():
    return pl.BlockSpec(memory_space=pltpu.VMEM)


def hbm_spec():
    return pl.BlockSpec(memory_space=pltpu.HBM)


def params(mebibytes):
    return pltpu.CompilerParams(vmem_limit_bytes=mebibytes * 1024 * 1024)


def cost(flops, moved):
    return pl.CostEstimate(flops=flops, bytes_accessed=moved, transcendentals=0)


def codes(steps):
    listed = [((), 0)]
    for bit in steps:
        listed = [(at + (b,), code | (b << bit)) for at, code in listed for b in (0, 1)]
    return listed


def forward_kernel(*refs, planes, slots, seg, heads):
    place_ref, start_ref, gain_ref, weight_ref = refs[:4]
    pieces = refs[4 : 4 + slots]
    refs = refs[4 + slots :]
    length = planes * slots * seg
    tiles = length // TILE
    first_to, joined_to = refs[:2]
    sent = refs[2 : 2 + slots]
    shares_to = refs[2 + slots : 2 + slots + tiles]
    rows_ref, first_ref, joined_ref, attention_ref = refs[2 + slots + tiles : 6 + slots + tiles]
    shares = refs[6 + slots + tiles : 6 + slots + 2 * tiles]
    ready = refs[-1]
    copies = [
        pltpu.make_async_copy(source, target, ready.at[at])
        for at, (source, target) in enumerate(
            zip((first_ref, joined_ref) + shares, (first_to, joined_to) + shares_to)
        )
    ]
    plane, slot = place_ref[0], place_ref[1]
    for u in range(slots):
        for k in range(planes):
            offset = ((plane ^ k) * slots + (slot ^ u)) * seg
            rows_ref[pl.ds(pl.multiple_of(offset, seg), seg), :] = pieces[u][k]
    width = heads * HEAD

    def project(tile, carry):
        rows = pl.ds(pl.multiple_of(tile * TILE, TILE), TILE)
        normal, _ = normalized(rows_ref[rows, :].astype(f32))
        first = (normal * gain_ref[...]).astype(bf16)
        first_ref[rows, :] = first
        joined = dot(first, weight_ref[...]).astype(bf16)
        for part in range(3):
            for h in range(heads):
                column = part * width + h * HEAD
                value = joined[:, column : column + HEAD]
                if part == 0:
                    value = value * jnp.asarray(0.125, bf16)
                joined_ref[part * heads + h, rows, :] = value
        return carry

    lax.fori_loop(0, tiles, project, 0)
    copies[0].start()
    copies[1].start()
    for q in reversed(range(tiles)):
        rows = slice(q * TILE, (q + 1) * TILE)
        reach = (q + 1) * TILE
        query_pos = q * TILE + lax.broadcasted_iota(jnp.int32, (TILE, reach), 0)
        key_pos = lax.broadcasted_iota(jnp.int32, (TILE, reach), 1)
        allowed = (key_pos <= query_pos) & (key_pos >= start_ref[rows, :])
        for h in range(heads):
            scores = dot_nt(joined_ref[h, rows, :], joined_ref[heads + h, :reach, :])
            scores = jnp.where(allowed, scores, big_negative)
            peak = jnp.max(scores, axis=-1, keepdims=True)
            raised = jnp.exp(scores - peak)
            total = jnp.sum(raised, axis=-1, keepdims=True)
            share = (raised * (1.0 / total)).astype(bf16)
            shares[q][h] = share
            attention_ref[h, rows, :] = dot(share, joined_ref[2 * heads + h, :reach, :])
        copies[2 + q].start()
    half = planes // 2
    for u in range(slots):
        for k in range(planes):
            offset = ((plane ^ k) * slots + (slot ^ u)) * seg
            rows = slice(k % half * seg, (k % half + 1) * seg)
            for h in range(heads):
                part = attention_ref[h, pl.ds(pl.multiple_of(offset, seg), seg), :]
                column = k // half * width + h * HEAD
                sent[u][rows, column : column + HEAD] = part.astype(bf16)
    for copy in copies:
        copy.wait()


def forward_call(place, start, gain, weight, pieces):
    slots = len(pieces)
    planes, seg, width = pieces[0].shape
    length = planes * slots * seg
    heads = weight.shape[1] // (3 * HEAD)
    kernel = functools.partial(forward_kernel, planes=planes, slots=slots, seg=seg, heads=heads)
    packed = jax.ShapeDtypeStruct((planes * seg // 2, 2 * heads * HEAD), bf16)
    tiled = [(heads, TILE, reach) for reach in range(TILE, length + 1, TILE)]
    outs = pl.pallas_call(
        kernel,
        out_shape=(
            pltpu.HBM((length, width), bf16),
            pltpu.HBM((3 * heads, length, HEAD), bf16),
        )
        + (packed,) * slots
        + tuple(pltpu.HBM(shape, bf16) for shape in tiled),
        in_specs=[pl.BlockSpec(memory_space=pltpu.SMEM)] + [vmem_spec()] * (3 + slots),
        out_specs=(hbm_spec(),) * 2 + (vmem_spec(),) * slots + (hbm_spec(),) * len(tiled),
        scratch_shapes=[
            pltpu.VMEM((length, width), bf16),
            pltpu.VMEM((length, width), bf16),
            pltpu.VMEM((3 * heads, length, HEAD), bf16),
            pltpu.VMEM((heads, length, HEAD), f32),
        ]
        + [pltpu.VMEM(shape, bf16) for shape in tiled]
        + [pltpu.SemaphoreType.DMA((2 + len(tiled),))],
        compiler_params=params(FORWARD_MIB * length // 1024),
        cost_estimate=cost(8 << 30, 8 << 20),
        name="attention_forward",
    )(place, start, gain, weight, *pieces)
    return outs[:2], outs[2 : 2 + slots], outs[2 + slots :]


def backward_kernel(*refs, planes, slots, seg, heads, rows_each):
    place_ref, first_from, joined_from, weight_ref, gain_ref, parts_ref = refs[:6]
    pieces = refs[6 : 6 + slots]
    length = planes * slots * seg
    tiles = length // TILE
    refs = refs[6 + slots :]
    shares_from = refs[:tiles]
    joined_out, branch_keep, branch_give = refs[tiles : tiles + 3]
    (
        grad_ref, arrived_ref, key_ref, value_ref, total_ref, outer_ref, row_ref,
        first_ref, joined_ref,
    ) = refs[tiles + 3 : tiles + 12]
    shares = refs[tiles + 12 : 2 * tiles + 12]
    ready = refs[-1]
    copies = [
        pltpu.make_async_copy(source, target, ready.at[at])
        for at, (source, target) in enumerate(
            zip((joined_from, first_from) + shares_from, (joined_ref, first_ref) + shares)
        )
    ]
    copies[0].start()
    for q in reversed(range(tiles)):
        copies[2 + q].start()
    copies[1].start()
    plane, slot = place_ref[0], place_ref[1]
    width = heads * HEAD
    half = planes // 2
    for u in range(slots):
        for k in range(planes):
            offset = ((plane ^ k) * slots + (slot ^ u)) * seg
            column = k // half * width
            arrived_ref[pl.ds(pl.multiple_of(offset, seg), seg), :] = pieces[u][
                k % half * seg : (k % half + 1) * seg, column : column + width
            ]
    copies[0].wait()
    for h in range(heads):
        for q in reversed(range(tiles)):
            rows = slice(q * TILE, (q + 1) * TILE)
            reach = (q + 1) * TILE
            grad = arrived_ref[rows, h * HEAD : (h + 1) * HEAD]
            if h == 0:
                copies[2 + q].wait()
            share = shares[q][h]
            product = share.astype(f32) * dot_nt(grad, joined_ref[2 * heads + h, :reach, :])
            inner = jnp.sum(product, axis=-1, keepdims=True)
            grad_scores = (product - share.astype(f32) * inner).astype(bf16)
            query_grad = dot(grad_scores, joined_ref[heads + h, :reach, :]) * 0.125
            grad_ref[rows, h * HEAD : (h + 1) * HEAD] = query_grad.astype(bf16)
            key_add = dot_tn(joined_ref[h, rows, :], grad_scores)
            value_add = dot_tn(grad, share)
            if q == tiles - 1:
                key_ref[...] = key_add
                value_ref[...] = value_add
            else:
                key_ref[:, :reach] += key_add
                value_ref[:, :reach] += value_add
        for part, source in ((1, key_ref), (2, value_ref)):
            column = part * width + h * HEAD
            for q in range(tiles):
                rows = slice(q * TILE, (q + 1) * TILE)
                grad_ref[rows, column : column + HEAD] = source[:, rows].T.astype(bf16)

    def back(tile, carry):
        rows = pl.ds(pl.multiple_of(tile * TILE, TILE), TILE)
        total_ref[rows, :] = dot_nt(grad_ref[rows, :], weight_ref[...])
        return carry

    lax.fori_loop(0, tiles, back, 0)
    for at, code in codes(range(1, bits_of(slots))):
        for out, u in ((branch_keep, code), (branch_give, code | 1)):
            for k in range(planes):
                offset = ((plane ^ k) * slots + (slot ^ u)) * seg
                out[at + (slice(k * seg, (k + 1) * seg),)] = total_ref[
                    pl.ds(pl.multiple_of(offset, seg), seg), :
                ].astype(bf16)
    model = first_ref.shape[1]
    copies[1].wait()
    for d in range(0, model, TILE):
        outer = dot_tn(first_ref[:, d : d + TILE], grad_ref[...])
        outer_ref[d : d + TILE, :] = outer
        scaled = jnp.sum(outer * weight_ref[d : d + TILE, :].astype(f32), axis=-1, keepdims=True)
        scaled = jnp.broadcast_to(scaled / gain_ref[d : d + TILE, :], (TILE, 128)).T
        row_ref[:, d : d + TILE] = scaled[:1]
    wide = 3 * width
    row_ref[:, model : model + parts_ref.shape[1]] = parts_ref[...]
    gains = model + parts_ref.shape[1]
    at = 0
    for _, code in codes(range(bits_of(planes))):
        for u in range(slots):
            offset = ((plane ^ code) * slots + (slot ^ u)) * rows_each
            joined_out[at] = outer_ref[
                pl.ds(pl.multiple_of(offset, rows_each), rows_each), :
            ].astype(bf16)
            at += 1
    joined_out[at] = jnp.zeros((rows_each, wide), bf16)
    for r in range(-(-gains // wide)):
        end = min((r + 1) * wide, gains)
        joined_out[at, r : r + 1, : end - r * wide] = row_ref[:, r * wide : end].astype(bf16)


def backward_call(
    place, first, joined, weight, gain, parts, pieces, shares, planes
):
    slots = len(pieces)
    tokens = pieces[0].shape[0] * 2
    heads, length = joined.shape[0] // 3, joined.shape[1]
    width = weight.shape[0]
    rows_each = width // (planes * slots)
    kernel = functools.partial(
        backward_kernel, planes=planes, slots=slots, seg=tokens // planes, heads=heads,
        rows_each=rows_each,
    )
    pairs = (2,) * (bits_of(slots) - 1)
    wide = 3 * heads * HEAD
    row = -(-(width + parts.shape[1]) // 128) * 128
    return pl.pallas_call(
        kernel,
        out_shape=(
            jax.ShapeDtypeStruct((planes * slots + 1, rows_each, wide), bf16),
            jax.ShapeDtypeStruct(pairs + (tokens, width), bf16),
            jax.ShapeDtypeStruct(pairs + (tokens, width), bf16),
        ),
        in_specs=[pl.BlockSpec(memory_space=pltpu.SMEM)]
        + [hbm_spec()] * 2
        + [vmem_spec()] * (3 + slots)
        + [hbm_spec()] * len(shares),
        out_specs=(vmem_spec(),) * 3,
        scratch_shapes=[
            pltpu.VMEM((length, wide), bf16),
            pltpu.VMEM((length, heads * HEAD), bf16),
            pltpu.VMEM((HEAD, length), f32),
            pltpu.VMEM((HEAD, length), f32),
            pltpu.VMEM((length, width), f32),
            pltpu.VMEM((width, wide), f32),
            pltpu.VMEM((1, row), f32),
            pltpu.VMEM(first.shape, bf16),
            pltpu.VMEM(joined.shape, bf16),
        ]
        + [pltpu.VMEM(share.shape, bf16) for share in shares]
        + [pltpu.SemaphoreType.DMA((2 + len(shares),))],
        compiler_params=params(BACKWARD_MIB * length // 1024),
        cost_estimate=cost(10 << 30, 10 << 20),
        name="attention_backward",
    )(place, first, joined, weight, gain, parts, *pieces, *shares)


def widen_kernel(*refs, slots, planes, groups, width, spread, block):
    place_ref = refs[0]
    pieces = refs[1 : 1 + slots]
    blocks = refs[1 + slots : 1 + slots + planes]
    refs = refs[1 + slots + planes :]
    (
        valid_ref, input_ref, mixed_gain_ref, second_gain_ref, hidden_gain_ref, merge_ref, expand_from,
    ) = refs[:7]
    (
        mixed_ref, middle_ref, second_ref, hidden_ref, hidden_give_ref, normal_ref, slope_ref,
        held_ref, mixed_rate_ref, hidden_rate_ref, branch_ref,
    ) = refs[7:18]
    expand_ref, gelu_ref, ready = refs[18:]
    steps = spread // WIDE

    def copy(step):
        at = pl.ds(step * WIDE, WIDE)
        return pltpu.make_async_copy(
            expand_from.at[:, at], expand_ref.at[:, at], ready.at[step]
        )

    for step in range(steps):
        copy(step).start()
    slot = place_ref[1]
    piece = width // groups
    tokens = input_ref.shape[0]
    half = tokens // 2
    for u in range(slots):
        for side in range(2):
            held_ref[slot ^ u, side * half : (side + 1) * half, :] = pieces[u][
                :, side * piece : (side + 1) * piece
            ].astype(f32)
    mean = sum(jnp.sum(held_ref[g], axis=-1, keepdims=True) for g in range(groups)) * (1.0 / width)
    square = 0.0
    for g in range(groups):
        centred = held_ref[g] - mean
        held_ref[g] = centred
        square = square + jnp.sum(centred * centred, axis=-1, keepdims=True)
    mixed_rate = lax.rsqrt(square * (1.0 / width) + norm_epsilon)
    mixed_rate_ref[...] = mixed_rate
    middle = input_ref[...].astype(f32)
    for g in range(groups):
        normal = held_ref[g] * mixed_rate
        held_ref[g] = normal
        mixed = (normal * mixed_gain_ref[g]).astype(bf16)
        mixed_ref[:, g * piece : (g + 1) * piece] = mixed
        middle = middle + dot(mixed, merge_ref[g * piece : (g + 1) * piece, :])
    middle_ref[...] = middle
    seg = tokens // planes
    for k in range(planes):
        at = slice(k * seg, (k + 1) * seg)
        branch_ref[at, :] = (blocks[k][...].astype(f32) * valid_ref[at, :]).astype(bf16)
    second_normal, _ = normalized(middle)
    second = (second_normal * second_gain_ref[...]).astype(bf16)
    second_ref[...] = second
    total = jnp.zeros((tokens, 1), f32)
    for step in range(steps):
        copy(step).wait()
        at = slice(step * WIDE, (step + 1) * WIDE)
        value = dot(second, expand_ref[:, at])
        share = 0.5 * (1.0 + lax.erf(value * 0.7071067811865476))
        gelu = value * share
        gelu_ref[:, at] = gelu
        slope = share + value * (0.3989422804014327 * jnp.exp(-0.5 * value * value))
        slope_ref[:, at] = slope.astype(bf16)
        total = total + jnp.sum(gelu, axis=-1, keepdims=True)
    mean = total * (1.0 / spread)
    total = jnp.zeros((tokens, 1), f32)
    for step in range(steps):
        centred = gelu_ref[:, step * WIDE : (step + 1) * WIDE] - mean
        total = total + jnp.sum(centred * centred, axis=-1, keepdims=True)
    rate = lax.rsqrt(total * (1.0 / spread) + norm_epsilon)
    hidden_rate_ref[...] = rate
    core = slot % 2
    for at in range(0, spread, 2 * BAND):
        ours, theirs = [], []
        for start in range(at, at + 2 * BAND, 2 * block):
            low = slice(start, start + block)
            high = slice(start + block, start + 2 * block)
            parts = []
            for part in (low, high):
                normal = (gelu_ref[:, part] - mean) * rate
                normal_ref[:, part] = normal.astype(bf16)
                parts.append((normal * hidden_gain_ref[:, part]).astype(bf16))
            ours.append(parts[0])
            theirs.append(parts[1])
        even, odd = jnp.concatenate(ours, axis=1), jnp.concatenate(theirs, axis=1)
        half_at = slice(at // 2, at // 2 + BAND)
        hidden_ref[:, half_at] = jnp.where(core == 0, even, odd)
        hidden_give_ref[:, half_at] = jnp.where(core == 0, odd, even)


def widen_call(
    place, pieces, blocks, valid, inputs, mixed_gain, second_gain, hidden_gain, merge, expand
):
    slots = len(pieces)
    tokens = inputs.shape[0]
    piece = pieces[0].shape[1] // 2
    width, spread = expand.shape
    groups = width // piece

    def low(*shape):
        return jax.ShapeDtypeStruct(shape, bf16)

    def full(*shape):
        return jax.ShapeDtypeStruct(shape, f32)

    return pl.pallas_call(
        functools.partial(
            widen_kernel, slots=slots, planes=len(blocks), groups=groups, width=width,
            spread=spread, block=spread // (slots * len(blocks)),
        ),
        out_shape=(
            low(tokens, width),
            full(tokens, width),
            low(tokens, width),
            low(tokens, spread // 2),
            low(tokens, spread // 2),
            low(tokens, spread),
            low(tokens, spread),
            full(slots, tokens, piece),
            full(tokens, 1),
            full(tokens, 1),
            low(tokens, width),
        ),
        in_specs=[pl.BlockSpec(memory_space=pltpu.SMEM)]
        + [vmem_spec()] * (6 + slots + len(blocks))
        + [hbm_spec()],
        out_specs=(vmem_spec(),) * 11,
        scratch_shapes=[
            pltpu.VMEM((width, spread), bf16),
            pltpu.VMEM((tokens, spread), f32),
            pltpu.SemaphoreType.DMA((spread // WIDE,)),
        ],
        compiler_params=params(WIDEN_MIB),
        cost_estimate=cost(6 << 30, 6 << 20),
        name="widen",
    )(
        place, *pieces, *blocks, valid, inputs, mixed_gain.reshape(groups, 1, piece),
        second_gain.reshape(1, width), hidden_gain.reshape(1, spread), merge, expand,
    )


def turn_kernel(*refs, slots, planes, groups, width, spread):
    (
        place_ref, branch_ref, normal_ref, slope_ref, middle_ref, held_ref,
        mixed_rate_ref, hidden_rate_ref,
        mixed_gain_ref, second_gain_ref, hidden_gain_ref, merge_ref, shrink_from, expand_from,
    ) = refs[:14]
    expanded_ref, mix_ref, grad_ref, parts_ref = refs[14:18]
    away = refs[18 : 18 + slots]
    results = refs[18 + slots : 18 + slots + planes]
    shrink_ref, expand_ref, weighted_ref, sent_ref, ready = refs[18 + slots + planes :]
    steps = spread // WIDE

    def copy_shrink(step):
        at = pl.ds(step * WIDE, WIDE)
        return pltpu.make_async_copy(shrink_from.at[at], shrink_ref.at[at], ready.at[step])

    def copy_expand(step):
        at = pl.ds(step * WIDE, WIDE)
        return pltpu.make_async_copy(
            expand_from.at[:, at], expand_ref.at[:, at], ready.at[steps + step]
        )

    for step in range(steps):
        copy_shrink(step).start()
    for step in range(steps):
        copy_expand(step).start()
    slot = place_ref[1]
    piece = width // groups
    tokens = middle_ref.shape[0]
    half = tokens // 2
    branch = branch_ref[...]
    result = middle_ref[...]
    weighted_sum = jnp.zeros((tokens, 1), f32)
    inner_sum = jnp.zeros((tokens, 1), f32)
    for step in range(steps):
        copy_shrink(step).wait()
        at = slice(step * WIDE, (step + 1) * WIDE)
        normal = normal_ref[:, at].astype(f32)
        hidden = (normal * hidden_gain_ref[:, at]).astype(bf16)
        result = result + dot(hidden, shrink_ref[at, :])
        grad_hidden = dot_nt(branch, shrink_ref[at, :])
        start = 2 * width + step * WIDE
        parts_ref[:, start : start + WIDE] = jnp.sum(grad_hidden * normal, axis=0, keepdims=True)
        weighted = grad_hidden * hidden_gain_ref[:, at]
        weighted_ref[:, at] = weighted
        weighted_sum = weighted_sum + jnp.sum(weighted, axis=-1, keepdims=True)
        inner_sum = inner_sum + jnp.sum(weighted * normal, axis=-1, keepdims=True)
    seg = tokens // planes
    for k in range(planes):
        results[k][...] = result[k * seg : (k + 1) * seg, :].astype(bf16)
    weighted_mean = weighted_sum * (1.0 / spread)
    inner_mean = inner_sum * (1.0 / spread)
    rate = hidden_rate_ref[...]
    grad_second = jnp.zeros((tokens, width), f32)
    for step in range(steps):
        copy_expand(step).wait()
        at = slice(step * WIDE, (step + 1) * WIDE)
        grad = rate * (
            weighted_ref[:, at] - weighted_mean - normal_ref[:, at].astype(f32) * inner_mean
        )
        expanded = (grad * slope_ref[:, at].astype(f32)).astype(bf16)
        expanded_ref[:, at] = expanded
        grad_second = grad_second + dot_nt(expanded, expand_ref[:, at])
    second_normal, second_rate = normalized(middle_ref[...])
    parts_ref[:, width : 2 * width] = jnp.sum(grad_second * second_normal, axis=0, keepdims=True)
    grad_middle = branch.astype(f32) + norm_back(
        second_normal, second_rate, grad_second * second_gain_ref[...]
    )
    grad_ref[...] = grad_middle
    mix = grad_middle.astype(bf16)
    mix_ref[...] = mix
    grads = []
    weighted_sum = 0.0
    inner_sum = 0.0
    for g in range(groups):
        grad_mixed = dot_nt(mix, merge_ref[g * piece : (g + 1) * piece, :])
        parts_ref[:, g * piece : (g + 1) * piece] = jnp.sum(
            grad_mixed * held_ref[g], axis=0, keepdims=True
        )
        weighted = grad_mixed * mixed_gain_ref[g]
        grads.append(weighted)
        weighted_sum = weighted_sum + jnp.sum(weighted, axis=-1, keepdims=True)
        inner_sum = inner_sum + jnp.sum(weighted * held_ref[g], axis=-1, keepdims=True)
    weighted_mean = weighted_sum * (1.0 / width)
    inner_mean = inner_sum * (1.0 / width)
    for g in range(slots):
        if g < groups:
            sent_ref[g] = mixed_rate_ref[...] * (
                grads[g] - weighted_mean - held_ref[g] * inner_mean
            )
        else:
            sent_ref[g] = jnp.zeros(sent_ref.shape[1:], f32)
    for u in range(slots):
        for side in range(2):
            away[u][:, side * piece : (side + 1) * piece] = sent_ref[
                slot ^ u, side * half : (side + 1) * half, :
            ].astype(bf16)


def turn_call(
    place, branch, normal, slope, middle, held, mixed_rate, hidden_rate,
    mixed_gain, second_gain, hidden_gain, merge, shrink, expand, planes,
):
    slots, tokens, piece = held.shape
    width, spread = expand.shape
    groups = width // piece

    def low(*shape):
        return jax.ShapeDtypeStruct(shape, bf16)

    def full(*shape):
        return jax.ShapeDtypeStruct(shape, f32)

    outs = pl.pallas_call(
        functools.partial(
            turn_kernel, slots=slots, planes=planes, groups=groups, width=width, spread=spread
        ),
        out_shape=(
            low(tokens, spread),
            low(tokens, width),
            full(tokens, width),
            full(1, 2 * width + spread),
        )
        + (low(tokens // 2, 2 * piece),) * slots
        + (low(tokens // planes, width),) * planes,
        in_specs=[pl.BlockSpec(memory_space=pltpu.SMEM)] + [vmem_spec()] * 11 + [hbm_spec()] * 2,
        out_specs=(vmem_spec(),) * (4 + slots + planes),
        scratch_shapes=[
            pltpu.VMEM((spread, width), bf16),
            pltpu.VMEM((width, spread), bf16),
            pltpu.VMEM((tokens, spread), f32),
            pltpu.VMEM((slots, tokens, piece), f32),
            pltpu.SemaphoreType.DMA((2 * spread // WIDE,)),
        ],
        compiler_params=params(TURN_MIB),
        cost_estimate=cost(9 << 30, 8 << 20),
        name="turn",
    )(
        place, branch, normal, slope, middle, held, mixed_rate, hidden_rate,
        mixed_gain.reshape(groups, 1, piece), second_gain.reshape(1, width),
        hidden_gain.reshape(1, spread), merge, shrink, expand,
    )
    return outs[:4], outs[4 : 4 + slots], outs[4 + slots :]


def cut_out(outs, total_ref, place_ref, bands, steps, rows_each, axis, cut):
    whole_ref, firsts = outs[0], outs[1:]
    far_rank, side = place_ref[2] // 2, place_ref[3]
    for at, code in codes(steps):
        other, far = code & 1, code >> 1
        offset = pl.multiple_of((far_rank ^ far) * rows_each, rows_each)
        parts = []
        for first, wide in bands:
            column = pl.multiple_of(first + (side ^ other) * wide, 128)
            parts.append(
                total_ref[pl.ds(offset, rows_each), pl.ds(column, wide)].astype(bf16)
            )
        value = parts[0] if len(parts) == 1 else jnp.concatenate(parts, axis=1)
        whole_ref[at] = value
        for chain, first_ref in enumerate(firsts):
            if at[chain] == 1:
                band = slice(0, cut) if chain == 0 else slice(cut, None)
                first_ref[at[:chain] + at[chain + 1 :]] = (
                    value[band] if axis == 0 else value[:, band]
                )


def shrink_kernel(
    place_ref, hidden_ref, branch_ref, hidden_got_ref, branch_got_ref, *refs, cutting
):
    total_ref = refs[-1]
    spread, _ = total_ref.shape
    branch = jnp.concatenate([branch_ref[...], branch_got_ref[...]], axis=0)
    for at in range(0, spread, WIDE):
        hidden = jnp.concatenate(
            [hidden_ref[:, at : at + WIDE], hidden_got_ref[:, at : at + WIDE]], axis=0
        )
        total_ref[at : at + WIDE, :] = dot_tn(hidden, branch)
    cut_out(refs[:-1], total_ref, place_ref, **cutting)


def expand_kernel(
    place_ref, second_ref, mixed_ref, second_got_ref, mixed_got_ref,
    expanded_ref, mix_ref, expanded_got_ref, mix_got_ref, *refs, cutting,
):
    turned_ref, total_ref = refs[-2:]
    tokens, spread = expanded_ref.shape
    width = second_ref.shape[1]
    core = place_ref[2] % 2
    rows_each = cutting["rows_each"]

    def left(own_ref, got_ref):
        turned_ref[:, :tokens] = own_ref[...].astype(f32).T
        turned_ref[:, tokens:] = got_ref[...].astype(f32).T
        rows = [
            turned_ref[pl.ds(pl.multiple_of((2 * i + core) * rows_each, rows_each), rows_each), :]
            for i in range(width // (2 * rows_each))
        ]
        return jnp.concatenate(rows, axis=0).astype(bf16)

    second = left(second_ref, second_got_ref)
    for at in range(0, spread, WIDE):
        band = slice(at, at + WIDE)
        total_ref[:, band] = dot(
            second, jnp.concatenate([expanded_ref[:, band], expanded_got_ref[:, band]], axis=0)
        )
    mixed = left(mixed_ref, mixed_got_ref)
    total_ref[:, spread:] = dot(
        mixed, jnp.concatenate([mix_ref[...], mix_got_ref[...]], axis=0)
    )
    cut_out(refs[:-2], total_ref, place_ref, **cutting)


def outer_call(kernel, place, operands, rows, columns, bands, steps, size, axis, cut, scratch, name):
    rows_each = rows // size
    shape = (rows_each, columns // 2)
    low = (cut, shape[1]) if axis == 0 else (shape[0], cut)
    high = (shape[0] - cut, shape[1]) if axis == 0 else (shape[0], shape[1] - cut)
    pairs = (2,) * (len(steps) - 1)
    return pl.pallas_call(
        functools.partial(
            kernel,
            cutting=dict(bands=bands, steps=steps, rows_each=rows_each, axis=axis, cut=cut),
        ),
        out_shape=(
            jax.ShapeDtypeStruct((2,) + pairs + shape, bf16),
            jax.ShapeDtypeStruct(pairs + low, bf16),
            jax.ShapeDtypeStruct(pairs + high, bf16),
        ),
        in_specs=[pl.BlockSpec(memory_space=pltpu.SMEM)] + [vmem_spec()] * len(operands),
        out_specs=(vmem_spec(),) * 3,
        scratch_shapes=scratch + [pltpu.VMEM((rows // 2, columns), f32)],
        compiler_params=params(OUTER_MIB),
        cost_estimate=cost(2 << 30, 10 << 20),
        name=name,
    )(place, *operands)


def settle_kernel(place_ref, *refs):
    out = refs[-1]
    for k, ref in enumerate(refs[:-1]):
        out[place_ref[0] ^ k] = ref[...]


def settle_call(place, blocks):
    return pl.pallas_call(
        settle_kernel,
        out_shape=jax.ShapeDtypeStruct((len(blocks),) + blocks[0].shape, blocks[0].dtype),
        in_specs=[pl.BlockSpec(memory_space=pltpu.SMEM)] + [vmem_spec()] * len(blocks),
        out_specs=vmem_spec(),
        compiler_params=params(8),
        name="settle",
    )(place, *blocks)


def heads_kernel(place_ref, *refs, groups, gains):
    joined_out, gains_out, held_ref = refs[-3:]
    pieces = refs[:-3]
    sums = []
    for u, ref in enumerate(pieces):
        held_ref[place_ref[1] ^ u] = ref[0].astype(f32)
        sums.append(ref[1].astype(f32))
    piece = pieces[0].shape[2] // 3
    for part in range(3):
        for g in range(groups):
            start = (part * groups + g) * piece
            joined_out[:, start : start + piece] = held_ref[
                g, :, part * piece : (part + 1) * piece
            ]
    while len(sums) > 1:
        sums = [sums[i] + sums[i + 1] for i in range(0, len(sums), 2)]
    wide = 3 * piece
    for r in range(-(-gains // wide)):
        end = min((r + 1) * wide, gains)
        gains_out[:, r * wide : end] = sums[0][r : r + 1, : end - r * wide]


def heads_call(place, blocks, width, gains):
    _, rows, wide = blocks[0].shape
    return pl.pallas_call(
        functools.partial(heads_kernel, groups=3 * width // wide, gains=gains),
        out_shape=(
            jax.ShapeDtypeStruct((rows, 3 * width), f32),
            jax.ShapeDtypeStruct((1, gains), f32),
        ),
        in_specs=[pl.BlockSpec(memory_space=pltpu.SMEM)] + [vmem_spec()] * len(blocks),
        out_specs=(vmem_spec(),) * 2,
        scratch_shapes=[pltpu.VMEM((len(blocks), rows, wide), f32)],
        compiler_params=params(8),
        name="heads_side_by_side",
    )(place, *blocks)


def input_kernel(*refs, planes, parts):
    input_ref, grad_ref, gain_ref = refs[:3]
    grad = sum(ref[at].astype(f32) for ref, at in zip(refs[3 : 3 + len(parts)], parts))
    outs = refs[3 + len(parts) :]
    normal, rate = normalized(input_ref[...].astype(f32))
    value = grad_ref[...] + norm_back(normal, rate, grad * gain_ref[...])
    seg = value.shape[0] // planes
    for k in range(planes):
        outs[k][...] = value[k * seg : (k + 1) * seg, :].astype(bf16)


def input_call(inputs, grad_middle, gain, held, parts, planes):
    tokens, width = inputs.shape
    return pl.pallas_call(
        functools.partial(input_kernel, planes=planes, parts=parts),
        out_shape=(jax.ShapeDtypeStruct((tokens // planes, width), bf16),) * planes,
        in_specs=[vmem_spec()] * (3 + len(held)),
        out_specs=(vmem_spec(),) * planes,
        compiler_params=params(16),
        name="input_back",
    )(inputs, grad_middle, gain.reshape(1, width), *held)


def swap(value, axis, bits):
    size = lax.axis_size(axis)
    return lax.ppermute(value, axis, [(i, i ^ bits) for i in range(size)])


def pick(value, index, axis=0):
    return lax.dynamic_index_in_dim(value, index, axis, keepdims=False)


def in_hbm(*values):
    return [pltpu.with_memory_space_constraint(value, pltpu.HBM) for value in values]


def bits_of(size):
    return size.bit_length() - 1


def total(values):
    return sum(v.astype(f32) for v in values)


class Halves:
    def __init__(self, bands):
        self.entries = []
        self.bands = bands
        self.chosen = {}

    def hold(self, array, names):
        self.entries.append((array, names))

    def summed(self, choice=()):
        chosen = dict(self.chosen)
        chosen.update(choice)
        values = []
        for array, names in self.entries:
            at = tuple(
                chosen[n] if n in chosen
                else self.bands.get(n, slice(None)) if len(names) == len(self.entries[0][1])
                else slice(None)
                for n in names
            )
            values.append(array[at].astype(f32))
        return sum(values)

    def send(self, name):
        return self.summed({name: 1}).astype(bf16)

    def receive(self, name, array):
        self.chosen[name] = 0
        self.hold(array, [n for n in self.entries[0][1] if n not in self.chosen])


def per_device(
    layer_input, cotangent, doc_lengths, joined_weight, merge_weight, expand_weight,
    shrink_weight, first_gain, mixed_gain, second_gain, hidden_gain,
):
    _, planes, seg, width = layer_input.shape
    size = lax.axis_size("blk")
    slots = size // planes
    batches = lax.axis_size("batch")
    rank = lax.axis_index("blk")
    group_rank = lax.axis_index("batch")
    plane = rank // slots
    slot = rank % slots
    head_count = width // HEAD
    heads = -(-head_count // slots)
    groups = head_count // heads
    piece = heads * HEAD
    tokens = planes * seg
    length = slots * tokens
    side = group_rank % 2
    place = jnp.stack([plane, slot, rank, side]).astype(jnp.int32)

    def to_planes(blocks):
        return [pick(blocks, plane)] + [
            swap(pick(blocks, plane ^ k), "blk", k * slots) for k in range(1, planes)
        ]

    def all_slots(value):
        held = {0: value}
        for bit in reversed(range(bits_of(slots))):
            held.update({u | 1 << bit: swap(v, "blk", 1 << bit) for u, v in held.items()})
        return [held[u] for u in range(slots)]

    def over_slots(blocks):
        return [blocks[0]] + [swap(blocks[u], "blk", u) for u in range(1, slots)]

    spread = expand_weight.shape[1]
    expand_weight, shrink_weight = in_hbm(expand_weight, shrink_weight)
    first_arrived = to_planes(layer_input[0])
    ends = jnp.cumsum(pick(doc_lengths[0], plane), axis=-1)
    positions = jnp.arange(length, dtype=jnp.int32)
    reached = ends[None, :] <= positions[:, None]
    start = jnp.max(jnp.where(reached, ends[None, :], 0), axis=-1, keepdims=True)
    own_start = jnp.minimum(slot, groups - 1) * piece
    own_weight = jnp.concatenate(
        [
            lax.dynamic_slice_in_dim(joined_weight, part * width + own_start, piece, 1)
            for part in range(3)
        ],
        axis=1,
    )
    own_pos = (
        (plane ^ jnp.arange(planes, dtype=jnp.int32))[:, None] * (slots * seg)
        + slot * seg
        + jnp.arange(seg, dtype=jnp.int32)[None, :]
    ).reshape(tokens, 1)
    valid = (own_pos < ends[-1]).astype(f32)
    first_arrived, start, own_weight, valid, cotangent = lax.optimization_barrier(
        (first_arrived, start, own_weight, valid, cotangent)
    )
    arrived = jnp.stack(first_arrived)
    cotangent_blocks = to_planes(cotangent[0])
    pieces = all_slots(arrived)
    (first, joined), sent, shares = forward_call(
        place, start, first_gain.reshape(1, width), own_weight, pieces
    )
    sent, cotangent_blocks = lax.optimization_barrier((sent, cotangent_blocks))
    input_rows = arrived.reshape(tokens, width)
    (
        mixed, middle, second, hidden, hidden_give, normal, slope, held, mixed_rate, hidden_rate,
        branch,
    ) = widen_call(
        place, over_slots(sent), cotangent_blocks, valid, input_rows, mixed_gain, second_gain,
        hidden_gain, merge_weight, expand_weight,
    )

    row_bits = list(range(1, bits_of(slots)))
    plane_bits = list(range(bits_of(slots), bits_of(size)))
    names = ["side"] + row_bits + plane_bits + ["rows", "columns"]
    steps = [0] + row_bits + plane_bits
    orders = (["side"] + row_bits, row_bits + ["side"])
    stages = len(orders[0])

    def cross(name, value):
        return swap(value, "batch", 1) if name == "side" else swap(value, "blk", 1 << name)

    def chains(axis, cut, whole):
        both = []
        for band in (slice(0, cut), slice(cut, None)):
            chain = Halves({axis: band})
            chain.hold(whole, names)
            both.append(chain)
        return both

    def sends(pair, at):
        return [chain.send(order[at]) for chain, order in zip(pair, orders)]

    def crossed(at, values):
        return [cross(order[at], value) for order, value in zip(orders, values)]

    def arrive(pair, at, values):
        for chain, order, value in zip(pair, orders, values):
            chain.receive(order[at], value)

    def plane_depart(pair, bit, axis):
        return cross(bit, jnp.concatenate([chain.send(bit) for chain in pair], axis=axis))

    def plane_arrive(pair, bit, axis, both):
        if axis == -2:
            cut = pair[0].bands["rows"].stop
            values = both[..., :cut, :], both[..., cut:, :]
        else:
            cut = pair[0].bands["columns"].stop
            values = both[..., :cut], both[..., cut:]
        for chain, value in zip(pair, values):
            chain.receive(bit, value)

    def closed(pair, axis):
        value = jnp.concatenate([chain.summed() for chain in pair], axis=axis).astype(bf16)
        for bit in range(1, bits_of(batches)):
            value = total([value, swap(value, "batch", 1 << bit)]).astype(bf16)
        return value

    def both_sides(value):
        other = swap(value, "batch", 1)
        return jnp.where(side == 0, value, other), jnp.where(side == 0, other, value)

    cut = spread // size // 2
    shrink_whole, *shrink_firsts = outer_call(
        shrink_kernel, place,
        [hidden, branch, swap(hidden_give, "blk", 1), swap(branch, "blk", 1)],
        spread, width, ((0, width // 2),), steps, size, 0, cut, [], "shrink_outer",
    )
    shrink_sent = crossed(0, shrink_firsts)
    second_got, mixed_got = swap(second, "blk", 1), swap(mixed, "blk", 1)
    (expanded, mix, grad_middle, parts), away, results = turn_call(
        place, branch, normal, slope, middle, held, mixed_rate, hidden_rate,
        mixed_gain, second_gain, hidden_gain, merge_weight, shrink_weight, expand_weight, planes,
    )
    shrink_sent, second_got, mixed_got, expanded, mix = lax.optimization_barrier(
        (shrink_sent, second_got, mixed_got, expanded, mix)
    )
    shrink_chains = chains("rows", cut, shrink_whole)
    arrive(shrink_chains, 0, shrink_sent)

    returned = over_slots(away)
    expanded_got, mix_got = swap(expanded, "blk", 1), swap(mix, "blk", 1)
    returned, expanded_got, mix_got = lax.optimization_barrier((returned, expanded_got, mix_got))
    cut = ((spread + width) // 4 + 127) // 128 * 128
    expand_whole, *expand_firsts = outer_call(
        expand_kernel, place,
        [second, mixed, second_got, mixed_got, expanded, mix, expanded_got, mix_got],
        width, spread + width, ((0, spread // 2), (spread, width // 2)), steps, size, 1, cut,
        [pltpu.VMEM((width, 2 * tokens), f32)], "expand_outer",
    )
    for at in range(1, stages):
        shrink_sent = crossed(at, sends(shrink_chains, at))
        if at < stages - 1:
            arrive(shrink_chains, at, shrink_sent)
    expand_firsts, results = lax.optimization_barrier((expand_firsts, results))
    result_blocks = [results[0]] + [
        swap(results[k], "blk", k * slots) for k in range(1, planes)
    ]
    returned, expand_firsts, shrink_sent = lax.optimization_barrier(
        (returned, expand_firsts, shrink_sent)
    )
    arrive(shrink_chains, stages - 1, shrink_sent)
    expand_sent = crossed(0, expand_firsts)
    shrink_both = plane_depart(shrink_chains, plane_bits[0], -2)
    joined_part, branch_keep, branch_give = backward_call(
        place, *in_hbm(first, joined), own_weight, first_gain.reshape(width, 1), parts,
        returned, in_hbm(*shares), planes,
    )
    (
        joined_part, branch_give, shrink_both, expand_sent, result_blocks,
    ) = lax.optimization_barrier(
        (joined_part, branch_give, shrink_both, expand_sent, result_blocks)
    )
    plane_arrive(shrink_chains, plane_bits[0], -2, shrink_both)
    expand_chains = chains("columns", cut, expand_whole)
    arrive(expand_chains, 0, expand_sent)

    blocks = planes * slots
    gains, joined_sum = joined_part[blocks].astype(f32), [joined_part[:blocks]]

    def joined_depart(bit):
        half = joined_sum[0].shape[0] // 2
        give = sum(v[half:].astype(f32) for v in joined_sum).astype(bf16)
        return swap(jnp.concatenate([give, gains.astype(bf16)[None]]), "blk", 1 << bit)

    def joined_arrive(got):
        half = got.shape[0] - 1
        return (
            [v[:half] for v in joined_sum] + [got[:half]],
            gains.astype(bf16).astype(f32) + got[half].astype(f32),
        )

    joined_got = joined_depart(plane_bits[0])
    branch_got = swap(branch_give, "blk", 1)
    for at in range(1, stages):
        expand_sent = crossed(at, sends(expand_chains, at))
        if at < stages - 1:
            arrive(expand_chains, at, expand_sent)
    for bit in plane_bits[1:]:
        shrink_both = plane_depart(shrink_chains, bit, -2)
        if bit != plane_bits[-1]:
            plane_arrive(shrink_chains, bit, -2, shrink_both)
    joined_got, branch_got, expand_sent, shrink_both = lax.optimization_barrier(
        (joined_got, branch_got, expand_sent, shrink_both)
    )
    joined_sum, gains = joined_arrive(joined_got)
    arrive(expand_chains, stages - 1, expand_sent)
    plane_arrive(shrink_chains, plane_bits[-1], -2, shrink_both)

    branch_held, prefixes = [branch_keep, branch_got], [(), ()]
    for bit in row_bits:
        give = sum(v[p + (1,)].astype(f32) for v, p in zip(branch_held, prefixes)).astype(bf16)
        prefixes = [p + (0,) for p in prefixes] + [()]
        branch_held.append(swap(give, "blk", 1 << bit))
    expand_both = plane_depart(expand_chains, plane_bits[0], -1)
    for bit in plane_bits[1:]:
        joined_got = joined_depart(bit)
        if bit != plane_bits[-1]:
            joined_sum, gains = joined_arrive(joined_got)
    joined_got, expand_both, branch_held = lax.optimization_barrier(
        (joined_got, expand_both, branch_held)
    )
    joined_sum, gains = joined_arrive(joined_got)
    plane_arrive(expand_chains, plane_bits[0], -1, expand_both)

    input_blocks = input_call(
        input_rows, grad_middle, first_gain, branch_held, prefixes, planes
    )
    input_blocks = [input_blocks[0]] + [
        swap(input_blocks[k], "blk", k * slots) for k in range(1, planes)
    ]
    joined_last = jnp.concatenate(
        [sum(v.astype(f32) for v in joined_sum), gains[None]]
    ).astype(bf16)
    for bit in range(bits_of(batches)):
        joined_last = total([joined_last, swap(joined_last, "batch", 1 << bit)]).astype(bf16)
    for bit in plane_bits[1:]:
        expand_both = plane_depart(expand_chains, bit, -1)
        if bit != plane_bits[-1]:
            plane_arrive(expand_chains, bit, -1, expand_both)
    joined_last, expand_both = lax.optimization_barrier((joined_last, expand_both))
    plane_arrive(expand_chains, plane_bits[-1], -1, expand_both)

    joined_grad, gain_row = heads_call(
        place,
        [jnp.stack([joined_last[0], joined_last[slots]])]
        + [
            swap(jnp.stack([joined_last[u], joined_last[slots]]), "blk", u)
            for u in range(1, slots)
        ],
        width, 3 * width + spread,
    )
    shrink_lower, shrink_upper = both_sides(closed(shrink_chains, -2))
    shrink_grad = jnp.concatenate([shrink_lower, shrink_upper], axis=1).astype(f32)
    expand_lower, expand_upper = both_sides(closed(expand_chains, -1))
    cut = spread // 2
    expand_grad = jnp.concatenate([expand_lower[:, :cut], expand_upper[:, :cut]], axis=1)
    merge_grad = jnp.concatenate([expand_lower[:, cut:], expand_upper[:, cut:]], axis=1)
    layer_result = settle_call(place, result_blocks).reshape(layer_input.shape)
    input_grad = settle_call(place, input_blocks).reshape(layer_input.shape)
    gain_row = gain_row[0]
    return (
        layer_result, input_grad, joined_grad, merge_grad.astype(f32), expand_grad.astype(f32),
        shrink_grad, gain_row[:width], gain_row[width : 2 * width],
        gain_row[2 * width : 3 * width], gain_row[3 * width :],
    )


def solution(mesh):
    rows = P("batch", None, "blk", None)
    return jax.shard_map(
        per_device,
        mesh=mesh,
        in_specs=(rows, rows, P("batch", None, None)) + (P(),) * 8,
        out_specs=(rows, rows) + (P("blk", None),) * 4 + (P(),) * 4,
        check_vma=False,
    )
```

```python
import functools

import jax
import jax.numpy as jnp
from jax import lax
from jax.experimental import pallas as pl
from jax.experimental.pallas import tpu as pltpu
from jax.sharding import PartitionSpec as P

HEAD = 64
TILE = 256
WIDE = 512
BAND = 384
FORWARD_MIB = 14
BACKWARD_MIB = 14
WIDEN_MIB = 16
TURN_MIB = 20
OUTER_MIB = 16
big_negative = -1e30
norm_epsilon = 1e-05

f32 = jnp.float32
bf16 = jnp.bfloat16


def dot(left, right):
    return jnp.dot(left, right, preferred_element_type=f32)


def dot_nt(left, right):
    return lax.dot_general(left, right, (((1,), (1,)), ((), ())), preferred_element_type=f32)


def dot_tn(left, right):
    return lax.dot_general(left, right, (((0,), (0,)), ((), ())), preferred_element_type=f32)


def normalized(values):
    centred = values - jnp.mean(values, axis=-1, keepdims=True)
    rate = lax.rsqrt(jnp.mean(centred * centred, axis=-1, keepdims=True) + norm_epsilon)
    return centred * rate, rate


def norm_back(normal, rate, weighted):
    return rate * (
        weighted
        - jnp.mean(weighted, axis=-1, keepdims=True)
        - normal * jnp.mean(weighted * normal, axis=-1, keepdims=True)
    )


def vmem_spec():
    return pl.BlockSpec(memory_space=pltpu.VMEM)


def hbm_spec():
    return pl.BlockSpec(memory_space=pltpu.HBM)


def params(mebibytes):
    return pltpu.CompilerParams(vmem_limit_bytes=mebibytes * 1024 * 1024)


def cost(flops, moved):
    return pl.CostEstimate(flops=flops, bytes_accessed=moved, transcendentals=0)


def document_ends(lengths_ref, plane):
    ends, end = [], jnp.int32(0)
    for d in range(lengths_ref.shape[1]):
        end = end + lengths_ref[plane, d]
        ends.append(end)
    return ends


def codes(steps):
    listed = [((), 0)]
    for bit in steps:
        listed = [(at + (b,), code | (b << bit)) for at, code in listed for b in (0, 1)]
    return listed


def forward_kernel(*refs, planes, slots, seg, heads):
    place_ref, lengths_ref, gain_ref, weight_ref = refs[:4]
    pieces = refs[4 : 4 + slots * planes]
    refs = refs[4 + slots * planes :]
    length = planes * slots * seg
    tiles = length // TILE
    first_ref, joined_ref = refs[:2]
    sent = refs[2 : 2 + slots]
    shares = refs[2 + slots : 2 + slots + tiles]
    rows_ref, attention_ref = refs[2 + slots + tiles :]
    plane, slot = place_ref[0], place_ref[1]
    for u in range(slots):
        for k in range(planes):
            offset = ((plane ^ k) * slots + (slot ^ u)) * seg
            rows_ref[pl.ds(pl.multiple_of(offset, seg), seg), :] = pieces[k * slots + u][...]
    width = heads * HEAD

    def project(tile, carry):
        rows = pl.ds(pl.multiple_of(tile * TILE, TILE), TILE)
        normal, _ = normalized(rows_ref[rows, :].astype(f32))
        first = (normal * gain_ref[...]).astype(bf16)
        first_ref[rows, :] = first
        joined = dot(first, weight_ref[...]).astype(bf16)
        for part in range(3):
            for h in range(heads):
                column = part * width + h * HEAD
                value = joined[:, column : column + HEAD]
                if part == 0:
                    value = value * jnp.asarray(0.125, bf16)
                joined_ref[part * heads + h, rows, :] = value
        return carry

    lax.fori_loop(0, tiles, project, 0)
    ends = document_ends(lengths_ref, plane)
    for q in reversed(range(tiles)):
        rows = slice(q * TILE, (q + 1) * TILE)
        reach = (q + 1) * TILE
        places = q * TILE + lax.broadcasted_iota(jnp.int32, (TILE, 1), 0)
        start = jnp.zeros((TILE, 1), jnp.int32)
        for end in ends:
            start = jnp.maximum(start, jnp.where(places >= end, end, 0))
        query_pos = q * TILE + lax.broadcasted_iota(jnp.int32, (TILE, reach), 0)
        key_pos = lax.broadcasted_iota(jnp.int32, (TILE, reach), 1)
        allowed = (key_pos <= query_pos) & (key_pos >= start)
        for h in range(heads):
            scores = dot_nt(joined_ref[h, rows, :], joined_ref[heads + h, :reach, :])
            scores = jnp.where(allowed, scores, big_negative)
            peak = jnp.max(scores, axis=-1, keepdims=True)
            raised = jnp.exp(scores - peak)
            total = jnp.sum(raised, axis=-1, keepdims=True)
            share = (raised * (1.0 / total)).astype(bf16)
            shares[q][h] = share
            attention_ref[h, rows, :] = dot(share, joined_ref[2 * heads + h, :reach, :])
    half = planes // 2
    for u in range(slots):
        for k in range(planes):
            offset = ((plane ^ k) * slots + (slot ^ u)) * seg
            rows = slice(k % half * seg, (k % half + 1) * seg)
            for h in range(heads):
                part = attention_ref[h, pl.ds(pl.multiple_of(offset, seg), seg), :]
                column = k // half * width + h * HEAD
                sent[u][rows, column : column + HEAD] = part.astype(bf16)


def forward_call(place, lengths, gain, weight, pieces):
    planes, slots = len(pieces), len(pieces[0])
    seg, width = pieces[0][0].shape
    length = planes * slots * seg
    heads = weight.shape[1] // (3 * HEAD)
    kernel = functools.partial(forward_kernel, planes=planes, slots=slots, seg=seg, heads=heads)
    packed = jax.ShapeDtypeStruct((planes * seg // 2, 2 * heads * HEAD), bf16)
    tiled = [(heads, TILE, reach) for reach in range(TILE, length + 1, TILE)]
    outs = pl.pallas_call(
        kernel,
        out_shape=(
            pltpu.VMEM((length, width), bf16),
            pltpu.VMEM((3 * heads, length, HEAD), bf16),
        )
        + (packed,) * slots
        + tuple(pltpu.VMEM(shape, bf16) for shape in tiled),
        in_specs=[pl.BlockSpec(memory_space=pltpu.SMEM)] * 2
        + [vmem_spec()] * (2 + slots * planes),
        out_specs=(vmem_spec(),) * (2 + slots + len(tiled)),
        scratch_shapes=[
            pltpu.VMEM((length, width), bf16),
            pltpu.VMEM((heads, length, HEAD), f32),
        ],
        compiler_params=params(FORWARD_MIB * length // 1024),
        cost_estimate=cost(8 << 30, 8 << 20),
        name="attention_forward",
    )(place, lengths, gain, weight, *[block for blocks in pieces for block in blocks])
    return outs[:2], outs[2 : 2 + slots], outs[2 + slots :]


def backward_kernel(*refs, planes, slots, seg, heads, rows_each):
    place_ref, first_ref, joined_ref, weight_ref, gain_ref, parts_ref = refs[:6]
    pieces = refs[6 : 6 + slots]
    length = planes * slots * seg
    tiles = length // TILE
    refs = refs[6 + slots :]
    shares = refs[:tiles]
    joined_out, branch_keep, branch_give = refs[tiles : tiles + 3]
    grad_ref, arrived_ref, key_ref, value_ref, total_ref, outer_ref, row_ref = refs[tiles + 3 :]
    plane, slot = place_ref[0], place_ref[1]
    width = heads * HEAD
    half = planes // 2
    for u in range(slots):
        for k in range(planes):
            offset = ((plane ^ k) * slots + (slot ^ u)) * seg
            column = k // half * width
            arrived_ref[pl.ds(pl.multiple_of(offset, seg), seg), :] = pieces[u][
                k % half * seg : (k % half + 1) * seg, column : column + width
            ]
    for h in range(heads):
        for q in reversed(range(tiles)):
            rows = slice(q * TILE, (q + 1) * TILE)
            reach = (q + 1) * TILE
            grad = arrived_ref[rows, h * HEAD : (h + 1) * HEAD]
            share = shares[q][h]
            product = share.astype(f32) * dot_nt(grad, joined_ref[2 * heads + h, :reach, :])
            inner = jnp.sum(product, axis=-1, keepdims=True)
            grad_scores = (product - share.astype(f32) * inner).astype(bf16)
            query_grad = dot(grad_scores, joined_ref[heads + h, :reach, :]) * 0.125
            grad_ref[rows, h * HEAD : (h + 1) * HEAD] = query_grad.astype(bf16)
            key_add = dot_tn(joined_ref[h, rows, :], grad_scores)
            value_add = dot_tn(grad, share)
            if q == tiles - 1:
                key_ref[...] = key_add
                value_ref[...] = value_add
            else:
                key_ref[:, :reach] += key_add
                value_ref[:, :reach] += value_add
        for part, source in ((1, key_ref), (2, value_ref)):
            column = part * width + h * HEAD
            for q in range(tiles):
                rows = slice(q * TILE, (q + 1) * TILE)
                grad_ref[rows, column : column + HEAD] = source[:, rows].T.astype(bf16)

    def back(tile, carry):
        rows = pl.ds(pl.multiple_of(tile * TILE, TILE), TILE)
        total_ref[rows, :] = dot_nt(grad_ref[rows, :], weight_ref[...])
        return carry

    lax.fori_loop(0, tiles, back, 0)
    for at, code in codes(range(1, bits_of(slots))):
        for out, u in ((branch_keep, code), (branch_give, code | 1)):
            for k in range(planes):
                offset = ((plane ^ k) * slots + (slot ^ u)) * seg
                out[at + (slice(k * seg, (k + 1) * seg),)] = total_ref[
                    pl.ds(pl.multiple_of(offset, seg), seg), :
                ].astype(bf16)
    model = first_ref.shape[1]
    for d in range(0, model, TILE):
        outer = dot_tn(first_ref[:, d : d + TILE], grad_ref[...])
        outer_ref[d : d + TILE, :] = outer
        scaled = jnp.sum(outer * weight_ref[d : d + TILE, :].astype(f32), axis=-1, keepdims=True)
        scaled = jnp.broadcast_to(scaled, (TILE, 128)).T
        row_ref[:, d : d + TILE] = scaled[:1] / gain_ref[:, d : d + TILE]
    wide = 3 * width
    row_ref[:, model : model + parts_ref.shape[1]] = parts_ref[...]
    gains = model + parts_ref.shape[1]
    at = 0
    for _, code in codes(range(bits_of(planes))):
        for u in range(slots):
            offset = ((plane ^ code) * slots + (slot ^ u)) * rows_each
            joined_out[at] = outer_ref[
                pl.ds(pl.multiple_of(offset, rows_each), rows_each), :
            ].astype(bf16)
            at += 1
    joined_out[at] = jnp.zeros((rows_each, wide), bf16)
    for r in range(-(-gains // wide)):
        end = min((r + 1) * wide, gains)
        joined_out[at, r : r + 1, : end - r * wide] = row_ref[:, r * wide : end].astype(bf16)


def backward_call(
    place, first, joined, weight, gain, parts, pieces, shares, planes
):
    slots = len(pieces)
    tokens = pieces[0].shape[0] * 2
    heads, length = joined.shape[0] // 3, joined.shape[1]
    width = weight.shape[0]
    rows_each = width // (planes * slots)
    kernel = functools.partial(
        backward_kernel, planes=planes, slots=slots, seg=tokens // planes, heads=heads,
        rows_each=rows_each,
    )
    pairs = (2,) * (bits_of(slots) - 1)
    wide = 3 * heads * HEAD
    row = -(-(width + parts.shape[1]) // 128) * 128
    return pl.pallas_call(
        kernel,
        out_shape=(
            jax.ShapeDtypeStruct((planes * slots + 1, rows_each, wide), bf16),
            jax.ShapeDtypeStruct(pairs + (tokens, width), bf16),
            jax.ShapeDtypeStruct(pairs + (tokens, width), bf16),
        ),
        in_specs=[pl.BlockSpec(memory_space=pltpu.SMEM)]
        + [vmem_spec()] * (5 + slots + len(shares)),
        out_specs=(vmem_spec(),) * 3,
        scratch_shapes=[
            pltpu.VMEM((length, wide), bf16),
            pltpu.VMEM((length, heads * HEAD), bf16),
            pltpu.VMEM((HEAD, length), f32),
            pltpu.VMEM((HEAD, length), f32),
            pltpu.VMEM((length, width), f32),
            pltpu.VMEM((width, wide), f32),
            pltpu.VMEM((1, row), f32),
        ],
        compiler_params=params(BACKWARD_MIB * length // 1024),
        cost_estimate=cost(10 << 30, 10 << 20),
        name="attention_backward",
    )(place, first, joined, weight, gain, parts, *pieces, *shares)


def widen_kernel(*refs, slots, planes, groups, width, spread, block):
    place_ref = refs[0]
    pieces = refs[1 : 1 + slots]
    inputs = refs[1 + slots : 1 + slots + planes]
    refs = refs[1 + slots + planes :]
    mixed_gain_ref, second_gain_ref, hidden_gain_ref, merge_ref, expand_from = refs[:5]
    (
        mixed_ref, middle_ref, second_ref, hidden_ref, hidden_give_ref, normal_ref, slope_ref,
        held_ref, mixed_rate_ref, hidden_rate_ref,
    ) = refs[5:15]
    expand_ref, gelu_ref, ready = refs[15:]
    steps = spread // WIDE

    def copy(step):
        at = pl.ds(step * WIDE, WIDE)
        return pltpu.make_async_copy(
            expand_from.at[:, at], expand_ref.at[:, at], ready.at[step]
        )

    for step in range(steps):
        copy(step).start()
    slot = place_ref[1]
    piece = width // groups
    tokens = planes * inputs[0].shape[0]
    half = tokens // 2
    for u in range(slots):
        for side in range(2):
            held_ref[slot ^ u, side * half : (side + 1) * half, :] = pieces[u][
                :, side * piece : (side + 1) * piece
            ].astype(f32)
    mean = sum(jnp.sum(held_ref[g], axis=-1, keepdims=True) for g in range(groups)) * (1.0 / width)
    square = 0.0
    for g in range(groups):
        centred = held_ref[g] - mean
        held_ref[g] = centred
        square = square + jnp.sum(centred * centred, axis=-1, keepdims=True)
    mixed_rate = lax.rsqrt(square * (1.0 / width) + norm_epsilon)
    mixed_rate_ref[...] = mixed_rate
    middle = jnp.concatenate([block[...] for block in inputs], axis=0).astype(f32)
    for g in range(groups):
        normal = held_ref[g] * mixed_rate
        held_ref[g] = normal
        mixed = (normal * mixed_gain_ref[g]).astype(bf16)
        mixed_ref[:, g * piece : (g + 1) * piece] = mixed
        middle = middle + dot(mixed, merge_ref[g * piece : (g + 1) * piece, :])
    middle_ref[...] = middle
    second_normal, _ = normalized(middle)
    second = (second_normal * second_gain_ref[...]).astype(bf16)
    second_ref[...] = second
    total = jnp.zeros((tokens, 1), f32)
    for step in range(steps):
        copy(step).wait()
        at = slice(step * WIDE, (step + 1) * WIDE)
        value = dot(second, expand_ref[:, at])
        share = 0.5 * (1.0 + lax.erf(value * 0.7071067811865476))
        gelu = value * share
        gelu_ref[:, at] = gelu
        slope = share + value * (0.3989422804014327 * jnp.exp(-0.5 * value * value))
        slope_ref[:, at] = slope.astype(bf16)
        total = total + jnp.sum(gelu, axis=-1, keepdims=True)
    mean = total * (1.0 / spread)
    total = jnp.zeros((tokens, 1), f32)
    for step in range(steps):
        centred = gelu_ref[:, step * WIDE : (step + 1) * WIDE] - mean
        total = total + jnp.sum(centred * centred, axis=-1, keepdims=True)
    rate = lax.rsqrt(total * (1.0 / spread) + norm_epsilon)
    hidden_rate_ref[...] = rate
    core = slot % 2
    for at in range(0, spread, 2 * BAND):
        ours, theirs = [], []
        for start in range(at, at + 2 * BAND, 2 * block):
            low = slice(start, start + block)
            high = slice(start + block, start + 2 * block)
            parts = []
            for part in (low, high):
                normal = (gelu_ref[:, part] - mean) * rate
                normal_ref[:, part] = normal.astype(bf16)
                parts.append((normal * hidden_gain_ref[:, part]).astype(bf16))
            ours.append(parts[0])
            theirs.append(parts[1])
        even, odd = jnp.concatenate(ours, axis=1), jnp.concatenate(theirs, axis=1)
        half_at = slice(at // 2, at // 2 + BAND)
        hidden_ref[:, half_at] = jnp.where(core == 0, even, odd)
        hidden_give_ref[:, half_at] = jnp.where(core == 0, odd, even)


def widen_call(
    place, pieces, inputs, mixed_gain, second_gain, hidden_gain, merge, expand
):
    slots = len(pieces)
    tokens = len(inputs) * inputs[0].shape[0]
    piece = pieces[0].shape[1] // 2
    width, spread = expand.shape
    groups = width // piece

    def low(*shape):
        return jax.ShapeDtypeStruct(shape, bf16)

    def full(*shape):
        return jax.ShapeDtypeStruct(shape, f32)

    return pl.pallas_call(
        functools.partial(
            widen_kernel, slots=slots, planes=len(inputs), groups=groups, width=width,
            spread=spread, block=spread // (slots * len(inputs)),
        ),
        out_shape=(
            low(tokens, width),
            full(tokens, width),
            low(tokens, width),
            low(tokens, spread // 2),
            low(tokens, spread // 2),
            low(tokens, spread),
            low(tokens, spread),
            full(slots, tokens, piece),
            full(tokens, 1),
            full(tokens, 1),
        ),
        in_specs=[pl.BlockSpec(memory_space=pltpu.SMEM)]
        + [vmem_spec()] * (4 + slots + len(inputs))
        + [hbm_spec()],
        out_specs=(vmem_spec(),) * 10,
        scratch_shapes=[
            pltpu.VMEM((width, spread), bf16),
            pltpu.VMEM((tokens, spread), f32),
            pltpu.SemaphoreType.DMA((spread // WIDE,)),
        ],
        compiler_params=params(WIDEN_MIB),
        cost_estimate=cost(6 << 30, 6 << 20),
        name="widen",
    )(
        place, *pieces, *inputs, mixed_gain, second_gain, hidden_gain, merge, expand,
    )


def branch_kernel(place_ref, lengths_ref, *refs, slots):
    blocks, branch_ref = refs[:-1], refs[-1]
    seg = blocks[0].shape[0]
    limit = document_ends(lengths_ref, place_ref[0])[-1]
    for k, block in enumerate(blocks):
        offset = ((place_ref[0] ^ k) * slots + place_ref[1]) * seg
        valid = offset + lax.broadcasted_iota(jnp.int32, (seg, 1), 0) < limit
        branch_ref[k * seg : (k + 1) * seg, :] = jnp.where(
            valid, block[...], jnp.zeros((), bf16)
        )


def branch_call(place, lengths, blocks, slots):
    seg, width = blocks[0].shape
    return pl.pallas_call(
        functools.partial(branch_kernel, slots=slots),
        out_shape=jax.ShapeDtypeStruct((len(blocks) * seg, width), bf16),
        in_specs=[pl.BlockSpec(memory_space=pltpu.SMEM)] * 2 + [vmem_spec()] * len(blocks),
        out_specs=vmem_spec(),
        compiler_params=params(4),
        name="branch",
    )(place, lengths, *blocks)


def turn_kernel(*refs, slots, planes, groups, width, spread):
    (
        place_ref, branch_ref, normal_ref, slope_ref, middle_ref, held_ref,
        mixed_rate_ref, hidden_rate_ref,
        mixed_gain_ref, second_gain_ref, hidden_gain_ref, merge_ref, shrink_from, expand_from,
    ) = refs[:14]
    expanded_ref, mix_ref, grad_ref, parts_ref = refs[14:18]
    away = refs[18 : 18 + slots]
    results = refs[18 + slots : 18 + slots + planes]
    shrink_ref, expand_ref, weighted_ref, sent_ref, ready = refs[18 + slots + planes :]
    steps = spread // WIDE

    def copy_shrink(step):
        at = pl.ds(step * WIDE, WIDE)
        return pltpu.make_async_copy(shrink_from.at[at], shrink_ref.at[at], ready.at[step])

    def copy_expand(step):
        at = pl.ds(step * WIDE, WIDE)
        return pltpu.make_async_copy(
            expand_from.at[:, at], expand_ref.at[:, at], ready.at[steps + step]
        )

    for step in range(steps):
        copy_shrink(step).start()
    for step in range(steps):
        copy_expand(step).start()
    slot = place_ref[1]
    piece = width // groups
    tokens = middle_ref.shape[0]
    half = tokens // 2
    branch = branch_ref[...]
    result = middle_ref[...]
    weighted_sum = jnp.zeros((tokens, 1), f32)
    inner_sum = jnp.zeros((tokens, 1), f32)
    for step in range(steps):
        copy_shrink(step).wait()
        at = slice(step * WIDE, (step + 1) * WIDE)
        normal = normal_ref[:, at].astype(f32)
        hidden = (normal * hidden_gain_ref[:, at]).astype(bf16)
        result = result + dot(hidden, shrink_ref[at, :])
        grad_hidden = dot_nt(branch, shrink_ref[at, :])
        start = 2 * width + step * WIDE
        parts_ref[:, start : start + WIDE] = jnp.sum(grad_hidden * normal, axis=0, keepdims=True)
        weighted = grad_hidden * hidden_gain_ref[:, at]
        weighted_ref[:, at] = weighted
        weighted_sum = weighted_sum + jnp.sum(weighted, axis=-1, keepdims=True)
        inner_sum = inner_sum + jnp.sum(weighted * normal, axis=-1, keepdims=True)
    seg = tokens // planes
    for k in range(planes):
        results[k][...] = result[k * seg : (k + 1) * seg, :].astype(bf16)
    weighted_mean = weighted_sum * (1.0 / spread)
    inner_mean = inner_sum * (1.0 / spread)
    rate = hidden_rate_ref[...]
    grad_second = jnp.zeros((tokens, width), f32)
    for step in range(steps):
        copy_expand(step).wait()
        at = slice(step * WIDE, (step + 1) * WIDE)
        grad = rate * (
            weighted_ref[:, at] - weighted_mean - normal_ref[:, at].astype(f32) * inner_mean
        )
        expanded = (grad * slope_ref[:, at].astype(f32)).astype(bf16)
        expanded_ref[:, at] = expanded
        grad_second = grad_second + dot_nt(expanded, expand_ref[:, at])
    second_normal, second_rate = normalized(middle_ref[...])
    parts_ref[:, width : 2 * width] = jnp.sum(grad_second * second_normal, axis=0, keepdims=True)
    grad_middle = branch.astype(f32) + norm_back(
        second_normal, second_rate, grad_second * second_gain_ref[...]
    )
    grad_ref[...] = grad_middle
    mix = grad_middle.astype(bf16)
    mix_ref[...] = mix
    grads = []
    weighted_sum = 0.0
    inner_sum = 0.0
    for g in range(groups):
        grad_mixed = dot_nt(mix, merge_ref[g * piece : (g + 1) * piece, :])
        parts_ref[:, g * piece : (g + 1) * piece] = jnp.sum(
            grad_mixed * held_ref[g], axis=0, keepdims=True
        )
        weighted = grad_mixed * mixed_gain_ref[g]
        grads.append(weighted)
        weighted_sum = weighted_sum + jnp.sum(weighted, axis=-1, keepdims=True)
        inner_sum = inner_sum + jnp.sum(weighted * held_ref[g], axis=-1, keepdims=True)
    weighted_mean = weighted_sum * (1.0 / width)
    inner_mean = inner_sum * (1.0 / width)
    for g in range(slots):
        if g < groups:
            sent_ref[g] = mixed_rate_ref[...] * (
                grads[g] - weighted_mean - held_ref[g] * inner_mean
            )
        else:
            sent_ref[g] = jnp.zeros(sent_ref.shape[1:], f32)
    for u in range(slots):
        for side in range(2):
            away[u][:, side * piece : (side + 1) * piece] = sent_ref[
                slot ^ u, side * half : (side + 1) * half, :
            ].astype(bf16)


def turn_call(
    place, branch, normal, slope, middle, held, mixed_rate, hidden_rate,
    mixed_gain, second_gain, hidden_gain, merge, shrink, expand, planes,
):
    slots, tokens, piece = held.shape
    width, spread = expand.shape
    groups = width // piece

    def low(*shape):
        return jax.ShapeDtypeStruct(shape, bf16)

    def full(*shape):
        return jax.ShapeDtypeStruct(shape, f32)

    outs = pl.pallas_call(
        functools.partial(
            turn_kernel, slots=slots, planes=planes, groups=groups, width=width, spread=spread
        ),
        out_shape=(
            low(tokens, spread),
            low(tokens, width),
            full(tokens, width),
            full(1, 2 * width + spread),
        )
        + (low(tokens // 2, 2 * piece),) * slots
        + (low(tokens // planes, width),) * planes,
        in_specs=[pl.BlockSpec(memory_space=pltpu.SMEM)] + [vmem_spec()] * 11 + [hbm_spec()] * 2,
        out_specs=(vmem_spec(),) * (4 + slots + planes),
        scratch_shapes=[
            pltpu.VMEM((spread, width), bf16),
            pltpu.VMEM((width, spread), bf16),
            pltpu.VMEM((tokens, spread), f32),
            pltpu.VMEM((slots, tokens, piece), f32),
            pltpu.SemaphoreType.DMA((2 * spread // WIDE,)),
        ],
        compiler_params=params(TURN_MIB),
        cost_estimate=cost(9 << 30, 8 << 20),
        name="turn",
    )(
        place, branch, normal, slope, middle, held, mixed_rate, hidden_rate,
        mixed_gain, second_gain, hidden_gain, merge, shrink, expand,
    )
    return outs[:4], outs[4 : 4 + slots], outs[4 + slots :]


def cut_out(outs, total_ref, place_ref, bands, steps, rows_each, axis, cut):
    whole_ref, firsts = outs[0], outs[1:]
    far_rank, side = place_ref[2] // 2, place_ref[3]
    for at, code in codes(steps):
        other, far = code & 1, code >> 1
        offset = pl.multiple_of((far_rank ^ far) * rows_each, rows_each)
        parts = []
        for first, wide in bands:
            column = pl.multiple_of(first + (side ^ other) * wide, 128)
            parts.append(
                total_ref[pl.ds(offset, rows_each), pl.ds(column, wide)].astype(bf16)
            )
        value = parts[0] if len(parts) == 1 else jnp.concatenate(parts, axis=1)
        whole_ref[at] = value
        for chain, first_ref in enumerate(firsts):
            if at[chain] == 1:
                band = slice(0, cut) if chain == 0 else slice(cut, None)
                first_ref[at[:chain] + at[chain + 1 :]] = (
                    value[band] if axis == 0 else value[:, band]
                )


def shrink_kernel(
    place_ref, hidden_ref, branch_ref, hidden_got_ref, branch_got_ref, *refs, cutting
):
    total_ref = refs[-1]
    spread, _ = total_ref.shape
    branch = jnp.concatenate([branch_ref[...], branch_got_ref[...]], axis=0)
    for at in range(0, spread, WIDE):
        hidden = jnp.concatenate(
            [hidden_ref[:, at : at + WIDE], hidden_got_ref[:, at : at + WIDE]], axis=0
        )
        total_ref[at : at + WIDE, :] = dot_tn(hidden, branch)
    cut_out(refs[:-1], total_ref, place_ref, **cutting)


def expand_kernel(
    place_ref, second_ref, mixed_ref, second_got_ref, mixed_got_ref,
    expanded_ref, mix_ref, expanded_got_ref, mix_got_ref, *refs, cutting,
):
    turned_ref, total_ref = refs[-2:]
    tokens, spread = expanded_ref.shape
    width = second_ref.shape[1]
    core = place_ref[2] % 2
    rows_each = cutting["rows_each"]

    def left(own_ref, got_ref):
        turned_ref[:, :tokens] = own_ref[...].astype(f32).T
        turned_ref[:, tokens:] = got_ref[...].astype(f32).T
        rows = [
            turned_ref[pl.ds(pl.multiple_of((2 * i + core) * rows_each, rows_each), rows_each), :]
            for i in range(width // (2 * rows_each))
        ]
        return jnp.concatenate(rows, axis=0).astype(bf16)

    second = left(second_ref, second_got_ref)
    for at in range(0, spread, WIDE):
        band = slice(at, at + WIDE)
        total_ref[:, band] = dot(
            second, jnp.concatenate([expanded_ref[:, band], expanded_got_ref[:, band]], axis=0)
        )
    mixed = left(mixed_ref, mixed_got_ref)
    total_ref[:, spread:] = dot(
        mixed, jnp.concatenate([mix_ref[...], mix_got_ref[...]], axis=0)
    )
    cut_out(refs[:-2], total_ref, place_ref, **cutting)


def outer_call(kernel, place, operands, rows, columns, bands, steps, size, axis, cut, scratch, name):
    rows_each = rows // size
    shape = (rows_each, columns // 2)
    low = (cut, shape[1]) if axis == 0 else (shape[0], cut)
    high = (shape[0] - cut, shape[1]) if axis == 0 else (shape[0], shape[1] - cut)
    pairs = (2,) * (len(steps) - 1)
    return pl.pallas_call(
        functools.partial(
            kernel,
            cutting=dict(bands=bands, steps=steps, rows_each=rows_each, axis=axis, cut=cut),
        ),
        out_shape=(
            jax.ShapeDtypeStruct((2,) + pairs + shape, bf16),
            jax.ShapeDtypeStruct(pairs + low, bf16),
            jax.ShapeDtypeStruct(pairs + high, bf16),
        ),
        in_specs=[pl.BlockSpec(memory_space=pltpu.SMEM)] + [vmem_spec()] * len(operands),
        out_specs=(vmem_spec(),) * 3,
        scratch_shapes=scratch + [pltpu.VMEM((rows // 2, columns), f32)],
        compiler_params=params(OUTER_MIB),
        cost_estimate=cost(2 << 30, 10 << 20),
        name=name,
    )(place, *operands)


def settle_kernel(place_ref, *refs):
    out = refs[-1]
    for k, ref in enumerate(refs[:-1]):
        out[place_ref[0] ^ k] = ref[...]


def settle_call(place, blocks):
    return pl.pallas_call(
        settle_kernel,
        out_shape=jax.ShapeDtypeStruct((len(blocks),) + blocks[0].shape, blocks[0].dtype),
        in_specs=[pl.BlockSpec(memory_space=pltpu.SMEM)] + [vmem_spec()] * len(blocks),
        out_specs=vmem_spec(),
        compiler_params=params(8),
        name="settle",
    )(place, *blocks)


def heads_kernel(place_ref, *refs, groups, gains):
    joined_out, gains_out, held_ref = refs[-3:]
    pieces = refs[:-3]
    sums = []
    for u, ref in enumerate(pieces):
        held_ref[place_ref[1] ^ u] = ref[0].astype(f32)
        sums.append(ref[1].astype(f32))
    piece = pieces[0].shape[2] // 3
    for part in range(3):
        for g in range(groups):
            start = (part * groups + g) * piece
            joined_out[:, start : start + piece] = held_ref[
                g, :, part * piece : (part + 1) * piece
            ]
    while len(sums) > 1:
        sums = [sums[i] + sums[i + 1] for i in range(0, len(sums), 2)]
    wide = 3 * piece
    for r in range(-(-gains // wide)):
        end = min((r + 1) * wide, gains)
        gains_out[:, r * wide : end] = sums[0][r : r + 1, : end - r * wide]


def heads_call(place, blocks, width, gains):
    _, rows, wide = blocks[0].shape
    return pl.pallas_call(
        functools.partial(heads_kernel, groups=3 * width // wide, gains=gains),
        out_shape=(
            jax.ShapeDtypeStruct((rows, 3 * width), f32),
            jax.ShapeDtypeStruct((1, gains), f32),
        ),
        in_specs=[pl.BlockSpec(memory_space=pltpu.SMEM)] + [vmem_spec()] * len(blocks),
        out_specs=(vmem_spec(),) * 2,
        scratch_shapes=[pltpu.VMEM((len(blocks), rows, wide), f32)],
        compiler_params=params(8),
        name="heads_side_by_side",
    )(place, *blocks)


def input_kernel(*refs, planes, parts):
    inputs = refs[:planes]
    refs = refs[planes:]
    grad_ref, gain_ref = refs[:2]
    grad = sum(ref[at].astype(f32) for ref, at in zip(refs[2 : 2 + len(parts)], parts))
    outs = refs[2 + len(parts) :]
    normal, rate = normalized(
        jnp.concatenate([block[...] for block in inputs], axis=0).astype(f32)
    )
    value = grad_ref[...] + norm_back(normal, rate, grad * gain_ref[...])
    seg = value.shape[0] // planes
    for k in range(planes):
        outs[k][...] = value[k * seg : (k + 1) * seg, :].astype(bf16)


def input_call(inputs, grad_middle, gain, held, parts):
    planes = len(inputs)
    tokens, width = grad_middle.shape
    return pl.pallas_call(
        functools.partial(input_kernel, planes=planes, parts=parts),
        out_shape=(jax.ShapeDtypeStruct((tokens // planes, width), bf16),) * planes,
        in_specs=[vmem_spec()] * (2 + planes + len(held)),
        out_specs=(vmem_spec(),) * planes,
        compiler_params=params(16),
        name="input_back",
    )(*inputs, grad_middle, gain, *held)


def swap(value, axis, bits):
    size = lax.axis_size(axis)
    return lax.ppermute(value, axis, [(i, i ^ bits) for i in range(size)])


def pick(value, index, axis=0):
    return lax.dynamic_index_in_dim(value, index, axis, keepdims=False)


def in_hbm(*values):
    return [pltpu.with_memory_space_constraint(value, pltpu.HBM) for value in values]


def bits_of(size):
    return size.bit_length() - 1


def total(values):
    return sum(v.astype(f32) for v in values)


def sums_kernel(*refs, listed):
    outs = refs[-len(listed) :]
    for out, terms in zip(outs, listed):
        out[...] = sum(refs[i][at].astype(f32) for i, at in terms).astype(bf16)


def sums_call(sums, name):
    arrays, listed, shapes = [], [], []
    for terms in sums:
        entry = []
        for array, at in terms:
            where = [i for i, held in enumerate(arrays) if held is array]
            if not where:
                arrays.append(array)
                where = [len(arrays) - 1]
            entry.append((where[0], at))
        listed.append(entry)
        shapes.append(jax.eval_shape(lambda v, at=terms[0][1]: v[at], terms[0][0]).shape)
    return pl.pallas_call(
        functools.partial(sums_kernel, listed=listed),
        out_shape=tuple(jax.ShapeDtypeStruct(shape, bf16) for shape in shapes),
        in_specs=[vmem_spec()] * len(arrays),
        out_specs=(vmem_spec(),) * len(shapes),
        compiler_params=params(4),
        name=name,
    )(*arrays)


class Halves:
    def __init__(self, bands):
        self.entries = []
        self.bands = bands
        self.chosen = {}

    def hold(self, array, names):
        self.entries.append((array, names))

    def terms(self, choice=()):
        chosen = dict(self.chosen)
        chosen.update(choice)
        listed = []
        for array, names in self.entries:
            at = tuple(
                chosen[n] if n in chosen
                else self.bands.get(n, slice(None)) if len(names) == len(self.entries[0][1])
                else slice(None)
                for n in names
            )
            listed.append((array, at))
        return listed

    def summed(self, choice=()):
        return sum(array[at].astype(f32) for array, at in self.terms(choice))

    def send(self, name):
        return self.summed({name: 1}).astype(bf16)

    def receive(self, name, array):
        self.chosen[name] = 0
        self.hold(array, [n for n in self.entries[0][1] if n not in self.chosen])


def per_device(
    layer_input, cotangent, doc_lengths, joined_weight, merge_weight, expand_weight,
    shrink_weight, first_gain, mixed_gain, second_gain, hidden_gain,
):
    _, planes, seg, width = layer_input.shape
    size = lax.axis_size("blk")
    slots = size // planes
    batches = lax.axis_size("batch")
    rank = lax.axis_index("blk")
    group_rank = lax.axis_index("batch")
    plane = rank // slots
    slot = rank % slots
    head_count = width // HEAD
    heads = -(-head_count // slots)
    groups = head_count // heads
    piece = heads * HEAD
    tokens = planes * seg
    length = slots * tokens
    side = group_rank % 2
    place = jnp.stack([plane, slot, rank, side]).astype(jnp.int32)

    def to_planes(blocks):
        return [pick(blocks, plane)] + [
            swap(pick(blocks, plane ^ k), "blk", k * slots) for k in range(1, planes)
        ]

    def all_slots(value):
        held = {0: value}
        for bit in reversed(range(bits_of(slots))):
            held.update({u | 1 << bit: swap(v, "blk", 1 << bit) for u, v in held.items()})
        return [held[u] for u in range(slots)]

    def over_slots(blocks):
        return [blocks[0]] + [swap(blocks[u], "blk", u) for u in range(1, slots)]

    spread = expand_weight.shape[1]
    expand_weight, shrink_weight = in_hbm(expand_weight, shrink_weight)
    first_arrived = to_planes(layer_input[0])
    own_start = jnp.minimum(slot, groups - 1) * piece
    own_weight = jnp.concatenate(
        [
            lax.dynamic_slice_in_dim(joined_weight, part * width + own_start, piece, 1)
            for part in range(3)
        ],
        axis=1,
    )
    lengths = doc_lengths[0]
    gain_row = first_gain.reshape(1, width)
    mixed_gain = mixed_gain.reshape(groups, 1, piece)
    second_gain = second_gain.reshape(1, width)
    hidden_gain = hidden_gain.reshape(1, spread)
    (
        first_arrived[-1], place, lengths, gain_row, mixed_gain, second_gain, hidden_gain, own_weight,
    ) = lax.optimization_barrier(
        (
            first_arrived[-1], place, lengths, gain_row, mixed_gain, second_gain, hidden_gain,
            own_weight,
        )
    )
    pieces = [all_slots(block) for block in first_arrived]
    (first, joined), sent, shares = forward_call(
        place, lengths, gain_row, own_weight, pieces
    )
    sent, cotangent = lax.optimization_barrier((sent, cotangent))
    cotangent_blocks = to_planes(cotangent[0])
    (
        mixed, middle, second, hidden, hidden_give, normal, slope, held, mixed_rate, hidden_rate,
    ) = widen_call(
        place, over_slots(sent), first_arrived, mixed_gain, second_gain, hidden_gain, merge_weight,
        expand_weight,
    )
    hidden_give, cotangent_blocks = lax.optimization_barrier((hidden_give, cotangent_blocks))
    branch = branch_call(place, lengths, cotangent_blocks, slots)

    row_bits = list(range(1, bits_of(slots)))
    plane_bits = list(range(bits_of(slots), bits_of(size)))
    names = ["side"] + row_bits + plane_bits + ["rows", "columns"]
    steps = [0] + row_bits + plane_bits
    orders = (["side"] + row_bits, row_bits + ["side"])
    stages = len(orders[0])

    def cross(name, value):
        return swap(value, "batch", 1) if name == "side" else swap(value, "blk", 1 << name)

    def chains(axis, cut, whole):
        both = []
        for band in (slice(0, cut), slice(cut, None)):
            chain = Halves({axis: band})
            chain.hold(whole, names)
            both.append(chain)
        return both

    def sends(pair, at):
        return [chain.send(order[at]) for chain, order in zip(pair, orders)]

    def sends_in_kernel(pair, at):
        return sums_call(
            [chain.terms({order[at]: 1}) for chain, order in zip(pair, orders)], "next_halves"
        )

    def crossed(at, values):
        return [cross(order[at], value) for order, value in zip(orders, values)]

    def arrive(pair, at, values):
        for chain, order, value in zip(pair, orders, values):
            chain.receive(order[at], value)

    def plane_depart(pair, bit, axis):
        return cross(bit, jnp.concatenate([chain.send(bit) for chain in pair], axis=axis))

    def plane_arrive(pair, bit, axis, both):
        if axis == -2:
            cut = pair[0].bands["rows"].stop
            values = both[..., :cut, :], both[..., cut:, :]
        else:
            cut = pair[0].bands["columns"].stop
            values = both[..., :cut], both[..., cut:]
        for chain, value in zip(pair, values):
            chain.receive(bit, value)

    def closed(pair, axis):
        value = jnp.concatenate([chain.summed() for chain in pair], axis=axis).astype(bf16)
        for bit in range(1, bits_of(batches)):
            value = total([value, swap(value, "batch", 1 << bit)]).astype(bf16)
        return value

    def both_sides(value):
        other = swap(value, "batch", 1)
        return jnp.where(side == 0, value, other), jnp.where(side == 0, other, value)

    cut = spread // size // 2
    shrink_whole, *shrink_firsts = outer_call(
        shrink_kernel, place,
        [hidden, branch, swap(hidden_give, "blk", 1), swap(branch, "blk", 1)],
        spread, width, ((0, width // 2),), steps, size, 0, cut, [], "shrink_outer",
    )
    shrink_sent = crossed(0, shrink_firsts)
    second_got, mixed_got = swap(second, "blk", 1), swap(mixed, "blk", 1)
    (expanded, mix, grad_middle, parts), away, results = turn_call(
        place, branch, normal, slope, middle, held, mixed_rate, hidden_rate,
        mixed_gain, second_gain, hidden_gain, merge_weight, shrink_weight, expand_weight, planes,
    )
    shrink_sent, second_got, mixed_got, expanded, mix = lax.optimization_barrier(
        (shrink_sent, second_got, mixed_got, expanded, mix)
    )
    shrink_chains = chains("rows", cut, shrink_whole)
    arrive(shrink_chains, 0, shrink_sent)

    returned = over_slots(away)
    expanded_got, mix_got = swap(expanded, "blk", 1), swap(mix, "blk", 1)
    returned, expanded_got, mix_got = lax.optimization_barrier((returned, expanded_got, mix_got))
    cut = ((spread + width) // 4 + 127) // 128 * 128
    expand_whole, *expand_firsts = outer_call(
        expand_kernel, place,
        [second, mixed, second_got, mixed_got, expanded, mix, expanded_got, mix_got],
        width, spread + width, ((0, spread // 2), (spread, width // 2)), steps, size, 1, cut,
        [pltpu.VMEM((width, 2 * tokens), f32)], "expand_outer",
    )
    for at in range(1, stages):
        shrink_sent = crossed(at, sends_in_kernel(shrink_chains, at))
        if at < stages - 1:
            arrive(shrink_chains, at, shrink_sent)
    expand_firsts, results = lax.optimization_barrier((expand_firsts, results))
    result_blocks = [results[0]] + [
        swap(results[k], "blk", k * slots) for k in range(1, planes)
    ]
    returned, expand_firsts, shrink_sent = lax.optimization_barrier(
        (returned, expand_firsts, shrink_sent)
    )
    arrive(shrink_chains, stages - 1, shrink_sent)
    expand_sent = crossed(0, expand_firsts)
    shrink_both = [
        cross(plane_bits[0], value)
        for value in sums_call(
            [chain.terms({plane_bits[0]: 1}) for chain in shrink_chains], "plane_halves"
        )
    ]
    joined_part, branch_keep, branch_give = backward_call(
        place, first, joined, own_weight, gain_row, parts,
        returned, shares, planes,
    )
    (
        joined_part, branch_give, shrink_both, expand_sent, result_blocks,
    ) = lax.optimization_barrier(
        (joined_part, branch_give, shrink_both, expand_sent, result_blocks)
    )
    for chain, value in zip(shrink_chains, shrink_both):
        chain.receive(plane_bits[0], value)
    expand_chains = chains("columns", cut, expand_whole)
    arrive(expand_chains, 0, expand_sent)

    blocks = planes * slots
    gains, joined_sum = joined_part[blocks].astype(f32), [joined_part[:blocks]]

    def joined_depart(bit):
        half = joined_sum[0].shape[0] // 2
        give = sum(v[half:].astype(f32) for v in joined_sum).astype(bf16)
        return swap(jnp.concatenate([give, gains.astype(bf16)[None]]), "blk", 1 << bit)

    def joined_arrive(got):
        half = got.shape[0] - 1
        return (
            [v[:half] for v in joined_sum] + [got[:half]],
            gains.astype(bf16).astype(f32) + got[half].astype(f32),
        )

    joined_got = joined_depart(plane_bits[0])
    branch_got = swap(branch_give, "blk", 1)
    for at in range(1, stages):
        expand_sent = crossed(at, sends(expand_chains, at))
        if at < stages - 1:
            arrive(expand_chains, at, expand_sent)
    for bit in plane_bits[1:]:
        shrink_both = plane_depart(shrink_chains, bit, -2)
        if bit != plane_bits[-1]:
            plane_arrive(shrink_chains, bit, -2, shrink_both)
    joined_got, branch_got, expand_sent, shrink_both = lax.optimization_barrier(
        (joined_got, branch_got, expand_sent, shrink_both)
    )
    joined_sum, gains = joined_arrive(joined_got)
    arrive(expand_chains, stages - 1, expand_sent)
    plane_arrive(shrink_chains, plane_bits[-1], -2, shrink_both)

    branch_held, prefixes = [branch_keep, branch_got], [(), ()]
    for bit in row_bits:
        give = sum(v[p + (1,)].astype(f32) for v, p in zip(branch_held, prefixes)).astype(bf16)
        prefixes = [p + (0,) for p in prefixes] + [()]
        branch_held.append(swap(give, "blk", 1 << bit))
    expand_both = plane_depart(expand_chains, plane_bits[0], -1)
    for bit in plane_bits[1:]:
        joined_got = joined_depart(bit)
        if bit != plane_bits[-1]:
            joined_sum, gains = joined_arrive(joined_got)
    joined_sum, gains = joined_arrive(joined_got)
    plane_arrive(expand_chains, plane_bits[0], -1, expand_both)

    input_blocks = input_call(
        first_arrived, grad_middle, gain_row, branch_held, prefixes
    )
    input_blocks = [input_blocks[0]] + [
        swap(input_blocks[k], "blk", k * slots) for k in range(1, planes)
    ]
    joined_last = jnp.concatenate(
        [sum(v.astype(f32) for v in joined_sum), gains[None]]
    ).astype(bf16)
    for bit in range(bits_of(batches)):
        joined_last = total([joined_last, swap(joined_last, "batch", 1 << bit)]).astype(bf16)
    for bit in plane_bits[1:]:
        expand_both = plane_depart(expand_chains, bit, -1)
        if bit != plane_bits[-1]:
            plane_arrive(expand_chains, bit, -1, expand_both)
    plane_arrive(expand_chains, plane_bits[-1], -1, expand_both)

    joined_grad, gain_grads = heads_call(
        place,
        [jnp.stack([joined_last[0], joined_last[slots]])]
        + [
            swap(jnp.stack([joined_last[u], joined_last[slots]]), "blk", u)
            for u in range(1, slots)
        ],
        width, 3 * width + spread,
    )
    shrink_lower, shrink_upper = both_sides(closed(shrink_chains, -2))
    shrink_grad = jnp.concatenate([shrink_lower, shrink_upper], axis=1).astype(f32)
    expand_lower, expand_upper = both_sides(closed(expand_chains, -1))
    cut = spread // 2
    expand_grad = jnp.concatenate([expand_lower[:, :cut], expand_upper[:, :cut]], axis=1)
    merge_grad = jnp.concatenate([expand_lower[:, cut:], expand_upper[:, cut:]], axis=1)
    layer_result = settle_call(place, result_blocks).reshape(layer_input.shape)
    input_grad = settle_call(place, input_blocks).reshape(layer_input.shape)
    gain_grads = gain_grads[0]
    return (
        layer_result, input_grad, joined_grad, merge_grad.astype(f32), expand_grad.astype(f32),
        shrink_grad, gain_grads[:width], gain_grads[width : 2 * width],
        gain_grads[2 * width : 3 * width], gain_grads[3 * width :],
    )


def solution(mesh):
    rows = P("batch", None, "blk", None)
    return jax.shard_map(
        per_device,
        mesh=mesh,
        in_specs=(rows, rows, P("batch", None, None)) + (P(),) * 8,
        out_specs=(rows, rows) + (P("blk", None),) * 4 + (P(),) * 4,
        check_vma=False,
    )
```

```python
import functools

import jax
import jax.numpy as jnp
from jax import lax
from jax.experimental import pallas as pl
from jax.experimental.pallas import tpu as pltpu
from jax.sharding import PartitionSpec as P

HEAD = 64
TILE = 256
WIDE = 512
BAND = 384
FORWARD_MIB = 14
BACKWARD_MIB = 14
WIDEN_MIB = 11
TURN_MIB = 11
OUTER_MIB = 16
big_negative = -1e30
norm_epsilon = 1e-05

f32 = jnp.float32
bf16 = jnp.bfloat16


def dot(left, right):
    return jnp.dot(left, right, preferred_element_type=f32)


def dot_nt(left, right):
    return lax.dot_general(left, right, (((1,), (1,)), ((), ())), preferred_element_type=f32)


def dot_tn(left, right):
    return lax.dot_general(left, right, (((0,), (0,)), ((), ())), preferred_element_type=f32)


def normalized(values):
    centred = values - jnp.mean(values, axis=-1, keepdims=True)
    rate = lax.rsqrt(jnp.mean(centred * centred, axis=-1, keepdims=True) + norm_epsilon)
    return centred * rate, rate


def norm_back(normal, rate, weighted):
    return rate * (
        weighted
        - jnp.mean(weighted, axis=-1, keepdims=True)
        - normal * jnp.mean(weighted * normal, axis=-1, keepdims=True)
    )


def vmem_spec():
    return pl.BlockSpec(memory_space=pltpu.VMEM)


def hbm_spec():
    return pl.BlockSpec(memory_space=pltpu.HBM)


def params(mebibytes):
    return pltpu.CompilerParams(vmem_limit_bytes=mebibytes * 1024 * 1024)


def cost(flops, moved):
    return pl.CostEstimate(flops=flops, bytes_accessed=moved, transcendentals=0)


def document_ends(lengths_ref, plane):
    ends, end = [], jnp.int32(0)
    for d in range(lengths_ref.shape[1]):
        end = end + lengths_ref[plane, d]
        ends.append(end)
    return ends


def codes(steps):
    listed = [((), 0)]
    for bit in steps:
        listed = [(at + (b,), code | (b << bit)) for at, code in listed for b in (0, 1)]
    return listed


def forward_kernel(*refs, planes, slots, seg, heads):
    place_ref, lengths_ref, gain_ref, weight_ref = refs[:4]
    pieces = refs[4 : 4 + slots * planes]
    refs = refs[4 + slots * planes :]
    length = planes * slots * seg
    tiles = length // TILE
    first_ref, joined_ref, factor_ref = refs[:3]
    sent = refs[3 : 3 + slots]
    shares = refs[3 + slots : 3 + slots + tiles]
    rows_ref, attention_ref = refs[3 + slots + tiles :]
    plane, slot = place_ref[0], place_ref[1]
    for u in range(slots):
        for k in range(planes):
            offset = ((plane ^ k) * slots + (slot ^ u)) * seg
            rows_ref[pl.ds(pl.multiple_of(offset, seg), seg), :] = pieces[k * slots + u][...]
    width = heads * HEAD

    def project(tile, carry):
        rows = pl.ds(pl.multiple_of(tile * TILE, TILE), TILE)
        normal, _ = normalized(rows_ref[rows, :].astype(f32))
        first = (normal * gain_ref[...]).astype(bf16)
        first_ref[rows, :] = first
        joined = dot(first, weight_ref[...]).astype(bf16)
        for part in range(3):
            for h in range(heads):
                column = part * width + h * HEAD
                value = joined[:, column : column + HEAD]
                if part == 0:
                    value = value * jnp.asarray(0.125, bf16)
                joined_ref[part * heads + h, rows, :] = value
        return carry

    lax.fori_loop(0, tiles, project, 0, unroll=True)
    ends = document_ends(lengths_ref, plane)
    for q in reversed(range(tiles)):
        rows = slice(q * TILE, (q + 1) * TILE)
        reach = (q + 1) * TILE
        places = q * TILE + lax.broadcasted_iota(jnp.int32, (TILE, 1), 0)
        start = jnp.zeros((TILE, 1), jnp.int32)
        for end in ends:
            start = jnp.maximum(start, jnp.where(places >= end, end, 0))
        query_pos = q * TILE + lax.broadcasted_iota(jnp.int32, (TILE, reach), 0)
        key_pos = lax.broadcasted_iota(jnp.int32, (TILE, reach), 1)
        allowed = (key_pos <= query_pos) & (key_pos >= start)
        for h in range(heads):
            scores = dot_nt(joined_ref[h, rows, :], joined_ref[heads + h, :reach, :])
            scores = jnp.where(allowed, scores, big_negative)
            peak = jnp.max(scores, axis=-1, keepdims=True)
            raised = jnp.exp(scores - peak)
            total = jnp.sum(raised, axis=-1, keepdims=True)
            share = raised.astype(bf16)
            shares[q][h] = share
            factor = 1.0 / total
            factor_ref[rows, h : h + 1] = factor
            attention_ref[h, rows, :] = factor * dot(
                share, joined_ref[2 * heads + h, :reach, :]
            )
    half = planes // 2
    for u in range(slots):
        for k in range(planes):
            offset = ((plane ^ k) * slots + (slot ^ u)) * seg
            rows = slice(k % half * seg, (k % half + 1) * seg)
            for h in range(heads):
                part = attention_ref[h, pl.ds(pl.multiple_of(offset, seg), seg), :]
                column = k // half * width + h * HEAD
                sent[u][rows, column : column + HEAD] = part.astype(bf16)


def forward_call(place, lengths, gain, weight, pieces):
    planes, slots = len(pieces), len(pieces[0])
    seg, width = pieces[0][0].shape
    length = planes * slots * seg
    heads = weight.shape[1] // (3 * HEAD)
    kernel = functools.partial(forward_kernel, planes=planes, slots=slots, seg=seg, heads=heads)
    packed = jax.ShapeDtypeStruct((planes * seg // 2, 2 * heads * HEAD), bf16)
    tiled = [(heads, TILE, reach) for reach in range(TILE, length + 1, TILE)]
    outs = pl.pallas_call(
        kernel,
        out_shape=(
            pltpu.VMEM((length, width), bf16),
            pltpu.VMEM((3 * heads, length, HEAD), bf16),
            pltpu.VMEM((length, heads), f32),
        )
        + (packed,) * slots
        + tuple(pltpu.VMEM(shape, bf16) for shape in tiled),
        in_specs=[pl.BlockSpec(memory_space=pltpu.SMEM)] * 2
        + [vmem_spec()] * (2 + slots * planes),
        out_specs=(vmem_spec(),) * (3 + slots + len(tiled)),
        scratch_shapes=[
            pltpu.VMEM((length, width), bf16),
            pltpu.VMEM((heads, length, HEAD), f32),
        ],
        compiler_params=params(FORWARD_MIB * length // 1024),
        cost_estimate=cost(8 << 30, 8 << 20),
        name="attention_forward",
    )(place, lengths, gain, weight, *[block for blocks in pieces for block in blocks])
    return outs[:3], outs[3 : 3 + slots], outs[3 + slots :]


def backward_kernel(*refs, planes, slots, seg, heads, rows_each):
    place_ref, first_ref, joined_ref, factor_ref, weight_ref, gain_ref, parts_ref = refs[:7]
    pieces = refs[7 : 7 + slots]
    length = planes * slots * seg
    tiles = length // TILE
    refs = refs[7 + slots :]
    shares = refs[:tiles]
    joined_keep, joined_give, branch_keep, branch_give = refs[tiles : tiles + 4]
    grad_ref, arrived_ref, key_ref, value_ref, total_ref, outer_ref, row_ref = refs[tiles + 4 :]
    plane, slot = place_ref[0], place_ref[1]
    width = heads * HEAD
    half = planes // 2
    for u in range(slots):
        for k in range(planes):
            offset = ((plane ^ k) * slots + (slot ^ u)) * seg
            column = k // half * width
            arrived_ref[pl.ds(pl.multiple_of(offset, seg), seg), :] = pieces[u][
                k % half * seg : (k % half + 1) * seg, column : column + width
            ]
    for h in range(heads):
        for q in reversed(range(tiles)):
            rows = slice(q * TILE, (q + 1) * TILE)
            reach = (q + 1) * TILE
            factor = factor_ref[rows, h : h + 1]
            grad = (arrived_ref[rows, h * HEAD : (h + 1) * HEAD].astype(f32) * factor).astype(bf16)
            share = shares[q][h]
            product = share.astype(f32) * dot_nt(grad, joined_ref[2 * heads + h, :reach, :])
            inner = jnp.sum(product, axis=-1, keepdims=True)
            grad_scores = (product - share.astype(f32) * (inner * factor)).astype(bf16)
            query_grad = dot(grad_scores, joined_ref[heads + h, :reach, :]) * 0.125
            grad_ref[rows, h * HEAD : (h + 1) * HEAD] = query_grad.astype(bf16)
            key_add = dot_tn(joined_ref[h, rows, :], grad_scores)
            value_add = dot_tn(grad, share)
            if q == tiles - 1:
                key_ref[...] = key_add
                value_ref[...] = value_add
            else:
                key_ref[:, :reach] += key_add
                value_ref[:, :reach] += value_add
        for part, source in ((1, key_ref), (2, value_ref)):
            column = part * width + h * HEAD
            for q in range(tiles):
                rows = slice(q * TILE, (q + 1) * TILE)
                grad_ref[rows, column : column + HEAD] = source[:, rows].T.astype(bf16)

    def back(tile, carry):
        rows = pl.ds(pl.multiple_of(tile * TILE, TILE), TILE)
        total_ref[rows, :] = dot_nt(grad_ref[rows, :], weight_ref[...])
        return carry

    lax.fori_loop(0, tiles, back, 0, unroll=True)
    for at, code in codes(range(1, bits_of(slots))):
        for out, u in ((branch_keep, code), (branch_give, code | 1)):
            for k in range(planes):
                offset = ((plane ^ k) * slots + (slot ^ u)) * seg
                out[at + (slice(k * seg, (k + 1) * seg),)] = total_ref[
                    pl.ds(pl.multiple_of(offset, seg), seg), :
                ].astype(bf16)
    model = first_ref.shape[1]
    for d in range(0, model, TILE):
        outer = dot_tn(first_ref[:, d : d + TILE], grad_ref[...])
        outer_ref[d : d + TILE, :] = outer
        scaled = jnp.sum(outer * weight_ref[d : d + TILE, :].astype(f32), axis=-1, keepdims=True)
        scaled = jnp.broadcast_to(scaled, (TILE, 128)).T
        row_ref[:, d : d + TILE] = scaled[:1] / gain_ref[:, d : d + TILE]
    wide = 3 * width
    row_ref[:, model : model + parts_ref.shape[1]] = parts_ref[...]
    gains = model + parts_ref.shape[1]
    half = planes * slots // 2
    at = 0
    for _, code in codes(range(bits_of(planes))):
        for u in range(slots):
            offset = ((plane ^ code) * slots + (slot ^ u)) * rows_each
            out = joined_keep if at < half else joined_give
            out[at % half] = outer_ref[
                pl.ds(pl.multiple_of(offset, rows_each), rows_each), :
            ].astype(bf16)
            at += 1
    joined_give[half] = jnp.zeros((rows_each, wide), bf16)
    for r in range(-(-gains // wide)):
        end = min((r + 1) * wide, gains)
        joined_give[half, r : r + 1, : end - r * wide] = row_ref[:, r * wide : end].astype(bf16)


def backward_call(
    place, first, joined, factor, weight, gain, parts, pieces, shares, planes
):
    slots = len(pieces)
    tokens = pieces[0].shape[0] * 2
    heads, length = joined.shape[0] // 3, joined.shape[1]
    width = weight.shape[0]
    rows_each = width // (planes * slots)
    kernel = functools.partial(
        backward_kernel, planes=planes, slots=slots, seg=tokens // planes, heads=heads,
        rows_each=rows_each,
    )
    pairs = (2,) * (bits_of(slots) - 1)
    wide = 3 * heads * HEAD
    row = -(-(width + parts.shape[1]) // 128) * 128
    return pl.pallas_call(
        kernel,
        out_shape=(
            jax.ShapeDtypeStruct((planes * slots // 2, rows_each, wide), bf16),
            jax.ShapeDtypeStruct((planes * slots // 2 + 1, rows_each, wide), bf16),
            jax.ShapeDtypeStruct(pairs + (tokens, width), bf16),
            jax.ShapeDtypeStruct(pairs + (tokens, width), bf16),
        ),
        in_specs=[pl.BlockSpec(memory_space=pltpu.SMEM)]
        + [vmem_spec()] * (6 + slots + len(shares)),
        out_specs=(vmem_spec(),) * 4,
        scratch_shapes=[
            pltpu.VMEM((length, wide), bf16),
            pltpu.VMEM((length, heads * HEAD), bf16),
            pltpu.VMEM((HEAD, length), f32),
            pltpu.VMEM((HEAD, length), f32),
            pltpu.VMEM((length, width), f32),
            pltpu.VMEM((width, wide), f32),
            pltpu.VMEM((1, row), f32),
        ],
        compiler_params=params(BACKWARD_MIB * length // 1024),
        cost_estimate=cost(10 << 30, 10 << 20),
        name="attention_backward",
    )(place, first, joined, factor, weight, gain, parts, *pieces, *shares)


def widen_kernel(*refs, slots, planes, groups, width, spread, block):
    place_ref = refs[0]
    pieces = refs[1 : 1 + slots]
    inputs = refs[1 + slots : 1 + slots + planes]
    refs = refs[1 + slots + planes :]
    mixed_gain_ref, second_gain_ref, hidden_gain_ref, merge_ref, expand_ref = refs[:5]
    (
        mixed_ref, middle_ref, second_ref, hidden_ref, hidden_give_ref, normal_ref, slope_ref,
        held_ref, mixed_rate_ref, hidden_rate_ref,
    ) = refs[5:15]
    (gelu_ref,) = refs[15:]
    steps = spread // WIDE

    slot = place_ref[1]
    piece = width // groups
    tokens = planes * inputs[0].shape[0]
    half = tokens // 2
    for u in range(slots):
        for side in range(2):
            held_ref[slot ^ u, side * half : (side + 1) * half, :] = pieces[u][
                :, side * piece : (side + 1) * piece
            ].astype(f32)
    mean = sum(jnp.sum(held_ref[g], axis=-1, keepdims=True) for g in range(groups)) * (1.0 / width)
    square = 0.0
    for g in range(groups):
        centred = held_ref[g] - mean
        held_ref[g] = centred
        square = square + jnp.sum(centred * centred, axis=-1, keepdims=True)
    mixed_rate = lax.rsqrt(square * (1.0 / width) + norm_epsilon)
    mixed_rate_ref[...] = mixed_rate
    middle = jnp.concatenate([block[...] for block in inputs], axis=0).astype(f32)
    for g in range(groups):
        normal = held_ref[g] * mixed_rate
        held_ref[g] = normal
        mixed = (normal * mixed_gain_ref[g]).astype(bf16)
        mixed_ref[:, g * piece : (g + 1) * piece] = mixed
        middle = middle + dot(mixed, merge_ref[g * piece : (g + 1) * piece, :])
    middle_ref[...] = middle
    second_normal, _ = normalized(middle)
    second = (second_normal * second_gain_ref[...]).astype(bf16)
    second_ref[...] = second
    total = jnp.zeros((tokens, 1), f32)
    for step in range(steps):
        at = slice(step * WIDE, (step + 1) * WIDE)
        value = dot(second, expand_ref[:, at])
        share = 0.5 * (1.0 + lax.erf(value * 0.7071067811865476))
        gelu = value * share
        gelu_ref[:, at] = gelu
        slope = share + value * (0.3989422804014327 * jnp.exp(-0.5 * value * value))
        slope_ref[:, at] = slope.astype(bf16)
        total = total + jnp.sum(gelu, axis=-1, keepdims=True)
    mean = total * (1.0 / spread)
    total = jnp.zeros((tokens, 1), f32)
    for step in range(steps):
        centred = gelu_ref[:, step * WIDE : (step + 1) * WIDE] - mean
        total = total + jnp.sum(centred * centred, axis=-1, keepdims=True)
    rate = lax.rsqrt(total * (1.0 / spread) + norm_epsilon)
    hidden_rate_ref[...] = rate
    core = slot % 2
    for at in range(0, spread, 2 * BAND):
        ours, theirs = [], []
        for start in range(at, at + 2 * BAND, 2 * block):
            low = slice(start, start + block)
            high = slice(start + block, start + 2 * block)
            parts = []
            for part in (low, high):
                normal = (gelu_ref[:, part] - mean) * rate
                normal_ref[:, part] = normal.astype(bf16)
                parts.append((normal * hidden_gain_ref[:, part]).astype(bf16))
            ours.append(parts[0])
            theirs.append(parts[1])
        even, odd = jnp.concatenate(ours, axis=1), jnp.concatenate(theirs, axis=1)
        half_at = slice(at // 2, at // 2 + BAND)
        hidden_ref[:, half_at] = jnp.where(core == 0, even, odd)
        hidden_give_ref[:, half_at] = jnp.where(core == 0, odd, even)


def widen_call(
    place, pieces, inputs, mixed_gain, second_gain, hidden_gain, merge, expand
):
    slots = len(pieces)
    tokens = len(inputs) * inputs[0].shape[0]
    piece = pieces[0].shape[1] // 2
    width, spread = expand.shape
    groups = width // piece

    def low(*shape):
        return jax.ShapeDtypeStruct(shape, bf16)

    def full(*shape):
        return jax.ShapeDtypeStruct(shape, f32)

    return pl.pallas_call(
        functools.partial(
            widen_kernel, slots=slots, planes=len(inputs), groups=groups, width=width,
            spread=spread, block=spread // (slots * len(inputs)),
        ),
        out_shape=(
            low(tokens, width),
            full(tokens, width),
            low(tokens, width),
            low(tokens, spread // 2),
            low(tokens, spread // 2),
            low(tokens, spread),
            low(tokens, spread),
            full(slots, tokens, piece),
            full(tokens, 1),
            full(tokens, 1),
        ),
        in_specs=[pl.BlockSpec(memory_space=pltpu.SMEM)]
        + [vmem_spec()] * (5 + slots + len(inputs)),
        out_specs=(vmem_spec(),) * 10,
        scratch_shapes=[
            pltpu.VMEM((tokens, spread), f32),
        ],
        compiler_params=params(WIDEN_MIB),
        cost_estimate=cost(6 << 30, 6 << 20),
        name="widen",
    )(
        place, *pieces, *inputs, mixed_gain, second_gain, hidden_gain, merge, expand,
    )


def branch_kernel(place_ref, lengths_ref, *refs, slots):
    blocks, branch_ref = refs[:-1], refs[-1]
    seg = blocks[0].shape[0]
    limit = document_ends(lengths_ref, place_ref[0])[-1]
    for k, block in enumerate(blocks):
        offset = ((place_ref[0] ^ k) * slots + place_ref[1]) * seg
        valid = offset + lax.broadcasted_iota(jnp.int32, (seg, 1), 0) < limit
        branch_ref[k * seg : (k + 1) * seg, :] = jnp.where(
            valid, block[...], jnp.zeros((), bf16)
        )


def branch_call(place, lengths, blocks, slots):
    seg, width = blocks[0].shape
    return pl.pallas_call(
        functools.partial(branch_kernel, slots=slots),
        out_shape=jax.ShapeDtypeStruct((len(blocks) * seg, width), bf16),
        in_specs=[pl.BlockSpec(memory_space=pltpu.SMEM)] * 2 + [vmem_spec()] * len(blocks),
        out_specs=vmem_spec(),
        compiler_params=params(4),
        name="branch",
    )(place, lengths, *blocks)


def turn_kernel(*refs, slots, planes, groups, width, spread):
    (
        place_ref, branch_ref, normal_ref, slope_ref, middle_ref, held_ref,
        mixed_rate_ref, hidden_rate_ref,
        mixed_gain_ref, second_gain_ref, hidden_gain_ref, merge_ref, shrink_ref, expand_ref,
    ) = refs[:14]
    expanded_ref, mix_ref, grad_ref, parts_ref = refs[14:18]
    away = refs[18 : 18 + slots]
    results = refs[18 + slots : 18 + slots + planes]
    weighted_ref, sent_ref = refs[18 + slots + planes :]
    steps = spread // WIDE

    slot = place_ref[1]
    piece = width // groups
    tokens = middle_ref.shape[0]
    half = tokens // 2
    branch = branch_ref[...]
    result = middle_ref[...]
    weighted_sum = jnp.zeros((tokens, 1), f32)
    inner_sum = jnp.zeros((tokens, 1), f32)
    for step in range(steps):
        at = slice(step * WIDE, (step + 1) * WIDE)
        normal = normal_ref[:, at].astype(f32)
        hidden = (normal * hidden_gain_ref[:, at]).astype(bf16)
        result = result + dot(hidden, shrink_ref[at, :])
        grad_hidden = dot_nt(branch, shrink_ref[at, :])
        start = 2 * width + step * WIDE
        parts_ref[:, start : start + WIDE] = jnp.sum(grad_hidden * normal, axis=0, keepdims=True)
        weighted = grad_hidden * hidden_gain_ref[:, at]
        weighted_ref[:, at] = weighted
        weighted_sum = weighted_sum + jnp.sum(weighted, axis=-1, keepdims=True)
        inner_sum = inner_sum + jnp.sum(weighted * normal, axis=-1, keepdims=True)
    seg = tokens // planes
    for k in range(planes):
        results[k][...] = result[k * seg : (k + 1) * seg, :].astype(bf16)
    weighted_mean = weighted_sum * (1.0 / spread)
    inner_mean = inner_sum * (1.0 / spread)
    rate = hidden_rate_ref[...]
    grad_second = jnp.zeros((tokens, width), f32)
    for step in range(steps):
        at = slice(step * WIDE, (step + 1) * WIDE)
        grad = rate * (
            weighted_ref[:, at] - weighted_mean - normal_ref[:, at].astype(f32) * inner_mean
        )
        expanded = (grad * slope_ref[:, at].astype(f32)).astype(bf16)
        expanded_ref[:, at] = expanded
        grad_second = grad_second + dot_nt(expanded, expand_ref[:, at])
    second_normal, second_rate = normalized(middle_ref[...])
    parts_ref[:, width : 2 * width] = jnp.sum(grad_second * second_normal, axis=0, keepdims=True)
    grad_middle = branch.astype(f32) + norm_back(
        second_normal, second_rate, grad_second * second_gain_ref[...]
    )
    grad_ref[...] = grad_middle
    mix = grad_middle.astype(bf16)
    mix_ref[...] = mix
    grads = []
    weighted_sum = 0.0
    inner_sum = 0.0
    for g in range(groups):
        grad_mixed = dot_nt(mix, merge_ref[g * piece : (g + 1) * piece, :])
        parts_ref[:, g * piece : (g + 1) * piece] = jnp.sum(
            grad_mixed * held_ref[g], axis=0, keepdims=True
        )
        weighted = grad_mixed * mixed_gain_ref[g]
        grads.append(weighted)
        weighted_sum = weighted_sum + jnp.sum(weighted, axis=-1, keepdims=True)
        inner_sum = inner_sum + jnp.sum(weighted * held_ref[g], axis=-1, keepdims=True)
    weighted_mean = weighted_sum * (1.0 / width)
    inner_mean = inner_sum * (1.0 / width)
    for g in range(slots):
        if g < groups:
            sent_ref[g] = mixed_rate_ref[...] * (
                grads[g] - weighted_mean - held_ref[g] * inner_mean
            )
        else:
            sent_ref[g] = jnp.zeros(sent_ref.shape[1:], f32)
    for u in range(slots):
        for side in range(2):
            away[u][:, side * piece : (side + 1) * piece] = sent_ref[
                slot ^ u, side * half : (side + 1) * half, :
            ].astype(bf16)


def turn_call(
    place, branch, normal, slope, middle, held, mixed_rate, hidden_rate,
    mixed_gain, second_gain, hidden_gain, merge, shrink, expand, planes,
):
    slots, tokens, piece = held.shape
    width, spread = expand.shape
    groups = width // piece

    def low(*shape):
        return jax.ShapeDtypeStruct(shape, bf16)

    def full(*shape):
        return jax.ShapeDtypeStruct(shape, f32)

    outs = pl.pallas_call(
        functools.partial(
            turn_kernel, slots=slots, planes=planes, groups=groups, width=width, spread=spread
        ),
        out_shape=(
            low(tokens, spread),
            low(tokens, width),
            full(tokens, width),
            full(1, 2 * width + spread),
        )
        + (low(tokens // 2, 2 * piece),) * slots
        + (low(tokens // planes, width),) * planes,
        in_specs=[pl.BlockSpec(memory_space=pltpu.SMEM)] + [vmem_spec()] * 13,
        out_specs=(vmem_spec(),) * (4 + slots + planes),
        scratch_shapes=[
            pltpu.VMEM((tokens, spread), f32),
            pltpu.VMEM((slots, tokens, piece), f32),
        ],
        compiler_params=params(TURN_MIB),
        cost_estimate=cost(9 << 30, 8 << 20),
        name="turn",
    )(
        place, branch, normal, slope, middle, held, mixed_rate, hidden_rate,
        mixed_gain, second_gain, hidden_gain, merge, shrink, expand,
    )
    return outs[:4], outs[4 : 4 + slots], outs[4 + slots :]


def cut_out(outs, total_ref, place_ref, bands, steps, rows_each, axis, cut):
    whole_ref, firsts = outs[0], outs[1:]
    far_rank, side = place_ref[2] // 2, place_ref[3]
    for at, code in codes(steps):
        other, far = code & 1, code >> 1
        offset = pl.multiple_of((far_rank ^ far) * rows_each, rows_each)
        parts = []
        for first, wide in bands:
            column = pl.multiple_of(first + (side ^ other) * wide, 128)
            parts.append(
                total_ref[pl.ds(offset, rows_each), pl.ds(column, wide)].astype(bf16)
            )
        value = parts[0] if len(parts) == 1 else jnp.concatenate(parts, axis=1)
        whole_ref[at] = value
        for chain, first_ref in enumerate(firsts):
            if at[chain] == 1:
                band = slice(0, cut) if chain == 0 else slice(cut, None)
                first_ref[at[:chain] + at[chain + 1 :]] = (
                    value[band] if axis == 0 else value[:, band]
                )


def shrink_kernel(
    place_ref, hidden_ref, branch_ref, hidden_got_ref, branch_got_ref, *refs, cutting
):
    total_ref = refs[-1]
    spread, _ = total_ref.shape
    branch = jnp.concatenate([branch_ref[...], branch_got_ref[...]], axis=0)
    for at in range(0, spread, WIDE):
        hidden = jnp.concatenate(
            [hidden_ref[:, at : at + WIDE], hidden_got_ref[:, at : at + WIDE]], axis=0
        )
        total_ref[at : at + WIDE, :] = dot_tn(hidden, branch)
    cut_out(refs[:-1], total_ref, place_ref, **cutting)


def expand_kernel(
    place_ref, second_ref, mixed_ref, second_got_ref, mixed_got_ref,
    expanded_ref, mix_ref, expanded_got_ref, mix_got_ref, *refs, cutting,
):
    turned_ref, total_ref = refs[-2:]
    tokens, spread = expanded_ref.shape
    width = second_ref.shape[1]
    core = place_ref[2] % 2
    rows_each = cutting["rows_each"]

    def left(own_ref, got_ref):
        turned_ref[:, :tokens] = own_ref[...].astype(f32).T
        turned_ref[:, tokens:] = got_ref[...].astype(f32).T
        rows = [
            turned_ref[pl.ds(pl.multiple_of((2 * i + core) * rows_each, rows_each), rows_each), :]
            for i in range(width // (2 * rows_each))
        ]
        return jnp.concatenate(rows, axis=0).astype(bf16)

    second = left(second_ref, second_got_ref)
    for at in range(0, spread, WIDE):
        band = slice(at, at + WIDE)
        total_ref[:, band] = dot(
            second, jnp.concatenate([expanded_ref[:, band], expanded_got_ref[:, band]], axis=0)
        )
    mixed = left(mixed_ref, mixed_got_ref)
    total_ref[:, spread:] = dot(
        mixed, jnp.concatenate([mix_ref[...], mix_got_ref[...]], axis=0)
    )
    cut_out(refs[:-2], total_ref, place_ref, **cutting)


def outer_call(kernel, place, operands, rows, columns, bands, steps, size, axis, cut, scratch, name):
    rows_each = rows // size
    shape = (rows_each, columns // 2)
    low = (cut, shape[1]) if axis == 0 else (shape[0], cut)
    high = (shape[0] - cut, shape[1]) if axis == 0 else (shape[0], shape[1] - cut)
    pairs = (2,) * (len(steps) - 1)
    return pl.pallas_call(
        functools.partial(
            kernel,
            cutting=dict(bands=bands, steps=steps, rows_each=rows_each, axis=axis, cut=cut),
        ),
        out_shape=(
            jax.ShapeDtypeStruct((2,) + pairs + shape, bf16),
            jax.ShapeDtypeStruct(pairs + low, bf16),
            jax.ShapeDtypeStruct(pairs + high, bf16),
        ),
        in_specs=[pl.BlockSpec(memory_space=pltpu.SMEM)] + [vmem_spec()] * len(operands),
        out_specs=(vmem_spec(),) * 3,
        scratch_shapes=scratch + [pltpu.VMEM((rows // 2, columns), f32)],
        compiler_params=params(OUTER_MIB),
        cost_estimate=cost(2 << 30, 10 << 20),
        name=name,
    )(place, *operands)


def settle_kernel(place_ref, *refs):
    out = refs[-1]
    for k, ref in enumerate(refs[:-1]):
        out[place_ref[0] ^ k] = ref[...]


def settle_call(place, blocks):
    return pl.pallas_call(
        settle_kernel,
        out_shape=jax.ShapeDtypeStruct((len(blocks),) + blocks[0].shape, blocks[0].dtype),
        in_specs=[pl.BlockSpec(memory_space=pltpu.SMEM)] + [vmem_spec()] * len(blocks),
        out_specs=vmem_spec(),
        compiler_params=params(8),
        name="settle",
    )(place, *blocks)


def joined_slots_kernel(*refs, held):
    sources, outs = refs[:held], refs[held:]
    last = len(outs)
    for u, out in enumerate(outs):
        out[0] = sum(ref[u].astype(f32) for ref in sources).astype(bf16)
        out[1] = sum(ref[last].astype(f32) for ref in sources).astype(bf16)


def joined_slots_call(held, slots):
    _, rows, wide = held[0].shape
    return pl.pallas_call(
        functools.partial(joined_slots_kernel, held=len(held)),
        out_shape=(jax.ShapeDtypeStruct((2, rows, wide), bf16),) * slots,
        in_specs=[vmem_spec()] * len(held),
        out_specs=(vmem_spec(),) * slots,
        compiler_params=params(4),
        name="joined_slots",
    )(*held)


def heads_kernel(place_ref, *refs, groups, gains):
    joined_out, gains_out, held_ref = refs[-3:]
    pieces = refs[:-3]
    sums = []
    for u, ref in enumerate(pieces):
        held_ref[place_ref[1] ^ u] = ref[0].astype(f32)
        sums.append(ref[1].astype(f32))
    piece = pieces[0].shape[2] // 3
    for part in range(3):
        for g in range(groups):
            start = (part * groups + g) * piece
            joined_out[:, start : start + piece] = held_ref[
                g, :, part * piece : (part + 1) * piece
            ]
    while len(sums) > 1:
        sums = [sums[i] + sums[i + 1] for i in range(0, len(sums), 2)]
    wide = 3 * piece
    for r in range(-(-gains // wide)):
        end = min((r + 1) * wide, gains)
        gains_out[:, r * wide : end] = sums[0][r : r + 1, : end - r * wide]


def heads_call(place, blocks, width, gains):
    _, rows, wide = blocks[0].shape
    return pl.pallas_call(
        functools.partial(heads_kernel, groups=3 * width // wide, gains=gains),
        out_shape=(
            jax.ShapeDtypeStruct((rows, 3 * width), f32),
            jax.ShapeDtypeStruct((1, gains), f32),
        ),
        in_specs=[pl.BlockSpec(memory_space=pltpu.SMEM)] + [vmem_spec()] * len(blocks),
        out_specs=(vmem_spec(),) * 2,
        scratch_shapes=[pltpu.VMEM((len(blocks), rows, wide), f32)],
        compiler_params=params(8),
        name="heads_side_by_side",
    )(place, *blocks)


def input_kernel(*refs, planes, parts):
    inputs = refs[:planes]
    refs = refs[planes:]
    grad_ref, gain_ref = refs[:2]
    grad = sum(ref[at].astype(f32) for ref, at in zip(refs[2 : 2 + len(parts)], parts))
    outs = refs[2 + len(parts) :]
    normal, rate = normalized(
        jnp.concatenate([block[...] for block in inputs], axis=0).astype(f32)
    )
    value = grad_ref[...] + norm_back(normal, rate, grad * gain_ref[...])
    seg = value.shape[0] // planes
    for k in range(planes):
        outs[k][...] = value[k * seg : (k + 1) * seg, :].astype(bf16)


def input_call(inputs, grad_middle, gain, held, parts):
    planes = len(inputs)
    tokens, width = grad_middle.shape
    return pl.pallas_call(
        functools.partial(input_kernel, planes=planes, parts=parts),
        out_shape=(jax.ShapeDtypeStruct((tokens // planes, width), bf16),) * planes,
        in_specs=[vmem_spec()] * (2 + planes + len(held)),
        out_specs=(vmem_spec(),) * planes,
        compiler_params=params(16),
        name="input_back",
    )(*inputs, grad_middle, gain, *held)


def swap(value, axis, bits):
    size = lax.axis_size(axis)
    return lax.ppermute(value, axis, [(i, i ^ bits) for i in range(size)])


def pick(value, index, axis=0):
    return lax.dynamic_index_in_dim(value, index, axis, keepdims=False)


def in_hbm(*values):
    return [pltpu.with_memory_space_constraint(value, pltpu.HBM) for value in values]


def bits_of(size):
    return size.bit_length() - 1


def sums_kernel(*refs, listed, together):
    outs = refs[-1:] if together else refs[-len(listed) :]
    start = 0
    for i, terms in enumerate(listed):
        value = sum(refs[j][at].astype(f32) for j, at in terms).astype(bf16)
        if together:
            end = start + value.shape[together]
            outs[0][(..., slice(start, end)) + (slice(None),) * (-1 - together)] = value
            start = end
        else:
            outs[i][...] = value


def sums_call(sums, name, together=0):
    arrays, listed, shapes = [], [], []
    for terms in sums:
        entry = []
        for array, at in terms:
            where = [i for i, held in enumerate(arrays) if held is array]
            if not where:
                arrays.append(array)
                where = [len(arrays) - 1]
            entry.append((where[0], at))
        listed.append(entry)
        shapes.append(jax.eval_shape(lambda v, at=terms[0][1]: v[at], terms[0][0]).shape)
    if together:
        shape = list(shapes[0])
        shape[together] = sum(shape[together] for shape in shapes)
        shapes = [tuple(shape)]
    outs = pl.pallas_call(
        functools.partial(sums_kernel, listed=listed, together=together),
        out_shape=tuple(jax.ShapeDtypeStruct(shape, bf16) for shape in shapes),
        in_specs=[vmem_spec()] * len(arrays),
        out_specs=(vmem_spec(),) * len(shapes),
        compiler_params=params(4),
        name=name,
    )(*arrays)
    return outs[0] if together or len(shapes) == 1 else outs


class Halves:
    def __init__(self):
        self.entries = []
        self.chosen = {}

    def hold(self, array, names, bands=()):
        self.entries.append((array, names, dict(bands)))

    def terms(self, choice=()):
        chosen = dict(self.chosen)
        chosen.update(choice)
        return [
            (
                array,
                tuple(chosen[n] if n in chosen else bands.get(n, slice(None)) for n in names),
            )
            for array, names, bands in self.entries
        ]

    def receive(self, name, array, bands=()):
        self.chosen[name] = 0
        names = [n for n in self.entries[0][1] if n not in self.chosen]
        self.hold(array, names, bands)


def sides_kernel(place_ref, own_ref, other_ref, *outs):
    first = place_ref[3] == 0
    own, other = own_ref[...].astype(f32), other_ref[...].astype(f32)
    low, high = jnp.where(first, own, other), jnp.where(first, other, own)
    start = 0
    for out in outs:
        wide = out.shape[1] // 2
        out[:, :wide] = low[:, start : start + wide]
        out[:, wide:] = high[:, start : start + wide]
        start += wide


def sides_call(place, own, other, widths, name):
    rows = own.shape[0]
    return pl.pallas_call(
        sides_kernel,
        out_shape=tuple(jax.ShapeDtypeStruct((rows, wide), f32) for wide in widths),
        in_specs=[pl.BlockSpec(memory_space=pltpu.SMEM)] + [vmem_spec()] * 2,
        out_specs=(vmem_spec(),) * len(widths),
        compiler_params=params(8),
        name=name,
    )(place, own, other)


def per_device(
    layer_input, cotangent, doc_lengths, joined_weight, merge_weight, expand_weight,
    shrink_weight, first_gain, mixed_gain, second_gain, hidden_gain,
):
    _, planes, seg, width = layer_input.shape
    size = lax.axis_size("blk")
    slots = size // planes
    batches = lax.axis_size("batch")
    rank = lax.axis_index("blk")
    group_rank = lax.axis_index("batch")
    plane = rank // slots
    slot = rank % slots
    head_count = width // HEAD
    heads = -(-head_count // slots)
    groups = head_count // heads
    piece = heads * HEAD
    tokens = planes * seg
    length = slots * tokens
    side = group_rank % 2
    place = jnp.stack([plane, slot, rank, side]).astype(jnp.int32)

    def to_planes(blocks):
        return [pick(blocks, plane)] + [
            swap(pick(blocks, plane ^ k), "blk", k * slots) for k in range(1, planes)
        ]

    def all_slots(value):
        held = {0: value}
        for bit in reversed(range(bits_of(slots))):
            held.update({u | 1 << bit: swap(v, "blk", 1 << bit) for u, v in held.items()})
        return [held[u] for u in range(slots)]

    def over_slots(blocks):
        return [blocks[0]] + [swap(blocks[u], "blk", u) for u in range(1, slots)]

    spread = expand_weight.shape[1]
    first_arrived = to_planes(layer_input[0])
    own_start = jnp.minimum(slot, groups - 1) * piece
    own_weight = jnp.concatenate(
        [
            lax.dynamic_slice_in_dim(joined_weight, part * width + own_start, piece, 1)
            for part in range(3)
        ],
        axis=1,
    )
    lengths = doc_lengths[0]
    gain_row = first_gain.reshape(1, width)
    mixed_gain = mixed_gain.reshape(groups, 1, piece)
    second_gain = second_gain.reshape(1, width)
    hidden_gain = hidden_gain.reshape(1, spread)
    (
        first_arrived[-1], place, lengths, gain_row, mixed_gain, second_gain, hidden_gain, own_weight,
    ) = lax.optimization_barrier(
        (
            first_arrived[-1], place, lengths, gain_row, mixed_gain, second_gain, hidden_gain,
            own_weight,
        )
    )
    pieces = [all_slots(block) for block in first_arrived]
    (first, joined, factor), sent, shares = forward_call(
        place, lengths, gain_row, own_weight, pieces
    )
    sent, cotangent = lax.optimization_barrier((sent, cotangent))
    cotangent_blocks = to_planes(cotangent[0])
    (
        mixed, middle, second, hidden, hidden_give, normal, slope, held, mixed_rate, hidden_rate,
    ) = widen_call(
        place, over_slots(sent), first_arrived, mixed_gain, second_gain, hidden_gain, merge_weight,
        expand_weight,
    )
    hidden_give, cotangent_blocks = lax.optimization_barrier((hidden_give, cotangent_blocks))
    branch = branch_call(place, lengths, cotangent_blocks, slots)

    row_bits = list(range(1, bits_of(slots)))
    plane_bits = list(range(bits_of(slots), bits_of(size)))
    names = ["side"] + row_bits + plane_bits + ["rows", "columns"]
    steps = [0] + row_bits + plane_bits
    orders = (["side"] + row_bits, row_bits + ["side"])
    stages = len(orders[0])

    def cross(name, value):
        return swap(value, "batch", 1) if name == "side" else swap(value, "blk", 1 << name)

    def chains(axis, cut, whole):
        pair = [Halves(), Halves()]
        for chain, band in zip(pair, (slice(0, cut), slice(cut, None))):
            chain.hold(whole, names, {axis: band})
        return pair

    def sends(pair, at):
        return sums_call(
            [chain.terms({order[at]: 1}) for chain, order in zip(pair, orders)], "next_halves"
        )

    def crossed(at, values):
        return [cross(order[at], value) for order, value in zip(orders, values)]

    def arrive(pair, at, values):
        for chain, order, value in zip(pair, orders, values):
            chain.receive(order[at], value)

    def plane_depart(pair, bit, axis):
        together = -2 if axis == "rows" else -1
        return cross(
            bit, sums_call([chain.terms({bit: 1}) for chain in pair], "plane_halves", together)
        )

    def plane_arrive(pair, bit, axis, both):
        cut = pair[0].entries[0][2][axis].stop
        for chain, band in zip(pair, (slice(0, cut), slice(cut, None))):
            chain.receive(bit, both, {axis: band})

    def closed(pair, axis):
        together = -2 if axis == "rows" else -1
        value = sums_call([chain.terms() for chain in pair], "last_halves", together)
        for bit in range(1, bits_of(batches)):
            value = sums_call([[(value, ...), (swap(value, "batch", 1 << bit), ...)]], "groups")
        return value, swap(value, "batch", 1)

    cut = spread // size // 2
    shrink_whole, *shrink_firsts = outer_call(
        shrink_kernel, place,
        [hidden, branch, swap(hidden_give, "blk", 1), swap(branch, "blk", 1)],
        spread, width, ((0, width // 2),), steps, size, 0, cut, [], "shrink_outer",
    )
    shrink_sent = crossed(0, shrink_firsts)
    second_got, mixed_got = swap(second, "blk", 1), swap(mixed, "blk", 1)
    (expanded, mix, grad_middle, parts), away, results = turn_call(
        place, branch, normal, slope, middle, held, mixed_rate, hidden_rate,
        mixed_gain, second_gain, hidden_gain, merge_weight, shrink_weight, expand_weight, planes,
    )
    shrink_sent, second_got, mixed_got, expanded, mix = lax.optimization_barrier(
        (shrink_sent, second_got, mixed_got, expanded, mix)
    )
    shrink_chains = chains("rows", cut, shrink_whole)
    arrive(shrink_chains, 0, shrink_sent)

    returned = over_slots(away)
    expanded_got, mix_got = swap(expanded, "blk", 1), swap(mix, "blk", 1)
    returned, expanded_got, mix_got = lax.optimization_barrier((returned, expanded_got, mix_got))
    cut = ((spread + width) // 4 + 127) // 128 * 128
    expand_whole, *expand_firsts = outer_call(
        expand_kernel, place,
        [second, mixed, second_got, mixed_got, expanded, mix, expanded_got, mix_got],
        width, spread + width, ((0, spread // 2), (spread, width // 2)), steps, size, 1, cut,
        [pltpu.VMEM((width, 2 * tokens), f32)], "expand_outer",
    )
    for at in range(1, stages):
        shrink_sent = crossed(at, sends(shrink_chains, at))
        if at < stages - 1:
            arrive(shrink_chains, at, shrink_sent)
    expand_firsts, results = lax.optimization_barrier((expand_firsts, results))
    result_blocks = [results[0]] + [
        swap(results[k], "blk", k * slots) for k in range(1, planes)
    ]
    returned, expand_firsts, shrink_sent = lax.optimization_barrier(
        (returned, expand_firsts, shrink_sent)
    )
    arrive(shrink_chains, stages - 1, shrink_sent)
    expand_sent = crossed(0, expand_firsts)
    shrink_both = plane_depart(shrink_chains, plane_bits[0], "rows")
    joined_keep, joined_give, branch_keep, branch_give = backward_call(
        place, first, joined, factor, own_weight, gain_row, parts, returned, shares, planes
    )
    (
        joined_give, branch_give, shrink_both, expand_sent, result_blocks,
    ) = lax.optimization_barrier(
        (joined_give, branch_give, shrink_both, expand_sent, result_blocks)
    )
    plane_arrive(shrink_chains, plane_bits[0], "rows", shrink_both)
    expand_chains = chains("columns", cut, expand_whole)
    arrive(expand_chains, 0, expand_sent)

    joined_got = swap(joined_give, "blk", 1 << plane_bits[0])
    branch_got = swap(branch_give, "blk", 1)
    for at in range(1, stages):
        expand_sent = crossed(at, sends(expand_chains, at))
        if at < stages - 1:
            arrive(expand_chains, at, expand_sent)
    for bit in plane_bits[1:]:
        shrink_both = plane_depart(shrink_chains, bit, "rows")
        if bit != plane_bits[-1]:
            plane_arrive(shrink_chains, bit, "rows", shrink_both)
    branch_held, prefixes = [branch_keep, branch_got], [(), ()]
    for bit in row_bits:
        give = sums_call(
            [[(v, p + (1,)) for v, p in zip(branch_held, prefixes)]], "branch_halves"
        )
        prefixes = [p + (0,) for p in prefixes] + [()]
        branch_held.append(swap(give, "blk", 1 << bit))
    joined_got, branch_held[-1], expand_sent, shrink_both = lax.optimization_barrier(
        (joined_got, branch_held[-1], expand_sent, shrink_both)
    )
    arrive(expand_chains, stages - 1, expand_sent)
    plane_arrive(shrink_chains, plane_bits[-1], "rows", shrink_both)

    expand_both = plane_depart(expand_chains, plane_bits[0], "columns")
    joined_terms = [(joined_keep, 0), (joined_got, 0)]
    blocks = planes * slots // 2
    gain_terms = [(joined_give, blocks), (joined_got, blocks)]
    for bit in plane_bits[1:]:
        blocks //= 2
        joined_give = sums_call(
            [
                [(v, slice(start + blocks, start + 2 * blocks)) for v, start in joined_terms],
                [(v, slice(at, at + 1)) for v, at in gain_terms],
            ],
            "joined_halves", -3,
        )
        joined_got = swap(joined_give, "blk", 1 << bit)
        joined_terms.append((joined_got, 0))
        gain_terms = [(joined_give, blocks), (joined_got, blocks)]
    input_blocks = input_call(
        first_arrived, grad_middle, gain_row, branch_held, prefixes
    )
    input_blocks = [input_blocks[0]] + [
        swap(input_blocks[k], "blk", k * slots) for k in range(1, planes)
    ]
    joined_last = sums_call(
        [
            [(v, slice(start, start + slots)) for v, start in joined_terms],
            [(v, slice(at, at + 1)) for v, at in gain_terms],
        ],
        "joined_last", -3,
    )
    held = [joined_last]
    for bit in range(bits_of(batches)):
        if len(held) > 1:
            held = [sums_call([[(v, ...) for v in held]], "joined_groups")]
        held.append(swap(held[0], "batch", 1 << bit))
    joined_sent = joined_slots_call(held, slots)
    joined_grad, gain_grads = heads_call(
        place,
        [joined_sent[0]] + [swap(joined_sent[u], "blk", u) for u in range(1, slots)],
        width, 3 * width + spread,
    )
    shrink_grad, = sides_call(place, *closed(shrink_chains, "rows"), (width,), "shrink_sides")
    plane_arrive(expand_chains, plane_bits[0], "columns", expand_both)
    for bit in plane_bits[1:]:
        expand_both = plane_depart(expand_chains, bit, "columns")
        plane_arrive(expand_chains, bit, "columns", expand_both)
    expand_grad, merge_grad = sides_call(
        place, *closed(expand_chains, "columns"), (spread, width), "expand_sides"
    )
    layer_result = settle_call(place, result_blocks).reshape(layer_input.shape)
    input_grad = settle_call(place, input_blocks).reshape(layer_input.shape)
    gain_grads = gain_grads[0]
    return (
        layer_result, input_grad, joined_grad, merge_grad, expand_grad,
        shrink_grad, gain_grads[:width], gain_grads[width : 2 * width],
        gain_grads[2 * width : 3 * width], gain_grads[3 * width :],
    )


def solution(mesh):
    rows = P("batch", None, "blk", None)
    return jax.shard_map(
        per_device,
        mesh=mesh,
        in_specs=(rows, rows, P("batch", None, None)) + (P(),) * 8,
        out_specs=(rows, rows) + (P("blk", None),) * 4 + (P(),) * 4,
        check_vma=False,
    )
```

```python
import functools

import jax
import jax.numpy as jnp
from jax import lax
from jax.experimental import pallas as pl
from jax.experimental.pallas import tpu as pltpu
from jax.sharding import PartitionSpec as P

HEAD = 64
TILE = 256
WIDE = 512
BAND = 384
FORWARD_MIB = 14
BACKWARD_MIB = 14
WIDEN_MIB = 11
TURN_MIB = 11
OUTER_MIB = 16
big_negative = -1e30
norm_epsilon = 1e-05

f32 = jnp.float32
bf16 = jnp.bfloat16


def dot(left, right):
    return jnp.dot(left, right, preferred_element_type=f32)


def dot_nt(left, right):
    return lax.dot_general(left, right, (((1,), (1,)), ((), ())), preferred_element_type=f32)


def dot_tn(left, right):
    return lax.dot_general(left, right, (((0,), (0,)), ((), ())), preferred_element_type=f32)


def normalized(values):
    centred = values - jnp.mean(values, axis=-1, keepdims=True)
    rate = lax.rsqrt(jnp.mean(centred * centred, axis=-1, keepdims=True) + norm_epsilon)
    return centred * rate, rate


def norm_back(normal, rate, weighted):
    return rate * (
        weighted
        - jnp.mean(weighted, axis=-1, keepdims=True)
        - normal * jnp.mean(weighted * normal, axis=-1, keepdims=True)
    )


def vmem_spec():
    return pl.BlockSpec(memory_space=pltpu.VMEM)


def hbm_spec():
    return pl.BlockSpec(memory_space=pltpu.HBM)


def params(mebibytes):
    return pltpu.CompilerParams(vmem_limit_bytes=mebibytes * 1024 * 1024)


def cost(flops, moved):
    return pl.CostEstimate(flops=flops, bytes_accessed=moved, transcendentals=0)


def document_ends(lengths_ref, plane):
    ends, end = [], jnp.int32(0)
    for d in range(lengths_ref.shape[1]):
        end = end + lengths_ref[plane, d]
        ends.append(end)
    return ends


def columns_at(step):
    return pl.ds(pl.multiple_of(step * WIDE, WIDE), WIDE)


def codes(steps):
    listed = [((), 0)]
    for bit in steps:
        listed = [(at + (b,), code | (b << bit)) for at, code in listed for b in (0, 1)]
    return listed


def forward_kernel(*refs, planes, slots, seg, heads):
    place_ref, lengths_ref, gain_ref, weight_ref = refs[:4]
    pieces = refs[4 : 4 + slots * planes]
    refs = refs[4 + slots * planes :]
    length = planes * slots * seg
    tiles = length // TILE
    first_ref, joined_ref, factor_ref = refs[:3]
    sent = refs[3 : 3 + slots]
    shares = refs[3 + slots : 3 + slots + tiles]
    rows_ref, attention_ref = refs[3 + slots + tiles :]
    plane, slot = place_ref[0], place_ref[1]
    for u in range(slots):
        for k in range(planes):
            offset = ((plane ^ k) * slots + (slot ^ u)) * seg
            rows_ref[pl.ds(pl.multiple_of(offset, seg), seg), :] = pieces[k * slots + u][...]
    width = heads * HEAD

    def project(tile, carry):
        rows = pl.ds(pl.multiple_of(tile * TILE, TILE), TILE)
        normal, _ = normalized(rows_ref[rows, :].astype(f32))
        first = (normal * gain_ref[...]).astype(bf16)
        first_ref[rows, :] = first
        joined = dot(first, weight_ref[...]).astype(bf16)
        for part in range(3):
            for h in range(heads):
                column = part * width + h * HEAD
                value = joined[:, column : column + HEAD]
                if part == 0:
                    value = value * jnp.asarray(0.125, bf16)
                joined_ref[part * heads + h, rows, :] = value
        return carry

    lax.fori_loop(0, tiles, project, 0, unroll=True)
    ends = document_ends(lengths_ref, plane)
    for q in reversed(range(tiles)):
        rows = slice(q * TILE, (q + 1) * TILE)
        reach = (q + 1) * TILE
        places = q * TILE + lax.broadcasted_iota(jnp.int32, (TILE, 1), 0)
        start = jnp.zeros((TILE, 1), jnp.int32)
        for end in ends:
            start = jnp.maximum(start, jnp.where(places >= end, end, 0))
        query_pos = q * TILE + lax.broadcasted_iota(jnp.int32, (TILE, reach), 0)
        key_pos = lax.broadcasted_iota(jnp.int32, (TILE, reach), 1)
        allowed = (key_pos <= query_pos) & (key_pos >= start)
        for h in range(heads):
            scores = dot_nt(joined_ref[h, rows, :], joined_ref[heads + h, :reach, :])
            scores = jnp.where(allowed, scores, big_negative)
            peak = jnp.max(scores, axis=-1, keepdims=True)
            raised = jnp.exp(scores - peak)
            total = jnp.sum(raised, axis=-1, keepdims=True)
            share = raised.astype(bf16)
            shares[q][h] = share
            factor = 1.0 / total
            factor_ref[rows, h : h + 1] = factor
            attention_ref[h, rows, :] = factor * dot(
                share, joined_ref[2 * heads + h, :reach, :]
            )
    half = planes // 2
    for u in range(slots):
        for k in range(planes):
            offset = ((plane ^ k) * slots + (slot ^ u)) * seg
            rows = slice(k % half * seg, (k % half + 1) * seg)
            for h in range(heads):
                part = attention_ref[h, pl.ds(pl.multiple_of(offset, seg), seg), :]
                column = k // half * width + h * HEAD
                sent[u][rows, column : column + HEAD] = part.astype(bf16)


def forward_call(place, lengths, gain, weight, pieces):
    planes, slots = len(pieces), len(pieces[0])
    seg, width = pieces[0][0].shape
    length = planes * slots * seg
    heads = weight.shape[1] // (3 * HEAD)
    kernel = functools.partial(forward_kernel, planes=planes, slots=slots, seg=seg, heads=heads)
    packed = jax.ShapeDtypeStruct((planes * seg // 2, 2 * heads * HEAD), bf16)
    tiled = [(heads, TILE, reach) for reach in range(TILE, length + 1, TILE)]
    outs = pl.pallas_call(
        kernel,
        out_shape=(
            pltpu.VMEM((length, width), bf16),
            pltpu.VMEM((3 * heads, length, HEAD), bf16),
            pltpu.VMEM((length, heads), f32),
        )
        + (packed,) * slots
        + tuple(pltpu.VMEM(shape, bf16) for shape in tiled),
        in_specs=[pl.BlockSpec(memory_space=pltpu.SMEM)] * 2
        + [vmem_spec()] * (2 + slots * planes),
        out_specs=(vmem_spec(),) * (3 + slots + len(tiled)),
        scratch_shapes=[
            pltpu.VMEM((length, width), bf16),
            pltpu.VMEM((heads, length, HEAD), f32),
        ],
        compiler_params=params(FORWARD_MIB * length // 1024),
        cost_estimate=cost(8 << 30, 8 << 20),
        name="attention_forward",
    )(place, lengths, gain, weight, *[block for blocks in pieces for block in blocks])
    return outs[:3], outs[3 : 3 + slots], outs[3 + slots :]


def backward_kernel(*refs, planes, slots, seg, heads, rows_each):
    place_ref, first_ref, joined_ref, factor_ref, weight_ref, gain_ref, parts_ref = refs[:7]
    pieces = refs[7 : 7 + slots]
    length = planes * slots * seg
    tiles = length // TILE
    refs = refs[7 + slots :]
    shares = refs[:tiles]
    joined_keep, joined_give, branch_keep, branch_give = refs[tiles : tiles + 4]
    grad_ref, arrived_ref, key_ref, value_ref, total_ref, outer_ref, row_ref = refs[tiles + 4 :]
    plane, slot = place_ref[0], place_ref[1]
    width = heads * HEAD
    half = planes // 2
    for u in range(slots):
        for k in range(planes):
            offset = ((plane ^ k) * slots + (slot ^ u)) * seg
            column = k // half * width
            arrived_ref[pl.ds(pl.multiple_of(offset, seg), seg), :] = pieces[u][
                k % half * seg : (k % half + 1) * seg, column : column + width
            ]
    for h in range(heads):
        for q in reversed(range(tiles)):
            rows = slice(q * TILE, (q + 1) * TILE)
            reach = (q + 1) * TILE
            factor = factor_ref[rows, h : h + 1]
            grad = (arrived_ref[rows, h * HEAD : (h + 1) * HEAD].astype(f32) * factor).astype(bf16)
            share = shares[q][h]
            product = share.astype(f32) * dot_nt(grad, joined_ref[2 * heads + h, :reach, :])
            inner = jnp.sum(product, axis=-1, keepdims=True)
            grad_scores = (product - share.astype(f32) * (inner * factor)).astype(bf16)
            query_grad = dot(grad_scores, joined_ref[heads + h, :reach, :]) * 0.125
            grad_ref[rows, h * HEAD : (h + 1) * HEAD] = query_grad.astype(bf16)
            key_add = dot_tn(joined_ref[h, rows, :], grad_scores)
            value_add = dot_tn(grad, share)
            if q == tiles - 1:
                key_ref[...] = key_add
                value_ref[...] = value_add
            else:
                key_ref[:, :reach] += key_add
                value_ref[:, :reach] += value_add
        for part, source in ((1, key_ref), (2, value_ref)):
            column = part * width + h * HEAD
            for q in range(tiles):
                rows = slice(q * TILE, (q + 1) * TILE)
                grad_ref[rows, column : column + HEAD] = source[:, rows].T.astype(bf16)

    def back(tile, carry):
        rows = pl.ds(pl.multiple_of(tile * TILE, TILE), TILE)
        total_ref[rows, :] = dot_nt(grad_ref[rows, :], weight_ref[...])
        return carry

    lax.fori_loop(0, tiles, back, 0, unroll=True)
    for at, code in codes(range(1, bits_of(slots))):
        for out, u in ((branch_keep, code), (branch_give, code | 1)):
            for k in range(planes):
                offset = ((plane ^ k) * slots + (slot ^ u)) * seg
                out[at + (slice(k * seg, (k + 1) * seg),)] = total_ref[
                    pl.ds(pl.multiple_of(offset, seg), seg), :
                ].astype(bf16)
    model = first_ref.shape[1]
    for d in range(0, model, TILE):
        outer = dot_tn(first_ref[:, d : d + TILE], grad_ref[...])
        outer_ref[d : d + TILE, :] = outer
        scaled = jnp.sum(outer * weight_ref[d : d + TILE, :].astype(f32), axis=-1, keepdims=True)
        scaled = jnp.broadcast_to(scaled, (TILE, 128)).T
        row_ref[:, d : d + TILE] = scaled[:1] / gain_ref[:, d : d + TILE]
    wide = 3 * width
    row_ref[:, model : model + parts_ref.shape[1]] = parts_ref[...]
    gains = model + parts_ref.shape[1]
    half = planes * slots // 2
    at = 0
    for _, code in codes(range(bits_of(planes))):
        for u in range(slots):
            offset = ((plane ^ code) * slots + (slot ^ u)) * rows_each
            out = joined_keep if at < half else joined_give
            out[at % half] = outer_ref[
                pl.ds(pl.multiple_of(offset, rows_each), rows_each), :
            ].astype(bf16)
            at += 1
    joined_give[half] = jnp.zeros((rows_each, wide), bf16)
    for r in range(-(-gains // wide)):
        end = min((r + 1) * wide, gains)
        joined_give[half, r : r + 1, : end - r * wide] = row_ref[:, r * wide : end].astype(bf16)


def backward_call(
    place, first, joined, factor, weight, gain, parts, pieces, shares, planes
):
    slots = len(pieces)
    tokens = pieces[0].shape[0] * 2
    heads, length = joined.shape[0] // 3, joined.shape[1]
    width = weight.shape[0]
    rows_each = width // (planes * slots)
    kernel = functools.partial(
        backward_kernel, planes=planes, slots=slots, seg=tokens // planes, heads=heads,
        rows_each=rows_each,
    )
    pairs = (2,) * (bits_of(slots) - 1)
    wide = 3 * heads * HEAD
    row = -(-(width + parts.shape[1]) // 128) * 128
    return pl.pallas_call(
        kernel,
        out_shape=(
            jax.ShapeDtypeStruct((planes * slots // 2, rows_each, wide), bf16),
            jax.ShapeDtypeStruct((planes * slots // 2 + 1, rows_each, wide), bf16),
            jax.ShapeDtypeStruct(pairs + (tokens, width), bf16),
            jax.ShapeDtypeStruct(pairs + (tokens, width), bf16),
        ),
        in_specs=[pl.BlockSpec(memory_space=pltpu.SMEM)]
        + [vmem_spec()] * (6 + slots + len(shares)),
        out_specs=(vmem_spec(),) * 4,
        scratch_shapes=[
            pltpu.VMEM((length, wide), bf16),
            pltpu.VMEM((length, heads * HEAD), bf16),
            pltpu.VMEM((HEAD, length), f32),
            pltpu.VMEM((HEAD, length), f32),
            pltpu.VMEM((length, width), f32),
            pltpu.VMEM((width, wide), f32),
            pltpu.VMEM((1, row), f32),
        ],
        compiler_params=params(BACKWARD_MIB * length // 1024),
        cost_estimate=cost(10 << 30, 10 << 20),
        name="attention_backward",
    )(place, first, joined, factor, weight, gain, parts, *pieces, *shares)


def widen_kernel(*refs, slots, planes, groups, width, spread, block):
    place_ref = refs[0]
    pieces = refs[1 : 1 + slots]
    inputs = refs[1 + slots : 1 + slots + planes]
    refs = refs[1 + slots + planes :]
    mixed_gain_ref, second_gain_ref, hidden_gain_ref, merge_ref, expand_ref = refs[:5]
    (
        mixed_ref, middle_ref, second_ref, hidden_ref, hidden_give_ref, normal_ref, slope_ref,
        held_ref, mixed_rate_ref, hidden_rate_ref,
    ) = refs[5:15]
    (gelu_ref,) = refs[15:]
    steps = spread // WIDE

    slot = place_ref[1]
    piece = width // groups
    tokens = planes * inputs[0].shape[0]
    half = tokens // 2
    for u in range(slots):
        for side in range(2):
            held_ref[slot ^ u, side * half : (side + 1) * half, :] = pieces[u][
                :, side * piece : (side + 1) * piece
            ].astype(f32)
    mean = sum(jnp.sum(held_ref[g], axis=-1, keepdims=True) for g in range(groups)) * (1.0 / width)
    square = 0.0
    for g in range(groups):
        centred = held_ref[g] - mean
        held_ref[g] = centred
        square = square + jnp.sum(centred * centred, axis=-1, keepdims=True)
    mixed_rate = lax.rsqrt(square * (1.0 / width) + norm_epsilon)
    mixed_rate_ref[...] = mixed_rate
    middle = jnp.concatenate([block[...] for block in inputs], axis=0).astype(f32)
    for g in range(groups):
        normal = held_ref[g] * mixed_rate
        held_ref[g] = normal
        mixed = (normal * mixed_gain_ref[g]).astype(bf16)
        mixed_ref[:, g * piece : (g + 1) * piece] = mixed
        middle = middle + dot(mixed, merge_ref[g * piece : (g + 1) * piece, :])
    middle_ref[...] = middle
    second_normal, _ = normalized(middle)
    second = (second_normal * second_gain_ref[...]).astype(bf16)
    second_ref[...] = second
    total = jnp.zeros((tokens, 1), f32)

    def widen(step, total):
        at = columns_at(step)
        value = dot(second, expand_ref[:, at])
        share = 0.5 * (1.0 + lax.erf(value * 0.7071067811865476))
        gelu = value * share
        gelu_ref[:, at] = gelu
        slope = share + value * (0.3989422804014327 * jnp.exp(-0.5 * value * value))
        slope_ref[:, at] = slope.astype(bf16)
        return total + jnp.sum(gelu, axis=-1, keepdims=True)

    total = lax.fori_loop(0, steps, widen, total)
    mean = total * (1.0 / spread)
    total = jnp.zeros((tokens, 1), f32)
    for step in range(steps):
        centred = gelu_ref[:, step * WIDE : (step + 1) * WIDE] - mean
        total = total + jnp.sum(centred * centred, axis=-1, keepdims=True)
    rate = lax.rsqrt(total * (1.0 / spread) + norm_epsilon)
    hidden_rate_ref[...] = rate
    core = slot % 2
    for at in range(0, spread, 2 * BAND):
        ours, theirs = [], []
        for start in range(at, at + 2 * BAND, 2 * block):
            low = slice(start, start + block)
            high = slice(start + block, start + 2 * block)
            parts = []
            for part in (low, high):
                normal = (gelu_ref[:, part] - mean) * rate
                normal_ref[:, part] = normal.astype(bf16)
                parts.append((normal * hidden_gain_ref[:, part]).astype(bf16))
            ours.append(parts[0])
            theirs.append(parts[1])
        even, odd = jnp.concatenate(ours, axis=1), jnp.concatenate(theirs, axis=1)
        half_at = slice(at // 2, at // 2 + BAND)
        hidden_ref[:, half_at] = jnp.where(core == 0, even, odd)
        hidden_give_ref[:, half_at] = jnp.where(core == 0, odd, even)


def widen_call(
    place, pieces, inputs, mixed_gain, second_gain, hidden_gain, merge, expand
):
    slots = len(pieces)
    tokens = len(inputs) * inputs[0].shape[0]
    piece = pieces[0].shape[1] // 2
    width, spread = expand.shape
    groups = width // piece

    def low(*shape):
        return jax.ShapeDtypeStruct(shape, bf16)

    def full(*shape):
        return jax.ShapeDtypeStruct(shape, f32)

    return pl.pallas_call(
        functools.partial(
            widen_kernel, slots=slots, planes=len(inputs), groups=groups, width=width,
            spread=spread, block=spread // (slots * len(inputs)),
        ),
        out_shape=(
            low(tokens, width),
            full(tokens, width),
            low(tokens, width),
            low(tokens, spread // 2),
            low(tokens, spread // 2),
            low(tokens, spread),
            low(tokens, spread),
            full(slots, tokens, piece),
            full(tokens, 1),
            full(tokens, 1),
        ),
        in_specs=[pl.BlockSpec(memory_space=pltpu.SMEM)]
        + [vmem_spec()] * (5 + slots + len(inputs)),
        out_specs=(vmem_spec(),) * 10,
        scratch_shapes=[
            pltpu.VMEM((tokens, spread), f32),
        ],
        compiler_params=params(WIDEN_MIB),
        cost_estimate=cost(6 << 30, 6 << 20),
        name="widen",
    )(
        place, *pieces, *inputs, mixed_gain, second_gain, hidden_gain, merge, expand,
    )


def branch_kernel(place_ref, lengths_ref, *refs, slots):
    blocks, branch_ref = refs[:-1], refs[-1]
    seg = blocks[0].shape[0]
    limit = document_ends(lengths_ref, place_ref[0])[-1]
    for k, block in enumerate(blocks):
        offset = ((place_ref[0] ^ k) * slots + place_ref[1]) * seg
        valid = offset + lax.broadcasted_iota(jnp.int32, (seg, 1), 0) < limit
        branch_ref[k * seg : (k + 1) * seg, :] = jnp.where(
            valid, block[...], jnp.zeros((), bf16)
        )


def branch_call(place, lengths, blocks, slots):
    seg, width = blocks[0].shape
    return pl.pallas_call(
        functools.partial(branch_kernel, slots=slots),
        out_shape=jax.ShapeDtypeStruct((len(blocks) * seg, width), bf16),
        in_specs=[pl.BlockSpec(memory_space=pltpu.SMEM)] * 2 + [vmem_spec()] * len(blocks),
        out_specs=vmem_spec(),
        compiler_params=params(4),
        name="branch",
    )(place, lengths, *blocks)


def turn_kernel(*refs, slots, planes, groups, width, spread):
    (
        place_ref, branch_ref, normal_ref, slope_ref, middle_ref, held_ref,
        mixed_rate_ref, hidden_rate_ref,
        mixed_gain_ref, second_gain_ref, hidden_gain_ref, merge_ref, shrink_ref, expand_ref,
    ) = refs[:14]
    expanded_ref, mix_ref, grad_ref, parts_ref = refs[14:18]
    away = refs[18 : 18 + slots]
    results = refs[18 + slots : 18 + slots + planes]
    weighted_ref, sent_ref = refs[18 + slots + planes :]
    steps = spread // WIDE

    slot = place_ref[1]
    piece = width // groups
    tokens = middle_ref.shape[0]
    half = tokens // 2
    branch = branch_ref[...]
    result = middle_ref[...]
    weighted_sum = jnp.zeros((tokens, 1), f32)
    inner_sum = jnp.zeros((tokens, 1), f32)
    for step in range(steps):
        at = slice(step * WIDE, (step + 1) * WIDE)
        normal = normal_ref[:, at].astype(f32)
        hidden = (normal * hidden_gain_ref[:, at]).astype(bf16)
        result = result + dot(hidden, shrink_ref[at, :])
        grad_hidden = dot_nt(branch, shrink_ref[at, :])
        start = 2 * width + step * WIDE
        parts_ref[:, start : start + WIDE] = jnp.sum(grad_hidden * normal, axis=0, keepdims=True)
        weighted = grad_hidden * hidden_gain_ref[:, at]
        weighted_ref[:, at] = weighted
        weighted_sum = weighted_sum + jnp.sum(weighted, axis=-1, keepdims=True)
        inner_sum = inner_sum + jnp.sum(weighted * normal, axis=-1, keepdims=True)
    seg = tokens // planes
    for k in range(planes):
        results[k][...] = result[k * seg : (k + 1) * seg, :].astype(bf16)
    weighted_mean = weighted_sum * (1.0 / spread)
    inner_mean = inner_sum * (1.0 / spread)
    rate = hidden_rate_ref[...]
    grad_second = jnp.zeros((tokens, width), f32)
    for step in range(steps):
        at = slice(step * WIDE, (step + 1) * WIDE)
        grad = rate * (
            weighted_ref[:, at] - weighted_mean - normal_ref[:, at].astype(f32) * inner_mean
        )
        expanded = (grad * slope_ref[:, at].astype(f32)).astype(bf16)
        expanded_ref[:, at] = expanded
        grad_second = grad_second + dot_nt(expanded, expand_ref[:, at])
    second_normal, second_rate = normalized(middle_ref[...])
    parts_ref[:, width : 2 * width] = jnp.sum(grad_second * second_normal, axis=0, keepdims=True)
    grad_middle = branch.astype(f32) + norm_back(
        second_normal, second_rate, grad_second * second_gain_ref[...]
    )
    grad_ref[...] = grad_middle
    mix = grad_middle.astype(bf16)
    mix_ref[...] = mix
    grads = []
    weighted_sum = 0.0
    inner_sum = 0.0
    for g in range(groups):
        grad_mixed = dot_nt(mix, merge_ref[g * piece : (g + 1) * piece, :])
        parts_ref[:, g * piece : (g + 1) * piece] = jnp.sum(
            grad_mixed * held_ref[g], axis=0, keepdims=True
        )
        weighted = grad_mixed * mixed_gain_ref[g]
        grads.append(weighted)
        weighted_sum = weighted_sum + jnp.sum(weighted, axis=-1, keepdims=True)
        inner_sum = inner_sum + jnp.sum(weighted * held_ref[g], axis=-1, keepdims=True)
    weighted_mean = weighted_sum * (1.0 / width)
    inner_mean = inner_sum * (1.0 / width)
    for g in range(slots):
        if g < groups:
            sent_ref[g] = mixed_rate_ref[...] * (
                grads[g] - weighted_mean - held_ref[g] * inner_mean
            )
        else:
            sent_ref[g] = jnp.zeros(sent_ref.shape[1:], f32)
    for u in range(slots):
        for side in range(2):
            away[u][:, side * piece : (side + 1) * piece] = sent_ref[
                slot ^ u, side * half : (side + 1) * half, :
            ].astype(bf16)


def turn_call(
    place, branch, normal, slope, middle, held, mixed_rate, hidden_rate,
    mixed_gain, second_gain, hidden_gain, merge, shrink, expand, planes,
):
    slots, tokens, piece = held.shape
    width, spread = expand.shape
    groups = width // piece

    def low(*shape):
        return jax.ShapeDtypeStruct(shape, bf16)

    def full(*shape):
        return jax.ShapeDtypeStruct(shape, f32)

    outs = pl.pallas_call(
        functools.partial(
            turn_kernel, slots=slots, planes=planes, groups=groups, width=width, spread=spread
        ),
        out_shape=(
            low(tokens, spread),
            low(tokens, width),
            full(tokens, width),
            full(1, 2 * width + spread),
        )
        + (low(tokens // 2, 2 * piece),) * slots
        + (low(tokens // planes, width),) * planes,
        in_specs=[pl.BlockSpec(memory_space=pltpu.SMEM)] + [vmem_spec()] * 13,
        out_specs=(vmem_spec(),) * (4 + slots + planes),
        scratch_shapes=[
            pltpu.VMEM((tokens, spread), f32),
            pltpu.VMEM((slots, tokens, piece), f32),
        ],
        compiler_params=params(TURN_MIB),
        cost_estimate=cost(9 << 30, 8 << 20),
        name="turn",
    )(
        place, branch, normal, slope, middle, held, mixed_rate, hidden_rate,
        mixed_gain, second_gain, hidden_gain, merge, shrink, expand,
    )
    return outs[:4], outs[4 : 4 + slots], outs[4 + slots :]


def cut_out(outs, total_ref, place_ref, bands, steps, rows_each, axis, cut):
    whole_ref, firsts = outs[0], outs[1:]
    far_rank, side = place_ref[2] // 2, place_ref[3]
    for at, code in codes(steps):
        other, far = code & 1, code >> 1
        offset = pl.multiple_of((far_rank ^ far) * rows_each, rows_each)
        parts = []
        for first, wide in bands:
            column = pl.multiple_of(first + (side ^ other) * wide, 128)
            parts.append(
                total_ref[pl.ds(offset, rows_each), pl.ds(column, wide)].astype(bf16)
            )
        value = parts[0] if len(parts) == 1 else jnp.concatenate(parts, axis=1)
        whole_ref[at] = value
        for chain, first_ref in enumerate(firsts):
            if at[chain] == 1:
                band = slice(0, cut) if chain == 0 else slice(cut, None)
                first_ref[at[:chain] + at[chain + 1 :]] = (
                    value[band] if axis == 0 else value[:, band]
                )


def shrink_kernel(
    place_ref, hidden_ref, branch_ref, hidden_got_ref, branch_got_ref, *refs, cutting
):
    total_ref = refs[-1]
    spread, _ = total_ref.shape
    branch = jnp.concatenate([branch_ref[...], branch_got_ref[...]], axis=0)

    def multiply(step, carry):
        at = columns_at(step)
        hidden = jnp.concatenate([hidden_ref[:, at], hidden_got_ref[:, at]], axis=0)
        total_ref[at, :] = dot_tn(hidden, branch)
        return carry

    lax.fori_loop(0, spread // WIDE, multiply, 0)
    cut_out(refs[:-1], total_ref, place_ref, **cutting)


def expand_kernel(
    place_ref, second_ref, mixed_ref, second_got_ref, mixed_got_ref,
    expanded_ref, mix_ref, expanded_got_ref, mix_got_ref, *refs, cutting,
):
    turned_ref, total_ref = refs[-2:]
    tokens, spread = expanded_ref.shape
    width = second_ref.shape[1]
    core = place_ref[2] % 2
    rows_each = cutting["rows_each"]

    def left(own_ref, got_ref):
        turned_ref[:, :tokens] = own_ref[...].astype(f32).T
        turned_ref[:, tokens:] = got_ref[...].astype(f32).T
        rows = [
            turned_ref[pl.ds(pl.multiple_of((2 * i + core) * rows_each, rows_each), rows_each), :]
            for i in range(width // (2 * rows_each))
        ]
        return jnp.concatenate(rows, axis=0).astype(bf16)

    second = left(second_ref, second_got_ref)
    for at in range(0, spread, WIDE):
        band = slice(at, at + WIDE)
        total_ref[:, band] = dot(
            second, jnp.concatenate([expanded_ref[:, band], expanded_got_ref[:, band]], axis=0)
        )
    mixed = left(mixed_ref, mixed_got_ref)
    total_ref[:, spread:] = dot(
        mixed, jnp.concatenate([mix_ref[...], mix_got_ref[...]], axis=0)
    )
    cut_out(refs[:-2], total_ref, place_ref, **cutting)


def outer_call(kernel, place, operands, rows, columns, bands, steps, size, axis, cut, scratch, name):
    rows_each = rows // size
    shape = (rows_each, columns // 2)
    low = (cut, shape[1]) if axis == 0 else (shape[0], cut)
    high = (shape[0] - cut, shape[1]) if axis == 0 else (shape[0], shape[1] - cut)
    pairs = (2,) * (len(steps) - 1)
    return pl.pallas_call(
        functools.partial(
            kernel,
            cutting=dict(bands=bands, steps=steps, rows_each=rows_each, axis=axis, cut=cut),
        ),
        out_shape=(
            jax.ShapeDtypeStruct((2,) + pairs + shape, bf16),
            jax.ShapeDtypeStruct(pairs + low, bf16),
            jax.ShapeDtypeStruct(pairs + high, bf16),
        ),
        in_specs=[pl.BlockSpec(memory_space=pltpu.SMEM)] + [vmem_spec()] * len(operands),
        out_specs=(vmem_spec(),) * 3,
        scratch_shapes=scratch + [pltpu.VMEM((rows // 2, columns), f32)],
        compiler_params=params(OUTER_MIB),
        cost_estimate=cost(2 << 30, 10 << 20),
        name=name,
    )(place, *operands)


def settle_kernel(place_ref, *refs):
    out = refs[-1]
    for k, ref in enumerate(refs[:-1]):
        out[place_ref[0] ^ k] = ref[...]


def settle_call(place, blocks):
    return pl.pallas_call(
        settle_kernel,
        out_shape=jax.ShapeDtypeStruct((len(blocks),) + blocks[0].shape, blocks[0].dtype),
        in_specs=[pl.BlockSpec(memory_space=pltpu.SMEM)] + [vmem_spec()] * len(blocks),
        out_specs=vmem_spec(),
        compiler_params=params(8),
        name="settle",
    )(place, *blocks)


def joined_slots_kernel(*refs, held):
    sources, outs = refs[:held], refs[held:]
    last = len(outs)
    for u, out in enumerate(outs):
        out[0] = sum(ref[u].astype(f32) for ref in sources).astype(bf16)
        out[1] = sum(ref[last].astype(f32) for ref in sources).astype(bf16)


def joined_slots_call(held, slots):
    _, rows, wide = held[0].shape
    return pl.pallas_call(
        functools.partial(joined_slots_kernel, held=len(held)),
        out_shape=(jax.ShapeDtypeStruct((2, rows, wide), bf16),) * slots,
        in_specs=[vmem_spec()] * len(held),
        out_specs=(vmem_spec(),) * slots,
        compiler_params=params(4),
        name="joined_slots",
    )(*held)


def heads_kernel(place_ref, *refs, groups, gains):
    joined_out, gains_out, held_ref = refs[-3:]
    pieces = refs[:-3]
    sums = []
    for u, ref in enumerate(pieces):
        held_ref[place_ref[1] ^ u] = ref[0].astype(f32)
        sums.append(ref[1].astype(f32))
    piece = pieces[0].shape[2] // 3
    for part in range(3):
        for g in range(groups):
            start = (part * groups + g) * piece
            joined_out[:, start : start + piece] = held_ref[
                g, :, part * piece : (part + 1) * piece
            ]
    while len(sums) > 1:
        sums = [sums[i] + sums[i + 1] for i in range(0, len(sums), 2)]
    wide = 3 * piece
    for r in range(-(-gains // wide)):
        end = min((r + 1) * wide, gains)
        gains_out[:, r * wide : end] = sums[0][r : r + 1, : end - r * wide]


def heads_call(place, blocks, width, gains):
    _, rows, wide = blocks[0].shape
    return pl.pallas_call(
        functools.partial(heads_kernel, groups=3 * width // wide, gains=gains),
        out_shape=(
            jax.ShapeDtypeStruct((rows, 3 * width), f32),
            jax.ShapeDtypeStruct((1, gains), f32),
        ),
        in_specs=[pl.BlockSpec(memory_space=pltpu.SMEM)] + [vmem_spec()] * len(blocks),
        out_specs=(vmem_spec(),) * 2,
        scratch_shapes=[pltpu.VMEM((len(blocks), rows, wide), f32)],
        compiler_params=params(8),
        name="heads_side_by_side",
    )(place, *blocks)


def input_kernel(*refs, planes, parts):
    inputs = refs[:planes]
    refs = refs[planes:]
    grad_ref, gain_ref = refs[:2]
    grad = sum(ref[at].astype(f32) for ref, at in zip(refs[2 : 2 + len(parts)], parts))
    outs = refs[2 + len(parts) :]
    normal, rate = normalized(
        jnp.concatenate([block[...] for block in inputs], axis=0).astype(f32)
    )
    value = grad_ref[...] + norm_back(normal, rate, grad * gain_ref[...])
    seg = value.shape[0] // planes
    for k in range(planes):
        outs[k][...] = value[k * seg : (k + 1) * seg, :].astype(bf16)


def input_call(inputs, grad_middle, gain, held, parts):
    planes = len(inputs)
    tokens, width = grad_middle.shape
    return pl.pallas_call(
        functools.partial(input_kernel, planes=planes, parts=parts),
        out_shape=(jax.ShapeDtypeStruct((tokens // planes, width), bf16),) * planes,
        in_specs=[vmem_spec()] * (2 + planes + len(held)),
        out_specs=(vmem_spec(),) * planes,
        compiler_params=params(16),
        name="input_back",
    )(*inputs, grad_middle, gain, *held)


def swap(value, axis, bits):
    size = lax.axis_size(axis)
    return lax.ppermute(value, axis, [(i, i ^ bits) for i in range(size)])


def pick(value, index, axis=0):
    return lax.dynamic_index_in_dim(value, index, axis, keepdims=False)


def in_hbm(*values):
    return [pltpu.with_memory_space_constraint(value, pltpu.HBM) for value in values]


def bits_of(size):
    return size.bit_length() - 1


def sums_kernel(*refs, listed, together):
    outs = refs[-1:] if together else refs[-len(listed) :]
    start = 0
    for i, terms in enumerate(listed):
        value = sum(refs[j][at].astype(f32) for j, at in terms).astype(bf16)
        if together:
            end = start + value.shape[together]
            outs[0][(..., slice(start, end)) + (slice(None),) * (-1 - together)] = value
            start = end
        else:
            outs[i][...] = value


def sums_call(sums, name, together=0):
    arrays, listed, shapes = [], [], []
    for terms in sums:
        entry = []
        for array, at in terms:
            where = [i for i, held in enumerate(arrays) if held is array]
            if not where:
                arrays.append(array)
                where = [len(arrays) - 1]
            entry.append((where[0], at))
        listed.append(entry)
        shapes.append(jax.eval_shape(lambda v, at=terms[0][1]: v[at], terms[0][0]).shape)
    if together:
        shape = list(shapes[0])
        shape[together] = sum(shape[together] for shape in shapes)
        shapes = [tuple(shape)]
    outs = pl.pallas_call(
        functools.partial(sums_kernel, listed=listed, together=together),
        out_shape=tuple(jax.ShapeDtypeStruct(shape, bf16) for shape in shapes),
        in_specs=[vmem_spec()] * len(arrays),
        out_specs=(vmem_spec(),) * len(shapes),
        compiler_params=params(4),
        name=name,
    )(*arrays)
    return outs[0] if together or len(shapes) == 1 else outs


class Halves:
    def __init__(self):
        self.entries = []
        self.chosen = {}

    def hold(self, array, names, bands=()):
        self.entries.append((array, names, dict(bands)))

    def terms(self, choice=()):
        chosen = dict(self.chosen)
        chosen.update(choice)
        return [
            (
                array,
                tuple(chosen[n] if n in chosen else bands.get(n, slice(None)) for n in names),
            )
            for array, names, bands in self.entries
        ]

    def receive(self, name, array, bands=()):
        self.chosen[name] = 0
        names = [n for n in self.entries[0][1] if n not in self.chosen]
        self.hold(array, names, bands)


def sides_kernel(place_ref, own_ref, other_ref, *outs):
    first = place_ref[3] == 0
    own, other = own_ref[...].astype(f32), other_ref[...].astype(f32)
    low, high = jnp.where(first, own, other), jnp.where(first, other, own)
    start = 0
    for out in outs:
        wide = out.shape[1] // 2
        out[:, :wide] = low[:, start : start + wide]
        out[:, wide:] = high[:, start : start + wide]
        start += wide


def sides_call(place, own, other, widths, name):
    rows = own.shape[0]
    return pl.pallas_call(
        sides_kernel,
        out_shape=tuple(jax.ShapeDtypeStruct((rows, wide), f32) for wide in widths),
        in_specs=[pl.BlockSpec(memory_space=pltpu.SMEM)] + [vmem_spec()] * 2,
        out_specs=(vmem_spec(),) * len(widths),
        compiler_params=params(8),
        name=name,
    )(place, own, other)


def per_device(
    layer_input, cotangent, doc_lengths, joined_weight, merge_weight, expand_weight,
    shrink_weight, first_gain, mixed_gain, second_gain, hidden_gain,
):
    _, planes, seg, width = layer_input.shape
    size = lax.axis_size("blk")
    slots = size // planes
    batches = lax.axis_size("batch")
    rank = lax.axis_index("blk")
    group_rank = lax.axis_index("batch")
    plane = rank // slots
    slot = rank % slots
    head_count = width // HEAD
    heads = -(-head_count // slots)
    groups = head_count // heads
    piece = heads * HEAD
    tokens = planes * seg
    length = slots * tokens
    side = group_rank % 2
    place = jnp.stack([plane, slot, rank, side]).astype(jnp.int32)

    def to_planes(blocks):
        return [pick(blocks, plane)] + [
            swap(pick(blocks, plane ^ k), "blk", k * slots) for k in range(1, planes)
        ]

    def all_slots(value):
        held = {0: value}
        for bit in reversed(range(bits_of(slots))):
            held.update({u | 1 << bit: swap(v, "blk", 1 << bit) for u, v in held.items()})
        return [held[u] for u in range(slots)]

    def over_slots(blocks):
        return [blocks[0]] + [swap(blocks[u], "blk", u) for u in range(1, slots)]

    spread = expand_weight.shape[1]
    first_arrived = to_planes(layer_input[0])
    own_start = jnp.minimum(slot, groups - 1) * piece
    own_weight = jnp.concatenate(
        [
            lax.dynamic_slice_in_dim(joined_weight, part * width + own_start, piece, 1)
            for part in range(3)
        ],
        axis=1,
    )
    lengths = doc_lengths[0]
    gain_row = first_gain.reshape(1, width)
    mixed_gain = mixed_gain.reshape(groups, 1, piece)
    second_gain = second_gain.reshape(1, width)
    hidden_gain = hidden_gain.reshape(1, spread)
    (
        first_arrived[-1], place, lengths, gain_row, mixed_gain, second_gain, hidden_gain, own_weight,
    ) = lax.optimization_barrier(
        (
            first_arrived[-1], place, lengths, gain_row, mixed_gain, second_gain, hidden_gain,
            own_weight,
        )
    )
    pieces = [all_slots(block) for block in first_arrived]
    (first, joined, factor), sent, shares = forward_call(
        place, lengths, gain_row, own_weight, pieces
    )
    sent, cotangent = lax.optimization_barrier((sent, cotangent))
    cotangent_blocks = to_planes(cotangent[0])
    (
        mixed, middle, second, hidden, hidden_give, normal, slope, held, mixed_rate, hidden_rate,
    ) = widen_call(
        place, over_slots(sent), first_arrived, mixed_gain, second_gain, hidden_gain, merge_weight,
        expand_weight,
    )
    hidden_give, cotangent_blocks = lax.optimization_barrier((hidden_give, cotangent_blocks))
    branch = branch_call(place, lengths, cotangent_blocks, slots)

    row_bits = list(range(1, bits_of(slots)))
    plane_bits = list(range(bits_of(slots), bits_of(size)))
    names = ["side"] + row_bits + plane_bits + ["rows", "columns"]
    steps = [0] + row_bits + plane_bits
    orders = (["side"] + row_bits, row_bits + ["side"])
    stages = len(orders[0])

    def cross(name, value):
        return swap(value, "batch", 1) if name == "side" else swap(value, "blk", 1 << name)

    def chains(axis, cut, whole):
        pair = [Halves(), Halves()]
        for chain, band in zip(pair, (slice(0, cut), slice(cut, None))):
            chain.hold(whole, names, {axis: band})
        return pair

    def sends(pair, at):
        return sums_call(
            [chain.terms({order[at]: 1}) for chain, order in zip(pair, orders)], "next_halves"
        )

    def crossed(at, values):
        return [cross(order[at], value) for order, value in zip(orders, values)]

    def arrive(pair, at, values):
        for chain, order, value in zip(pair, orders, values):
            chain.receive(order[at], value)

    def plane_depart(pair, bit, axis):
        together = -2 if axis == "rows" else -1
        return cross(
            bit, sums_call([chain.terms({bit: 1}) for chain in pair], "plane_halves", together)
        )

    def plane_arrive(pair, bit, axis, both):
        cut = pair[0].entries[0][2][axis].stop
        for chain, band in zip(pair, (slice(0, cut), slice(cut, None))):
            chain.receive(bit, both, {axis: band})

    def closed(pair, axis):
        together = -2 if axis == "rows" else -1
        value = sums_call([chain.terms() for chain in pair], "last_halves", together)
        for bit in range(1, bits_of(batches)):
            value = sums_call([[(value, ...), (swap(value, "batch", 1 << bit), ...)]], "groups")
        return value, swap(value, "batch", 1)

    cut = spread // size // 2
    shrink_whole, *shrink_firsts = outer_call(
        shrink_kernel, place,
        [hidden, branch, swap(hidden_give, "blk", 1), swap(branch, "blk", 1)],
        spread, width, ((0, width // 2),), steps, size, 0, cut, [], "shrink_outer",
    )
    shrink_sent = crossed(0, shrink_firsts)
    second_got, mixed_got = swap(second, "blk", 1), swap(mixed, "blk", 1)
    (expanded, mix, grad_middle, parts), away, results = turn_call(
        place, branch, normal, slope, middle, held, mixed_rate, hidden_rate,
        mixed_gain, second_gain, hidden_gain, merge_weight, shrink_weight, expand_weight, planes,
    )
    shrink_sent, second_got, mixed_got, expanded, mix = lax.optimization_barrier(
        (shrink_sent, second_got, mixed_got, expanded, mix)
    )
    shrink_chains = chains("rows", cut, shrink_whole)
    arrive(shrink_chains, 0, shrink_sent)

    returned = over_slots(away)
    expanded_got, mix_got = swap(expanded, "blk", 1), swap(mix, "blk", 1)
    returned, expanded_got, mix_got = lax.optimization_barrier((returned, expanded_got, mix_got))
    cut = ((spread + width) // 4 + 127) // 128 * 128
    expand_whole, *expand_firsts = outer_call(
        expand_kernel, place,
        [second, mixed, second_got, mixed_got, expanded, mix, expanded_got, mix_got],
        width, spread + width, ((0, spread // 2), (spread, width // 2)), steps, size, 1, cut,
        [pltpu.VMEM((width, 2 * tokens), f32)], "expand_outer",
    )
    for at in range(1, stages):
        shrink_sent = crossed(at, sends(shrink_chains, at))
        if at < stages - 1:
            arrive(shrink_chains, at, shrink_sent)
    expand_firsts, results = lax.optimization_barrier((expand_firsts, results))
    result_blocks = [results[0]] + [
        swap(results[k], "blk", k * slots) for k in range(1, planes)
    ]
    returned, expand_firsts, shrink_sent = lax.optimization_barrier(
        (returned, expand_firsts, shrink_sent)
    )
    arrive(shrink_chains, stages - 1, shrink_sent)
    expand_sent = crossed(0, expand_firsts)
    shrink_both = plane_depart(shrink_chains, plane_bits[0], "rows")
    joined_keep, joined_give, branch_keep, branch_give = backward_call(
        place, first, joined, factor, own_weight, gain_row, parts, returned, shares, planes
    )
    (
        joined_give, branch_give, shrink_both, expand_sent, result_blocks,
    ) = lax.optimization_barrier(
        (joined_give, branch_give, shrink_both, expand_sent, result_blocks)
    )
    plane_arrive(shrink_chains, plane_bits[0], "rows", shrink_both)
    expand_chains = chains("columns", cut, expand_whole)
    arrive(expand_chains, 0, expand_sent)

    joined_got = swap(joined_give, "blk", 1 << plane_bits[0])
    branch_got = swap(branch_give, "blk", 1)
    for at in range(1, stages):
        expand_sent = crossed(at, sends(expand_chains, at))
        if at < stages - 1:
            arrive(expand_chains, at, expand_sent)
    for bit in plane_bits[1:]:
        shrink_both = plane_depart(shrink_chains, bit, "rows")
        if bit != plane_bits[-1]:
            plane_arrive(shrink_chains, bit, "rows", shrink_both)
    branch_held, prefixes = [branch_keep, branch_got], [(), ()]
    for bit in row_bits:
        give = sums_call(
            [[(v, p + (1,)) for v, p in zip(branch_held, prefixes)]], "branch_halves"
        )
        prefixes = [p + (0,) for p in prefixes] + [()]
        branch_held.append(swap(give, "blk", 1 << bit))
    joined_got, branch_held[-1], expand_sent, shrink_both = lax.optimization_barrier(
        (joined_got, branch_held[-1], expand_sent, shrink_both)
    )
    arrive(expand_chains, stages - 1, expand_sent)
    plane_arrive(shrink_chains, plane_bits[-1], "rows", shrink_both)

    expand_both = plane_depart(expand_chains, plane_bits[0], "columns")
    joined_terms = [(joined_keep, 0), (joined_got, 0)]
    blocks = planes * slots // 2
    gain_terms = [(joined_give, blocks), (joined_got, blocks)]
    for bit in plane_bits[1:]:
        blocks //= 2
        joined_give = sums_call(
            [
                [(v, slice(start + blocks, start + 2 * blocks)) for v, start in joined_terms],
                [(v, slice(at, at + 1)) for v, at in gain_terms],
            ],
            "joined_halves", -3,
        )
        joined_got = swap(joined_give, "blk", 1 << bit)
        joined_terms.append((joined_got, 0))
        gain_terms = [(joined_give, blocks), (joined_got, blocks)]
    input_blocks = input_call(
        first_arrived, grad_middle, gain_row, branch_held, prefixes
    )
    input_blocks = [input_blocks[0]] + [
        swap(input_blocks[k], "blk", k * slots) for k in range(1, planes)
    ]
    joined_last = sums_call(
        [
            [(v, slice(start, start + slots)) for v, start in joined_terms],
            [(v, slice(at, at + 1)) for v, at in gain_terms],
        ],
        "joined_last", -3,
    )
    held = [joined_last]
    for bit in range(bits_of(batches)):
        if len(held) > 1:
            held = [sums_call([[(v, ...) for v in held]], "joined_groups")]
        held.append(swap(held[0], "batch", 1 << bit))
    joined_sent = joined_slots_call(held, slots)
    joined_grad, gain_grads = heads_call(
        place,
        [joined_sent[0]] + [swap(joined_sent[u], "blk", u) for u in range(1, slots)],
        width, 3 * width + spread,
    )
    shrink_grad, = sides_call(place, *closed(shrink_chains, "rows"), (width,), "shrink_sides")
    plane_arrive(expand_chains, plane_bits[0], "columns", expand_both)
    for bit in plane_bits[1:]:
        expand_both = plane_depart(expand_chains, bit, "columns")
        plane_arrive(expand_chains, bit, "columns", expand_both)
    expand_grad, merge_grad = sides_call(
        place, *closed(expand_chains, "columns"), (spread, width), "expand_sides"
    )
    layer_result = settle_call(place, result_blocks).reshape(layer_input.shape)
    input_grad = settle_call(place, input_blocks).reshape(layer_input.shape)
    gain_grads = gain_grads[0]
    return (
        layer_result, input_grad, joined_grad, merge_grad, expand_grad,
        shrink_grad, gain_grads[:width], gain_grads[width : 2 * width],
        gain_grads[2 * width : 3 * width], gain_grads[3 * width :],
    )


def solution(mesh):
    rows = P("batch", None, "blk", None)
    return jax.shard_map(
        per_device,
        mesh=mesh,
        in_specs=(rows, rows, P("batch", None, None)) + (P(),) * 8,
        out_specs=(rows, rows) + (P("blk", None),) * 4 + (P(),) * 4,
        check_vma=False,
    )
```

```python
import functools

import jax
import jax.numpy as jnp
from jax import lax
from jax.experimental import pallas as pl
from jax.experimental.pallas import tpu as pltpu
from jax.sharding import PartitionSpec as P

HEAD = 64
TILE = 256
WIDE = 512
BAND = 384
FORWARD_MIB = 14
BACKWARD_MIB = 14
WIDEN_MIB = 11
TURN_MIB = 11
OUTER_MIB = 16
big_negative = -1e30
norm_epsilon = 1e-05

f32 = jnp.float32
bf16 = jnp.bfloat16


def dot(left, right):
    return jnp.dot(left, right, preferred_element_type=f32)


def dot_nt(left, right):
    return lax.dot_general(left, right, (((1,), (1,)), ((), ())), preferred_element_type=f32)


def dot_tn(left, right):
    return lax.dot_general(left, right, (((0,), (0,)), ((), ())), preferred_element_type=f32)


def normalized(values):
    centred = values - jnp.mean(values, axis=-1, keepdims=True)
    rate = lax.rsqrt(jnp.mean(centred * centred, axis=-1, keepdims=True) + norm_epsilon)
    return centred * rate, rate


def norm_back(normal, rate, weighted):
    return rate * (
        weighted
        - jnp.mean(weighted, axis=-1, keepdims=True)
        - normal * jnp.mean(weighted * normal, axis=-1, keepdims=True)
    )


def vmem_spec():
    return pl.BlockSpec(memory_space=pltpu.VMEM)


def hbm_spec():
    return pl.BlockSpec(memory_space=pltpu.HBM)


def params(mebibytes):
    return pltpu.CompilerParams(vmem_limit_bytes=mebibytes * 1024 * 1024)


def cost(flops, moved):
    return pl.CostEstimate(flops=flops, bytes_accessed=moved, transcendentals=0)


def document_ends(lengths_ref, plane):
    ends, end = [], jnp.int32(0)
    for d in range(lengths_ref.shape[1]):
        end = end + lengths_ref[plane, d]
        ends.append(end)
    return ends


def columns_at(step):
    return pl.ds(pl.multiple_of(step * WIDE, WIDE), WIDE)


def codes(steps):
    listed = [((), 0)]
    for bit in steps:
        listed = [(at + (b,), code | (b << bit)) for at, code in listed for b in (0, 1)]
    return listed


def forward_kernel(*refs, planes, slots, seg, heads):
    place_ref, lengths_ref, gain_ref, weight_ref = refs[:4]
    pieces = refs[4 : 4 + slots * planes]
    refs = refs[4 + slots * planes :]
    length = planes * slots * seg
    tiles = length // TILE
    first_ref, joined_ref, factor_ref = refs[:3]
    sent = refs[3 : 3 + slots]
    shares = refs[3 + slots : 3 + slots + tiles]
    rows_ref, attention_ref = refs[3 + slots + tiles :]
    plane, slot = place_ref[0], place_ref[1]
    for u in range(slots):
        for k in range(planes):
            offset = ((plane ^ k) * slots + (slot ^ u)) * seg
            rows_ref[pl.ds(pl.multiple_of(offset, seg), seg), :] = pieces[k * slots + u][...]
    width = heads * HEAD

    def project(tile, carry):
        rows = pl.ds(pl.multiple_of(tile * TILE, TILE), TILE)
        normal, _ = normalized(rows_ref[rows, :].astype(f32))
        first = (normal * gain_ref[...]).astype(bf16)
        first_ref[rows, :] = first
        joined = dot(first, weight_ref[...]).astype(bf16)
        for part in range(3):
            for h in range(heads):
                column = part * width + h * HEAD
                value = joined[:, column : column + HEAD]
                if part == 0:
                    value = value * jnp.asarray(0.125, bf16)
                joined_ref[part * heads + h, rows, :] = value
        return carry

    lax.fori_loop(0, tiles, project, 0, unroll=True)
    ends = document_ends(lengths_ref, plane)
    for q in reversed(range(tiles)):
        rows = slice(q * TILE, (q + 1) * TILE)
        reach = (q + 1) * TILE
        places = q * TILE + lax.broadcasted_iota(jnp.int32, (TILE, 1), 0)
        start = jnp.zeros((TILE, 1), jnp.int32)
        for end in ends:
            start = jnp.maximum(start, jnp.where(places >= end, end, 0))
        query_pos = q * TILE + lax.broadcasted_iota(jnp.int32, (TILE, reach), 0)
        key_pos = lax.broadcasted_iota(jnp.int32, (TILE, reach), 1)
        allowed = (key_pos <= query_pos) & (key_pos >= start)
        for h in range(heads):
            scores = dot_nt(joined_ref[h, rows, :], joined_ref[heads + h, :reach, :])
            scores = jnp.where(allowed, scores, big_negative)
            peak = jnp.max(scores, axis=-1, keepdims=True)
            raised = jnp.exp(scores - peak)
            total = jnp.sum(raised, axis=-1, keepdims=True)
            share = raised.astype(bf16)
            shares[q][h] = share
            factor = 1.0 / total
            factor_ref[rows, h : h + 1] = factor
            attention_ref[h, rows, :] = factor * dot(
                share, joined_ref[2 * heads + h, :reach, :]
            )
    half = planes // 2
    for u in range(slots):
        for k in range(planes):
            offset = ((plane ^ k) * slots + (slot ^ u)) * seg
            rows = slice(k % half * seg, (k % half + 1) * seg)
            for h in range(heads):
                part = attention_ref[h, pl.ds(pl.multiple_of(offset, seg), seg), :]
                column = k // half * width + h * HEAD
                sent[u][rows, column : column + HEAD] = part.astype(bf16)


def forward_call(place, lengths, gain, weight, pieces):
    planes, slots = len(pieces), len(pieces[0])
    seg, width = pieces[0][0].shape
    length = planes * slots * seg
    heads = weight.shape[1] // (3 * HEAD)
    kernel = functools.partial(forward_kernel, planes=planes, slots=slots, seg=seg, heads=heads)
    packed = jax.ShapeDtypeStruct((planes * seg // 2, 2 * heads * HEAD), bf16)
    tiled = [(heads, TILE, reach) for reach in range(TILE, length + 1, TILE)]
    outs = pl.pallas_call(
        kernel,
        out_shape=(
            pltpu.VMEM((length, width), bf16),
            pltpu.VMEM((3 * heads, length, HEAD), bf16),
            pltpu.VMEM((length, heads), f32),
        )
        + (packed,) * slots
        + tuple(pltpu.VMEM(shape, bf16) for shape in tiled),
        in_specs=[pl.BlockSpec(memory_space=pltpu.SMEM)] * 2
        + [vmem_spec()] * (2 + slots * planes),
        out_specs=(vmem_spec(),) * (3 + slots + len(tiled)),
        scratch_shapes=[
            pltpu.VMEM((length, width), bf16),
            pltpu.VMEM((heads, length, HEAD), f32),
        ],
        compiler_params=params(FORWARD_MIB * length // 1024),
        cost_estimate=cost(8 << 30, 8 << 20),
        name="attention_forward",
    )(place, lengths, gain, weight, *[block for blocks in pieces for block in blocks])
    return outs[:3], outs[3 : 3 + slots], outs[3 + slots :]


def backward_kernel(*refs, planes, slots, seg, heads, rows_each):
    place_ref, first_ref, joined_ref, factor_ref, weight_ref, gain_ref, parts_ref = refs[:7]
    pieces = refs[7 : 7 + slots]
    length = planes * slots * seg
    tiles = length // TILE
    refs = refs[7 + slots :]
    shares = refs[:tiles]
    joined_keep, joined_give, branch_keep, branch_give = refs[tiles : tiles + 4]
    grad_ref, arrived_ref, key_ref, value_ref, total_ref, outer_ref, row_ref = refs[tiles + 4 :]
    plane, slot = place_ref[0], place_ref[1]
    width = heads * HEAD
    half = planes // 2
    for u in range(slots):
        for k in range(planes):
            offset = ((plane ^ k) * slots + (slot ^ u)) * seg
            column = k // half * width
            arrived_ref[pl.ds(pl.multiple_of(offset, seg), seg), :] = pieces[u][
                k % half * seg : (k % half + 1) * seg, column : column + width
            ]
    for h in range(heads):
        for q in reversed(range(tiles)):
            rows = slice(q * TILE, (q + 1) * TILE)
            reach = (q + 1) * TILE
            factor = factor_ref[rows, h : h + 1]
            grad = (arrived_ref[rows, h * HEAD : (h + 1) * HEAD].astype(f32) * factor).astype(bf16)
            share = shares[q][h]
            product = share.astype(f32) * dot_nt(grad, joined_ref[2 * heads + h, :reach, :])
            inner = jnp.sum(product, axis=-1, keepdims=True)
            grad_scores = (product - share.astype(f32) * (inner * factor)).astype(bf16)
            query_grad = dot(grad_scores, joined_ref[heads + h, :reach, :]) * 0.125
            grad_ref[rows, h * HEAD : (h + 1) * HEAD] = query_grad.astype(bf16)
            key_add = dot_tn(joined_ref[h, rows, :], grad_scores)
            value_add = dot_tn(grad, share)
            if q == tiles - 1:
                key_ref[...] = key_add
                value_ref[...] = value_add
            else:
                key_ref[:, :reach] += key_add
                value_ref[:, :reach] += value_add
        for part, source in ((1, key_ref), (2, value_ref)):
            column = part * width + h * HEAD
            for q in range(tiles):
                rows = slice(q * TILE, (q + 1) * TILE)
                grad_ref[rows, column : column + HEAD] = source[:, rows].T.astype(bf16)

    def back(tile, carry):
        rows = pl.ds(pl.multiple_of(tile * TILE, TILE), TILE)
        total_ref[rows, :] = dot_nt(grad_ref[rows, :], weight_ref[...])
        return carry

    lax.fori_loop(0, tiles, back, 0, unroll=True)
    for at, code in codes(range(1, bits_of(slots))):
        for out, u in ((branch_keep, code), (branch_give, code | 1)):
            for k in range(planes):
                offset = ((plane ^ k) * slots + (slot ^ u)) * seg
                out[at + (slice(k * seg, (k + 1) * seg),)] = total_ref[
                    pl.ds(pl.multiple_of(offset, seg), seg), :
                ].astype(bf16)
    model = first_ref.shape[1]
    for d in range(0, model, TILE):
        outer = dot_tn(first_ref[:, d : d + TILE], grad_ref[...])
        outer_ref[d : d + TILE, :] = outer
        scaled = jnp.sum(outer * weight_ref[d : d + TILE, :].astype(f32), axis=-1, keepdims=True)
        scaled = jnp.broadcast_to(scaled, (TILE, 128)).T
        row_ref[:, d : d + TILE] = scaled[:1] / gain_ref[:, d : d + TILE]
    wide = 3 * width
    row_ref[:, model : model + parts_ref.shape[1]] = parts_ref[...]
    gains = model + parts_ref.shape[1]
    half = planes * slots // 2
    at = 0
    for _, code in codes(range(bits_of(planes))):
        for u in range(slots):
            offset = ((plane ^ code) * slots + (slot ^ u)) * rows_each
            out = joined_keep if at < half else joined_give
            out[at % half] = outer_ref[
                pl.ds(pl.multiple_of(offset, rows_each), rows_each), :
            ].astype(bf16)
            at += 1
    outer_ref[:rows_each, :] = jnp.zeros((rows_each, wide), f32)
    for r in range(-(-gains // wide)):
        end = min((r + 1) * wide, gains)
        outer_ref[r : r + 1, : end - r * wide] = row_ref[:, r * wide : end]
    joined_give[half] = outer_ref[:rows_each, :].astype(bf16)


def backward_call(
    place, first, joined, factor, weight, gain, parts, pieces, shares, planes
):
    slots = len(pieces)
    tokens = pieces[0].shape[0] * 2
    heads, length = joined.shape[0] // 3, joined.shape[1]
    width = weight.shape[0]
    rows_each = width // (planes * slots)
    kernel = functools.partial(
        backward_kernel, planes=planes, slots=slots, seg=tokens // planes, heads=heads,
        rows_each=rows_each,
    )
    pairs = (2,) * (bits_of(slots) - 1)
    wide = 3 * heads * HEAD
    row = -(-(width + parts.shape[1]) // 128) * 128
    return pl.pallas_call(
        kernel,
        out_shape=(
            jax.ShapeDtypeStruct((planes * slots // 2, rows_each, wide), bf16),
            jax.ShapeDtypeStruct((planes * slots // 2 + 1, rows_each, wide), bf16),
            jax.ShapeDtypeStruct(pairs + (tokens, width), bf16),
            jax.ShapeDtypeStruct(pairs + (tokens, width), bf16),
        ),
        in_specs=[pl.BlockSpec(memory_space=pltpu.SMEM)]
        + [vmem_spec()] * (6 + slots + len(shares)),
        out_specs=(vmem_spec(),) * 4,
        scratch_shapes=[
            pltpu.VMEM((length, wide), bf16),
            pltpu.VMEM((length, heads * HEAD), bf16),
            pltpu.VMEM((HEAD, length), f32),
            pltpu.VMEM((HEAD, length), f32),
            pltpu.VMEM((length, width), f32),
            pltpu.VMEM((width, wide), f32),
            pltpu.VMEM((1, row), f32),
        ],
        compiler_params=params(BACKWARD_MIB * length // 1024),
        cost_estimate=cost(10 << 30, 10 << 20),
        name="attention_backward",
    )(place, first, joined, factor, weight, gain, parts, *pieces, *shares)


def widen_kernel(*refs, slots, planes, groups, width, spread, block):
    place_ref = refs[0]
    pieces = refs[1 : 1 + slots]
    inputs = refs[1 + slots : 1 + slots + planes]
    refs = refs[1 + slots + planes :]
    mixed_gain_ref, second_gain_ref, hidden_gain_ref, merge_ref, expand_ref = refs[:5]
    (
        mixed_ref, middle_ref, second_ref, hidden_ref, hidden_give_ref, normal_ref, slope_ref,
        held_ref, mixed_rate_ref, hidden_rate_ref,
    ) = refs[5:15]
    (gelu_ref,) = refs[15:]
    steps = spread // WIDE

    slot = place_ref[1]
    piece = width // groups
    tokens = planes * inputs[0].shape[0]
    half = tokens // 2
    for u in range(slots):
        for side in range(2):
            held_ref[slot ^ u, side * half : (side + 1) * half, :] = pieces[u][
                :, side * piece : (side + 1) * piece
            ].astype(f32)
    mean = sum(jnp.sum(held_ref[g], axis=-1, keepdims=True) for g in range(groups)) * (1.0 / width)
    square = 0.0
    for g in range(groups):
        centred = held_ref[g] - mean
        held_ref[g] = centred
        square = square + jnp.sum(centred * centred, axis=-1, keepdims=True)
    mixed_rate = lax.rsqrt(square * (1.0 / width) + norm_epsilon)
    mixed_rate_ref[...] = mixed_rate
    middle = jnp.concatenate([block[...] for block in inputs], axis=0).astype(f32)
    for g in range(groups):
        normal = held_ref[g] * mixed_rate
        held_ref[g] = normal
        mixed = (normal * mixed_gain_ref[g]).astype(bf16)
        mixed_ref[:, g * piece : (g + 1) * piece] = mixed
        middle = middle + dot(mixed, merge_ref[g * piece : (g + 1) * piece, :])
    middle_ref[...] = middle
    second_normal, _ = normalized(middle)
    second = (second_normal * second_gain_ref[...]).astype(bf16)
    second_ref[...] = second
    total = jnp.zeros((tokens, 1), f32)

    def widen(step, total):
        at = columns_at(step)
        value = dot(second, expand_ref[:, at])
        share = 0.5 * (1.0 + lax.erf(value * 0.7071067811865476))
        gelu = value * share
        gelu_ref[:, at] = gelu
        slope = share + value * (0.3989422804014327 * jnp.exp(-0.5 * value * value))
        slope_ref[:, at] = slope.astype(bf16)
        return total + jnp.sum(gelu, axis=-1, keepdims=True)

    total = lax.fori_loop(0, steps, widen, total)
    mean = total * (1.0 / spread)
    total = jnp.zeros((tokens, 1), f32)
    for step in range(steps):
        centred = gelu_ref[:, step * WIDE : (step + 1) * WIDE] - mean
        total = total + jnp.sum(centred * centred, axis=-1, keepdims=True)
    rate = lax.rsqrt(total * (1.0 / spread) + norm_epsilon)
    hidden_rate_ref[...] = rate
    core = slot % 2
    for at in range(0, spread, 2 * BAND):
        ours, theirs = [], []
        for start in range(at, at + 2 * BAND, 2 * block):
            low = slice(start, start + block)
            high = slice(start + block, start + 2 * block)
            parts = []
            for part in (low, high):
                normal = (gelu_ref[:, part] - mean) * rate
                normal_ref[:, part] = normal.astype(bf16)
                parts.append((normal * hidden_gain_ref[:, part]).astype(bf16))
            ours.append(parts[0])
            theirs.append(parts[1])
        even, odd = jnp.concatenate(ours, axis=1), jnp.concatenate(theirs, axis=1)
        half_at = slice(at // 2, at // 2 + BAND)
        hidden_ref[:, half_at] = jnp.where(core == 0, even, odd)
        hidden_give_ref[:, half_at] = jnp.where(core == 0, odd, even)


def widen_call(
    place, pieces, inputs, mixed_gain, second_gain, hidden_gain, merge, expand
):
    slots = len(pieces)
    tokens = len(inputs) * inputs[0].shape[0]
    piece = pieces[0].shape[1] // 2
    width, spread = expand.shape
    groups = width // piece

    def low(*shape):
        return jax.ShapeDtypeStruct(shape, bf16)

    def full(*shape):
        return jax.ShapeDtypeStruct(shape, f32)

    return pl.pallas_call(
        functools.partial(
            widen_kernel, slots=slots, planes=len(inputs), groups=groups, width=width,
            spread=spread, block=spread // (slots * len(inputs)),
        ),
        out_shape=(
            low(tokens, width),
            full(tokens, width),
            low(tokens, width),
            low(tokens, spread // 2),
            low(tokens, spread // 2),
            low(tokens, spread),
            low(tokens, spread),
            full(slots, tokens, piece),
            full(tokens, 1),
            full(tokens, 1),
        ),
        in_specs=[pl.BlockSpec(memory_space=pltpu.SMEM)]
        + [vmem_spec()] * (5 + slots + len(inputs)),
        out_specs=(vmem_spec(),) * 10,
        scratch_shapes=[
            pltpu.VMEM((tokens, spread), f32),
        ],
        compiler_params=params(WIDEN_MIB),
        cost_estimate=cost(6 << 30, 6 << 20),
        name="widen",
    )(
        place, *pieces, *inputs, mixed_gain, second_gain, hidden_gain, merge, expand,
    )


def branch_kernel(place_ref, lengths_ref, *refs, slots):
    blocks, branch_ref = refs[:-1], refs[-1]
    seg = blocks[0].shape[0]
    limit = document_ends(lengths_ref, place_ref[0])[-1]
    for k, block in enumerate(blocks):
        offset = ((place_ref[0] ^ k) * slots + place_ref[1]) * seg
        valid = offset + lax.broadcasted_iota(jnp.int32, (seg, 1), 0) < limit
        branch_ref[k * seg : (k + 1) * seg, :] = jnp.where(
            valid, block[...], jnp.zeros((), bf16)
        )


def branch_call(place, lengths, blocks, slots):
    seg, width = blocks[0].shape
    return pl.pallas_call(
        functools.partial(branch_kernel, slots=slots),
        out_shape=jax.ShapeDtypeStruct((len(blocks) * seg, width), bf16),
        in_specs=[pl.BlockSpec(memory_space=pltpu.SMEM)] * 2 + [vmem_spec()] * len(blocks),
        out_specs=vmem_spec(),
        compiler_params=params(4),
        name="branch",
    )(place, lengths, *blocks)


def turn_kernel(*refs, slots, planes, groups, width, spread):
    (
        place_ref, branch_ref, normal_ref, slope_ref, middle_ref, held_ref,
        mixed_rate_ref, hidden_rate_ref,
        mixed_gain_ref, second_gain_ref, hidden_gain_ref, merge_ref, shrink_ref, expand_ref,
    ) = refs[:14]
    expanded_ref, mix_ref, grad_ref, parts_ref = refs[14:18]
    away = refs[18 : 18 + slots]
    results = refs[18 + slots : 18 + slots + planes]
    weighted_ref, sent_ref = refs[18 + slots + planes :]
    steps = spread // WIDE

    slot = place_ref[1]
    piece = width // groups
    tokens = middle_ref.shape[0]
    half = tokens // 2
    branch = branch_ref[...]
    result = middle_ref[...]
    weighted_sum = jnp.zeros((tokens, 1), f32)
    inner_sum = jnp.zeros((tokens, 1), f32)
    for step in range(steps):
        at = slice(step * WIDE, (step + 1) * WIDE)
        normal = normal_ref[:, at].astype(f32)
        hidden = (normal * hidden_gain_ref[:, at]).astype(bf16)
        result = result + dot(hidden, shrink_ref[at, :])
        grad_hidden = dot_nt(branch, shrink_ref[at, :])
        start = 2 * width + step * WIDE
        parts_ref[:, start : start + WIDE] = jnp.sum(grad_hidden * normal, axis=0, keepdims=True)
        weighted = grad_hidden * hidden_gain_ref[:, at]
        weighted_ref[:, at] = weighted
        weighted_sum = weighted_sum + jnp.sum(weighted, axis=-1, keepdims=True)
        inner_sum = inner_sum + jnp.sum(weighted * normal, axis=-1, keepdims=True)
    seg = tokens // planes
    for k in range(planes):
        results[k][...] = result[k * seg : (k + 1) * seg, :].astype(bf16)
    weighted_mean = weighted_sum * (1.0 / spread)
    inner_mean = inner_sum * (1.0 / spread)
    rate = hidden_rate_ref[...]
    grad_second = jnp.zeros((tokens, width), f32)
    for step in range(steps):
        at = slice(step * WIDE, (step + 1) * WIDE)
        grad = rate * (
            weighted_ref[:, at] - weighted_mean - normal_ref[:, at].astype(f32) * inner_mean
        )
        expanded = (grad * slope_ref[:, at].astype(f32)).astype(bf16)
        expanded_ref[:, at] = expanded
        grad_second = grad_second + dot_nt(expanded, expand_ref[:, at])
    second_normal, second_rate = normalized(middle_ref[...])
    parts_ref[:, width : 2 * width] = jnp.sum(grad_second * second_normal, axis=0, keepdims=True)
    grad_middle = branch.astype(f32) + norm_back(
        second_normal, second_rate, grad_second * second_gain_ref[...]
    )
    grad_ref[...] = grad_middle
    mix = grad_middle.astype(bf16)
    mix_ref[...] = mix
    grads = []
    weighted_sum = 0.0
    inner_sum = 0.0
    for g in range(groups):
        grad_mixed = dot_nt(mix, merge_ref[g * piece : (g + 1) * piece, :])
        parts_ref[:, g * piece : (g + 1) * piece] = jnp.sum(
            grad_mixed * held_ref[g], axis=0, keepdims=True
        )
        weighted = grad_mixed * mixed_gain_ref[g]
        grads.append(weighted)
        weighted_sum = weighted_sum + jnp.sum(weighted, axis=-1, keepdims=True)
        inner_sum = inner_sum + jnp.sum(weighted * held_ref[g], axis=-1, keepdims=True)
    weighted_mean = weighted_sum * (1.0 / width)
    inner_mean = inner_sum * (1.0 / width)
    for g in range(slots):
        if g < groups:
            sent_ref[g] = mixed_rate_ref[...] * (
                grads[g] - weighted_mean - held_ref[g] * inner_mean
            )
        else:
            sent_ref[g] = jnp.zeros(sent_ref.shape[1:], f32)
    for u in range(slots):
        for side in range(2):
            away[u][:, side * piece : (side + 1) * piece] = sent_ref[
                slot ^ u, side * half : (side + 1) * half, :
            ].astype(bf16)


def turn_call(
    place, branch, normal, slope, middle, held, mixed_rate, hidden_rate,
    mixed_gain, second_gain, hidden_gain, merge, shrink, expand, planes,
):
    slots, tokens, piece = held.shape
    width, spread = expand.shape
    groups = width // piece

    def low(*shape):
        return jax.ShapeDtypeStruct(shape, bf16)

    def full(*shape):
        return jax.ShapeDtypeStruct(shape, f32)

    outs = pl.pallas_call(
        functools.partial(
            turn_kernel, slots=slots, planes=planes, groups=groups, width=width, spread=spread
        ),
        out_shape=(
            low(tokens, spread),
            low(tokens, width),
            full(tokens, width),
            full(1, 2 * width + spread),
        )
        + (low(tokens // 2, 2 * piece),) * slots
        + (low(tokens // planes, width),) * planes,
        in_specs=[pl.BlockSpec(memory_space=pltpu.SMEM)] + [vmem_spec()] * 13,
        out_specs=(vmem_spec(),) * (4 + slots + planes),
        scratch_shapes=[
            pltpu.VMEM((tokens, spread), f32),
            pltpu.VMEM((slots, tokens, piece), f32),
        ],
        compiler_params=params(TURN_MIB),
        cost_estimate=cost(9 << 30, 8 << 20),
        name="turn",
    )(
        place, branch, normal, slope, middle, held, mixed_rate, hidden_rate,
        mixed_gain, second_gain, hidden_gain, merge, shrink, expand,
    )
    return outs[:4], outs[4 : 4 + slots], outs[4 + slots :]


def cut_out(outs, total_ref, place_ref, bands, steps, rows_each, axis, cut):
    whole_ref, firsts = outs[0], outs[1:]
    far_rank, side = place_ref[2] // 2, place_ref[3]
    for at, code in codes(steps):
        other, far = code & 1, code >> 1
        offset = pl.multiple_of((far_rank ^ far) * rows_each, rows_each)
        parts = []
        for first, wide in bands:
            column = pl.multiple_of(first + (side ^ other) * wide, 128)
            parts.append(
                total_ref[pl.ds(offset, rows_each), pl.ds(column, wide)].astype(bf16)
            )
        value = parts[0] if len(parts) == 1 else jnp.concatenate(parts, axis=1)
        whole_ref[at] = value
        for chain, first_ref in enumerate(firsts):
            if at[chain] == 1:
                band = slice(0, cut) if chain == 0 else slice(cut, None)
                first_ref[at[:chain] + at[chain + 1 :]] = (
                    value[band] if axis == 0 else value[:, band]
                )


def shrink_kernel(
    place_ref, hidden_ref, branch_ref, hidden_got_ref, branch_got_ref, *refs, cutting
):
    total_ref = refs[-1]
    spread, _ = total_ref.shape
    branch = jnp.concatenate([branch_ref[...], branch_got_ref[...]], axis=0)

    def multiply(step, carry):
        at = columns_at(step)
        hidden = jnp.concatenate([hidden_ref[:, at], hidden_got_ref[:, at]], axis=0)
        total_ref[at, :] = dot_tn(hidden, branch)
        return carry

    lax.fori_loop(0, spread // WIDE, multiply, 0)
    cut_out(refs[:-1], total_ref, place_ref, **cutting)


def expand_kernel(
    place_ref, second_ref, mixed_ref, second_got_ref, mixed_got_ref,
    expanded_ref, mix_ref, expanded_got_ref, mix_got_ref, *refs, cutting,
):
    turned_ref, total_ref = refs[-2:]
    tokens, spread = expanded_ref.shape
    width = second_ref.shape[1]
    core = place_ref[2] % 2
    rows_each = cutting["rows_each"]

    def left(own_ref, got_ref):
        turned_ref[:, :tokens] = own_ref[...].astype(f32).T
        turned_ref[:, tokens:] = got_ref[...].astype(f32).T
        rows = [
            turned_ref[pl.ds(pl.multiple_of((2 * i + core) * rows_each, rows_each), rows_each), :]
            for i in range(width // (2 * rows_each))
        ]
        return jnp.concatenate(rows, axis=0).astype(bf16)

    second = left(second_ref, second_got_ref)
    for at in range(0, spread, WIDE):
        band = slice(at, at + WIDE)
        total_ref[:, band] = dot(
            second, jnp.concatenate([expanded_ref[:, band], expanded_got_ref[:, band]], axis=0)
        )
    mixed = left(mixed_ref, mixed_got_ref)
    total_ref[:, spread:] = dot(
        mixed, jnp.concatenate([mix_ref[...], mix_got_ref[...]], axis=0)
    )
    cut_out(refs[:-2], total_ref, place_ref, **cutting)


def outer_call(kernel, place, operands, rows, columns, bands, steps, size, axis, cut, scratch, name):
    rows_each = rows // size
    shape = (rows_each, columns // 2)
    low = (cut, shape[1]) if axis == 0 else (shape[0], cut)
    high = (shape[0] - cut, shape[1]) if axis == 0 else (shape[0], shape[1] - cut)
    pairs = (2,) * (len(steps) - 1)
    return pl.pallas_call(
        functools.partial(
            kernel,
            cutting=dict(bands=bands, steps=steps, rows_each=rows_each, axis=axis, cut=cut),
        ),
        out_shape=(
            jax.ShapeDtypeStruct((2,) + pairs + shape, bf16),
            jax.ShapeDtypeStruct(pairs + low, bf16),
            jax.ShapeDtypeStruct(pairs + high, bf16),
        ),
        in_specs=[pl.BlockSpec(memory_space=pltpu.SMEM)] + [vmem_spec()] * len(operands),
        out_specs=(vmem_spec(),) * 3,
        scratch_shapes=scratch + [pltpu.VMEM((rows // 2, columns), f32)],
        compiler_params=params(OUTER_MIB),
        cost_estimate=cost(2 << 30, 10 << 20),
        name=name,
    )(place, *operands)


def settle_kernel(place_ref, *refs):
    out = refs[-1]
    for k, ref in enumerate(refs[:-1]):
        out[place_ref[0] ^ k] = ref[...]


def settle_call(place, blocks):
    return pl.pallas_call(
        settle_kernel,
        out_shape=jax.ShapeDtypeStruct((len(blocks),) + blocks[0].shape, blocks[0].dtype),
        in_specs=[pl.BlockSpec(memory_space=pltpu.SMEM)] + [vmem_spec()] * len(blocks),
        out_specs=vmem_spec(),
        compiler_params=params(8),
        name="settle",
    )(place, *blocks)


def joined_slots_kernel(*refs, held):
    sources, outs = refs[:held], refs[held:]
    last = len(outs)
    for u, out in enumerate(outs):
        out[0] = sum(ref[u].astype(f32) for ref in sources).astype(bf16)
        out[1] = sum(ref[last].astype(f32) for ref in sources).astype(bf16)


def joined_slots_call(held, slots):
    _, rows, wide = held[0].shape
    return pl.pallas_call(
        functools.partial(joined_slots_kernel, held=len(held)),
        out_shape=(jax.ShapeDtypeStruct((2, rows, wide), bf16),) * slots,
        in_specs=[vmem_spec()] * len(held),
        out_specs=(vmem_spec(),) * slots,
        compiler_params=params(4),
        name="joined_slots",
    )(*held)


def heads_kernel(place_ref, *refs, groups, gains):
    joined_out, gains_out, held_ref = refs[-3:]
    pieces = refs[:-3]
    sums = []
    for u, ref in enumerate(pieces):
        held_ref[place_ref[1] ^ u] = ref[0].astype(f32)
        sums.append(ref[1].astype(f32))
    piece = pieces[0].shape[2] // 3
    for part in range(3):
        for g in range(groups):
            start = (part * groups + g) * piece
            joined_out[:, start : start + piece] = held_ref[
                g, :, part * piece : (part + 1) * piece
            ]
    while len(sums) > 1:
        sums = [sums[i] + sums[i + 1] for i in range(0, len(sums), 2)]
    wide = 3 * piece
    for r in range(-(-gains // wide)):
        end = min((r + 1) * wide, gains)
        gains_out[:, r * wide : end] = sums[0][r : r + 1, : end - r * wide]


def heads_call(place, blocks, width, gains):
    _, rows, wide = blocks[0].shape
    return pl.pallas_call(
        functools.partial(heads_kernel, groups=3 * width // wide, gains=gains),
        out_shape=(
            jax.ShapeDtypeStruct((rows, 3 * width), f32),
            jax.ShapeDtypeStruct((1, gains), f32),
        ),
        in_specs=[pl.BlockSpec(memory_space=pltpu.SMEM)] + [vmem_spec()] * len(blocks),
        out_specs=(vmem_spec(),) * 2,
        scratch_shapes=[pltpu.VMEM((len(blocks), rows, wide), f32)],
        compiler_params=params(8),
        name="heads_side_by_side",
    )(place, *blocks)


def input_kernel(*refs, planes, parts):
    inputs = refs[:planes]
    refs = refs[planes:]
    grad_ref, gain_ref = refs[:2]
    grad = sum(ref[at].astype(f32) for ref, at in zip(refs[2 : 2 + len(parts)], parts))
    outs = refs[2 + len(parts) :]
    normal, rate = normalized(
        jnp.concatenate([block[...] for block in inputs], axis=0).astype(f32)
    )
    value = grad_ref[...] + norm_back(normal, rate, grad * gain_ref[...])
    seg = value.shape[0] // planes
    for k in range(planes):
        outs[k][...] = value[k * seg : (k + 1) * seg, :].astype(bf16)


def input_call(inputs, grad_middle, gain, held, parts):
    planes = len(inputs)
    tokens, width = grad_middle.shape
    return pl.pallas_call(
        functools.partial(input_kernel, planes=planes, parts=parts),
        out_shape=(jax.ShapeDtypeStruct((tokens // planes, width), bf16),) * planes,
        in_specs=[vmem_spec()] * (2 + planes + len(held)),
        out_specs=(vmem_spec(),) * planes,
        compiler_params=params(16),
        name="input_back",
    )(*inputs, grad_middle, gain, *held)


def swap(value, axis, bits):
    size = lax.axis_size(axis)
    return lax.ppermute(value, axis, [(i, i ^ bits) for i in range(size)])


def pick(value, index, axis=0):
    return lax.dynamic_index_in_dim(value, index, axis, keepdims=False)


def in_hbm(*values):
    return [pltpu.with_memory_space_constraint(value, pltpu.HBM) for value in values]


def bits_of(size):
    return size.bit_length() - 1


def sums_kernel(*refs, listed, together):
    outs = refs[-1:] if together else refs[-len(listed) :]
    start = 0
    for i, terms in enumerate(listed):
        value = sum(refs[j][at].astype(f32) for j, at in terms).astype(bf16)
        if together:
            end = start + value.shape[together]
            outs[0][(..., slice(start, end)) + (slice(None),) * (-1 - together)] = value
            start = end
        else:
            outs[i][...] = value


def sums_call(sums, name, together=0):
    arrays, listed, shapes = [], [], []
    for terms in sums:
        entry = []
        for array, at in terms:
            where = [i for i, held in enumerate(arrays) if held is array]
            if not where:
                arrays.append(array)
                where = [len(arrays) - 1]
            entry.append((where[0], at))
        listed.append(entry)
        shapes.append(jax.eval_shape(lambda v, at=terms[0][1]: v[at], terms[0][0]).shape)
    if together:
        shape = list(shapes[0])
        shape[together] = sum(shape[together] for shape in shapes)
        shapes = [tuple(shape)]
    outs = pl.pallas_call(
        functools.partial(sums_kernel, listed=listed, together=together),
        out_shape=tuple(jax.ShapeDtypeStruct(shape, bf16) for shape in shapes),
        in_specs=[vmem_spec()] * len(arrays),
        out_specs=(vmem_spec(),) * len(shapes),
        compiler_params=params(4),
        name=name,
    )(*arrays)
    return outs[0] if together or len(shapes) == 1 else outs


class Halves:
    def __init__(self):
        self.entries = []
        self.chosen = {}

    def hold(self, array, names, bands=()):
        self.entries.append((array, names, dict(bands)))

    def terms(self, choice=()):
        chosen = dict(self.chosen)
        chosen.update(choice)
        return [
            (
                array,
                tuple(chosen[n] if n in chosen else bands.get(n, slice(None)) for n in names),
            )
            for array, names, bands in self.entries
        ]

    def receive(self, name, array, bands=()):
        self.chosen[name] = 0
        names = [n for n in self.entries[0][1] if n not in self.chosen]
        self.hold(array, names, bands)


def sides_kernel(place_ref, own_ref, other_ref, *outs):
    first = place_ref[3] == 0
    own, other = own_ref[...].astype(f32), other_ref[...].astype(f32)
    low, high = jnp.where(first, own, other), jnp.where(first, other, own)
    start = 0
    for out in outs:
        wide = out.shape[1] // 2
        out[:, :wide] = low[:, start : start + wide]
        out[:, wide:] = high[:, start : start + wide]
        start += wide


def sides_call(place, own, other, widths, name):
    rows = own.shape[0]
    return pl.pallas_call(
        sides_kernel,
        out_shape=tuple(jax.ShapeDtypeStruct((rows, wide), f32) for wide in widths),
        in_specs=[pl.BlockSpec(memory_space=pltpu.SMEM)] + [vmem_spec()] * 2,
        out_specs=(vmem_spec(),) * len(widths),
        compiler_params=params(8),
        name=name,
    )(place, own, other)


def per_device(
    layer_input, cotangent, doc_lengths, joined_weight, merge_weight, expand_weight,
    shrink_weight, first_gain, mixed_gain, second_gain, hidden_gain,
):
    _, planes, seg, width = layer_input.shape
    size = lax.axis_size("blk")
    slots = size // planes
    batches = lax.axis_size("batch")
    rank = lax.axis_index("blk")
    group_rank = lax.axis_index("batch")
    plane = rank // slots
    slot = rank % slots
    head_count = width // HEAD
    heads = -(-head_count // slots)
    groups = head_count // heads
    piece = heads * HEAD
    tokens = planes * seg
    length = slots * tokens
    side = group_rank % 2
    place = jnp.stack([plane, slot, rank, side]).astype(jnp.int32)

    def to_planes(blocks):
        return [pick(blocks, plane)] + [
            swap(pick(blocks, plane ^ k), "blk", k * slots) for k in range(1, planes)
        ]

    def all_slots(value):
        held = {0: value}
        for bit in reversed(range(bits_of(slots))):
            held.update({u | 1 << bit: swap(v, "blk", 1 << bit) for u, v in held.items()})
        return [held[u] for u in range(slots)]

    def over_slots(blocks):
        return [blocks[0]] + [swap(blocks[u], "blk", u) for u in range(1, slots)]

    spread = expand_weight.shape[1]
    first_arrived = to_planes(layer_input[0])
    own_start = jnp.minimum(slot, groups - 1) * piece
    own_weight = jnp.concatenate(
        [
            lax.dynamic_slice_in_dim(joined_weight, part * width + own_start, piece, 1)
            for part in range(3)
        ],
        axis=1,
    )
    lengths = doc_lengths[0]
    gain_row = first_gain.reshape(1, width)
    mixed_gain = mixed_gain.reshape(groups, 1, piece)
    second_gain = second_gain.reshape(1, width)
    hidden_gain = hidden_gain.reshape(1, spread)
    (
        first_arrived[-1], place, lengths, gain_row, mixed_gain, second_gain, hidden_gain, own_weight,
    ) = lax.optimization_barrier(
        (
            first_arrived[-1], place, lengths, gain_row, mixed_gain, second_gain, hidden_gain,
            own_weight,
        )
    )
    pieces = [all_slots(block) for block in first_arrived]
    (first, joined, factor), sent, shares = forward_call(
        place, lengths, gain_row, own_weight, pieces
    )
    sent, cotangent = lax.optimization_barrier((sent, cotangent))
    cotangent_blocks = to_planes(cotangent[0])
    (
        mixed, middle, second, hidden, hidden_give, normal, slope, held, mixed_rate, hidden_rate,
    ) = widen_call(
        place, over_slots(sent), first_arrived, mixed_gain, second_gain, hidden_gain, merge_weight,
        expand_weight,
    )
    hidden_give, cotangent_blocks = lax.optimization_barrier((hidden_give, cotangent_blocks))
    branch = branch_call(place, lengths, cotangent_blocks, slots)

    row_bits = list(range(1, bits_of(slots)))
    plane_bits = list(range(bits_of(slots), bits_of(size)))
    names = ["side"] + row_bits + plane_bits + ["rows", "columns"]
    steps = [0] + row_bits + plane_bits
    orders = (["side"] + row_bits, row_bits + ["side"])
    stages = len(orders[0])

    def cross(name, value):
        return swap(value, "batch", 1) if name == "side" else swap(value, "blk", 1 << name)

    def chains(axis, cut, whole):
        pair = [Halves(), Halves()]
        for chain, band in zip(pair, (slice(0, cut), slice(cut, None))):
            chain.hold(whole, names, {axis: band})
        return pair

    def sends(pair, at):
        return sums_call(
            [chain.terms({order[at]: 1}) for chain, order in zip(pair, orders)], "next_halves"
        )

    def crossed(at, values):
        return [cross(order[at], value) for order, value in zip(orders, values)]

    def arrive(pair, at, values):
        for chain, order, value in zip(pair, orders, values):
            chain.receive(order[at], value)

    def plane_depart(pair, bit, axis):
        together = -2 if axis == "rows" else -1
        return cross(
            bit, sums_call([chain.terms({bit: 1}) for chain in pair], "plane_halves", together)
        )

    def plane_arrive(pair, bit, axis, both):
        cut = pair[0].entries[0][2][axis].stop
        for chain, band in zip(pair, (slice(0, cut), slice(cut, None))):
            chain.receive(bit, both, {axis: band})

    def closed(pair, axis):
        together = -2 if axis == "rows" else -1
        value = sums_call([chain.terms() for chain in pair], "last_halves", together)
        for bit in range(1, bits_of(batches)):
            value = sums_call([[(value, ...), (swap(value, "batch", 1 << bit), ...)]], "groups")
        return value, swap(value, "batch", 1)

    cut = spread // size // 2
    shrink_whole, *shrink_firsts = outer_call(
        shrink_kernel, place,
        [hidden, branch, swap(hidden_give, "blk", 1), swap(branch, "blk", 1)],
        spread, width, ((0, width // 2),), steps, size, 0, cut, [], "shrink_outer",
    )
    shrink_sent = crossed(0, shrink_firsts)
    second_got, mixed_got = swap(second, "blk", 1), swap(mixed, "blk", 1)
    (expanded, mix, grad_middle, parts), away, results = turn_call(
        place, branch, normal, slope, middle, held, mixed_rate, hidden_rate,
        mixed_gain, second_gain, hidden_gain, merge_weight, shrink_weight, expand_weight, planes,
    )
    shrink_sent, second_got, mixed_got, expanded, mix = lax.optimization_barrier(
        (shrink_sent, second_got, mixed_got, expanded, mix)
    )
    shrink_chains = chains("rows", cut, shrink_whole)
    arrive(shrink_chains, 0, shrink_sent)

    returned = over_slots(away)
    expanded_got, mix_got = swap(expanded, "blk", 1), swap(mix, "blk", 1)
    returned, expanded_got, mix_got = lax.optimization_barrier((returned, expanded_got, mix_got))
    cut = ((spread + width) // 4 + 127) // 128 * 128
    expand_whole, *expand_firsts = outer_call(
        expand_kernel, place,
        [second, mixed, second_got, mixed_got, expanded, mix, expanded_got, mix_got],
        width, spread + width, ((0, spread // 2), (spread, width // 2)), steps, size, 1, cut,
        [pltpu.VMEM((width, 2 * tokens), f32)], "expand_outer",
    )
    for at in range(1, stages):
        shrink_sent = crossed(at, sends(shrink_chains, at))
        if at < stages - 1:
            arrive(shrink_chains, at, shrink_sent)
    expand_firsts, results = lax.optimization_barrier((expand_firsts, results))
    result_blocks = [results[0]] + [
        swap(results[k], "blk", k * slots) for k in range(1, planes)
    ]
    returned, expand_firsts, shrink_sent = lax.optimization_barrier(
        (returned, expand_firsts, shrink_sent)
    )
    arrive(shrink_chains, stages - 1, shrink_sent)
    expand_sent = crossed(0, expand_firsts)
    shrink_both = plane_depart(shrink_chains, plane_bits[0], "rows")
    joined_keep, joined_give, branch_keep, branch_give = backward_call(
        place, first, joined, factor, own_weight, gain_row, parts, returned, shares, planes
    )
    (
        joined_give, branch_give, shrink_both, expand_sent, result_blocks,
    ) = lax.optimization_barrier(
        (joined_give, branch_give, shrink_both, expand_sent, result_blocks)
    )
    plane_arrive(shrink_chains, plane_bits[0], "rows", shrink_both)
    expand_chains = chains("columns", cut, expand_whole)
    arrive(expand_chains, 0, expand_sent)

    joined_got = swap(joined_give, "blk", 1 << plane_bits[0])
    branch_got = swap(branch_give, "blk", 1)
    for at in range(1, stages):
        expand_sent = crossed(at, sends(expand_chains, at))
        if at < stages - 1:
            arrive(expand_chains, at, expand_sent)
    for bit in plane_bits[1:]:
        shrink_both = plane_depart(shrink_chains, bit, "rows")
        if bit != plane_bits[-1]:
            plane_arrive(shrink_chains, bit, "rows", shrink_both)
    branch_held, prefixes = [branch_keep, branch_got], [(), ()]
    for bit in row_bits:
        give = sums_call(
            [[(v, p + (1,)) for v, p in zip(branch_held, prefixes)]], "branch_halves"
        )
        prefixes = [p + (0,) for p in prefixes] + [()]
        branch_held.append(swap(give, "blk", 1 << bit))
    joined_got, branch_held[-1], expand_sent, shrink_both = lax.optimization_barrier(
        (joined_got, branch_held[-1], expand_sent, shrink_both)
    )
    arrive(expand_chains, stages - 1, expand_sent)
    plane_arrive(shrink_chains, plane_bits[-1], "rows", shrink_both)

    expand_both = plane_depart(expand_chains, plane_bits[0], "columns")
    joined_terms = [(joined_keep, 0), (joined_got, 0)]
    blocks = planes * slots // 2
    gain_terms = [(joined_give, blocks), (joined_got, blocks)]
    for bit in plane_bits[1:]:
        blocks //= 2
        joined_give = sums_call(
            [
                [(v, slice(start + blocks, start + 2 * blocks)) for v, start in joined_terms],
                [(v, slice(at, at + 1)) for v, at in gain_terms],
            ],
            "joined_halves", -3,
        )
        joined_got = swap(joined_give, "blk", 1 << bit)
        joined_terms.append((joined_got, 0))
        gain_terms = [(joined_give, blocks), (joined_got, blocks)]
    input_blocks = input_call(
        first_arrived, grad_middle, gain_row, branch_held, prefixes
    )
    input_blocks = [input_blocks[0]] + [
        swap(input_blocks[k], "blk", k * slots) for k in range(1, planes)
    ]
    joined_last = sums_call(
        [
            [(v, slice(start, start + slots)) for v, start in joined_terms],
            [(v, slice(at, at + 1)) for v, at in gain_terms],
        ],
        "joined_last", -3,
    )
    held = [joined_last]
    for bit in range(bits_of(batches)):
        if len(held) > 1:
            held = [sums_call([[(v, ...) for v in held]], "joined_groups")]
        held.append(swap(held[0], "batch", 1 << bit))
    joined_sent = joined_slots_call(held, slots)
    joined_grad, gain_grads = heads_call(
        place,
        [joined_sent[0]] + [swap(joined_sent[u], "blk", u) for u in range(1, slots)],
        width, 3 * width + spread,
    )
    shrink_grad, = sides_call(place, *closed(shrink_chains, "rows"), (width,), "shrink_sides")
    plane_arrive(expand_chains, plane_bits[0], "columns", expand_both)
    for bit in plane_bits[1:]:
        expand_both = plane_depart(expand_chains, bit, "columns")
        plane_arrive(expand_chains, bit, "columns", expand_both)
    expand_grad, merge_grad = sides_call(
        place, *closed(expand_chains, "columns"), (spread, width), "expand_sides"
    )
    layer_result = settle_call(place, result_blocks).reshape(layer_input.shape)
    input_grad = settle_call(place, input_blocks).reshape(layer_input.shape)
    gain_grads = gain_grads[0]
    return (
        layer_result, input_grad, joined_grad, merge_grad, expand_grad,
        shrink_grad, gain_grads[:width], gain_grads[width : 2 * width],
        gain_grads[2 * width : 3 * width], gain_grads[3 * width :],
    )


def solution(mesh):
    rows = P("batch", None, "blk", None)
    return jax.shard_map(
        per_device,
        mesh=mesh,
        in_specs=(rows, rows, P("batch", None, None)) + (P(),) * 8,
        out_specs=(rows, rows) + (P("blk", None),) * 4 + (P(),) * 4,
        check_vma=False,
    )
```

```python
import functools

import jax
import jax.numpy as jnp
from jax import lax
from jax.experimental import pallas as pl
from jax.experimental.pallas import tpu as pltpu
from jax.sharding import PartitionSpec as P

HEAD = 64
TILE = 256
WIDE = 512
BAND = 384
FORWARD_MIB = 14
BACKWARD_MIB = 14
WIDEN_MIB = 11
TURN_MIB = 11
OUTER_MIB = 16
big_negative = -1e30
norm_epsilon = 1e-05

f32 = jnp.float32
bf16 = jnp.bfloat16


def dot(left, right):
    return jnp.dot(left, right, preferred_element_type=f32)


def dot_nt(left, right):
    return lax.dot_general(left, right, (((1,), (1,)), ((), ())), preferred_element_type=f32)


def dot_tn(left, right):
    return lax.dot_general(left, right, (((0,), (0,)), ((), ())), preferred_element_type=f32)


def normalized(values):
    centred = values - jnp.mean(values, axis=-1, keepdims=True)
    rate = lax.rsqrt(jnp.mean(centred * centred, axis=-1, keepdims=True) + norm_epsilon)
    return centred * rate, rate


def norm_back(normal, rate, weighted):
    return rate * (
        weighted
        - jnp.mean(weighted, axis=-1, keepdims=True)
        - normal * jnp.mean(weighted * normal, axis=-1, keepdims=True)
    )


def vmem_spec():
    return pl.BlockSpec(memory_space=pltpu.VMEM)


def hbm_spec():
    return pl.BlockSpec(memory_space=pltpu.HBM)


def params(mebibytes):
    return pltpu.CompilerParams(vmem_limit_bytes=mebibytes * 1024 * 1024)


def cost(flops, moved):
    return pl.CostEstimate(flops=flops, bytes_accessed=moved, transcendentals=0)


def document_ends(lengths_ref, plane):
    ends, end = [], jnp.int32(0)
    for d in range(lengths_ref.shape[1]):
        end = end + lengths_ref[plane, d]
        ends.append(end)
    return ends


def columns_at(step):
    return pl.ds(pl.multiple_of(step * WIDE, WIDE), WIDE)


def codes(steps):
    listed = [((), 0)]
    for bit in steps:
        listed = [(at + (b,), code | (b << bit)) for at, code in listed for b in (0, 1)]
    return listed


def forward_kernel(*refs, planes, slots, seg, heads):
    place_ref, lengths_ref, gain_ref, weight_ref = refs[:4]
    pieces = refs[4 : 4 + slots * planes]
    refs = refs[4 + slots * planes :]
    length = planes * slots * seg
    tiles = length // TILE
    first_ref, joined_ref, factor_ref = refs[:3]
    sent = refs[3 : 3 + slots]
    shares = refs[3 + slots : 3 + slots + tiles]
    rows_ref, attention_ref = refs[3 + slots + tiles :]
    plane, slot = place_ref[0], place_ref[1]
    for u in range(slots):
        for k in range(planes):
            offset = ((plane ^ k) * slots + (slot ^ u)) * seg
            rows_ref[pl.ds(pl.multiple_of(offset, seg), seg), :] = pieces[k * slots + u][...]
    width = heads * HEAD

    def project(tile, carry):
        rows = pl.ds(pl.multiple_of(tile * TILE, TILE), TILE)
        normal, _ = normalized(rows_ref[rows, :].astype(f32))
        first = (normal * gain_ref[...]).astype(bf16)
        first_ref[rows, :] = first
        joined = dot(first, weight_ref[...]).astype(bf16)
        for part in range(3):
            for h in range(heads):
                column = part * width + h * HEAD
                value = joined[:, column : column + HEAD]
                if part == 0:
                    value = value * jnp.asarray(0.125, bf16)
                joined_ref[part * heads + h, rows, :] = value
        return carry

    lax.fori_loop(0, tiles, project, 0, unroll=True)
    ends = document_ends(lengths_ref, plane)
    for q in reversed(range(tiles)):
        rows = slice(q * TILE, (q + 1) * TILE)
        reach = (q + 1) * TILE
        places = q * TILE + lax.broadcasted_iota(jnp.int32, (TILE, 1), 0)
        start = jnp.zeros((TILE, 1), jnp.int32)
        for end in ends:
            start = jnp.maximum(start, jnp.where(places >= end, end, 0))
        query_pos = q * TILE + lax.broadcasted_iota(jnp.int32, (TILE, reach), 0)
        key_pos = lax.broadcasted_iota(jnp.int32, (TILE, reach), 1)
        allowed = (key_pos <= query_pos) & (key_pos >= start)
        for h in range(heads):
            scores = dot_nt(joined_ref[h, rows, :], joined_ref[heads + h, :reach, :])
            scores = jnp.where(allowed, scores, big_negative)
            peak = jnp.max(scores, axis=-1, keepdims=True)
            raised = jnp.exp(scores - peak)
            total = jnp.sum(raised, axis=-1, keepdims=True)
            share = raised.astype(bf16)
            shares[q][h] = share
            factor = 1.0 / total
            factor_ref[rows, h : h + 1] = factor
            attention_ref[h, rows, :] = factor * dot(
                share, joined_ref[2 * heads + h, :reach, :]
            )
    half = planes // 2
    for u in range(slots):
        for k in range(planes):
            offset = ((plane ^ k) * slots + (slot ^ u)) * seg
            rows = slice(k % half * seg, (k % half + 1) * seg)
            for h in range(heads):
                part = attention_ref[h, pl.ds(pl.multiple_of(offset, seg), seg), :]
                column = k // half * width + h * HEAD
                sent[u][rows, column : column + HEAD] = part.astype(bf16)


def forward_call(place, lengths, gain, weight, pieces):
    planes, slots = len(pieces), len(pieces[0])
    seg, width = pieces[0][0].shape
    length = planes * slots * seg
    heads = weight.shape[1] // (3 * HEAD)
    kernel = functools.partial(forward_kernel, planes=planes, slots=slots, seg=seg, heads=heads)
    packed = jax.ShapeDtypeStruct((planes * seg // 2, 2 * heads * HEAD), bf16)
    tiled = [(heads, TILE, reach) for reach in range(TILE, length + 1, TILE)]
    outs = pl.pallas_call(
        kernel,
        out_shape=(
            pltpu.VMEM((length, width), bf16),
            pltpu.VMEM((3 * heads, length, HEAD), bf16),
            pltpu.VMEM((length, heads), f32),
        )
        + (packed,) * slots
        + tuple(pltpu.VMEM(shape, bf16) for shape in tiled),
        in_specs=[pl.BlockSpec(memory_space=pltpu.SMEM)] * 2
        + [vmem_spec()] * (2 + slots * planes),
        out_specs=(vmem_spec(),) * (3 + slots + len(tiled)),
        scratch_shapes=[
            pltpu.VMEM((length, width), bf16),
            pltpu.VMEM((heads, length, HEAD), f32),
        ],
        compiler_params=params(FORWARD_MIB * length // 1024),
        cost_estimate=cost(8 << 30, 8 << 20),
        name="attention_forward",
    )(place, lengths, gain, weight, *[block for blocks in pieces for block in blocks])
    return outs[:3], outs[3 : 3 + slots], outs[3 + slots :]


def backward_kernel(*refs, planes, slots, seg, heads, rows_each):
    place_ref, first_ref, joined_ref, factor_ref, weight_ref, gain_ref, parts_ref = refs[:7]
    pieces = refs[7 : 7 + slots]
    length = planes * slots * seg
    tiles = length // TILE
    refs = refs[7 + slots :]
    shares = refs[:tiles]
    joined_keep, joined_give, branch_keep, branch_give = refs[tiles : tiles + 4]
    grad_ref, arrived_ref, key_ref, value_ref, total_ref, outer_ref, row_ref = refs[tiles + 4 :]
    plane, slot = place_ref[0], place_ref[1]
    width = heads * HEAD
    half = planes // 2
    for u in range(slots):
        for k in range(planes):
            offset = ((plane ^ k) * slots + (slot ^ u)) * seg
            column = k // half * width
            arrived_ref[pl.ds(pl.multiple_of(offset, seg), seg), :] = pieces[u][
                k % half * seg : (k % half + 1) * seg, column : column + width
            ]
    for h in range(heads):
        for q in reversed(range(tiles)):
            rows = slice(q * TILE, (q + 1) * TILE)
            reach = (q + 1) * TILE
            factor = factor_ref[rows, h : h + 1]
            grad = (arrived_ref[rows, h * HEAD : (h + 1) * HEAD].astype(f32) * factor).astype(bf16)
            share = shares[q][h]
            product = share.astype(f32) * dot_nt(grad, joined_ref[2 * heads + h, :reach, :])
            inner = jnp.sum(product, axis=-1, keepdims=True)
            grad_scores = (product - share.astype(f32) * (inner * factor)).astype(bf16)
            query_grad = dot(grad_scores, joined_ref[heads + h, :reach, :]) * 0.125
            grad_ref[rows, h * HEAD : (h + 1) * HEAD] = query_grad.astype(bf16)
            key_add = dot_tn(joined_ref[h, rows, :], grad_scores)
            value_add = dot_tn(grad, share)
            if q == tiles - 1:
                key_ref[...] = key_add
                value_ref[...] = value_add
            else:
                key_ref[:, :reach] += key_add
                value_ref[:, :reach] += value_add
        for part, source in ((1, key_ref), (2, value_ref)):
            column = part * width + h * HEAD
            for q in range(tiles):
                rows = slice(q * TILE, (q + 1) * TILE)
                grad_ref[rows, column : column + HEAD] = source[:, rows].T.astype(bf16)

    def back(tile, carry):
        rows = pl.ds(pl.multiple_of(tile * TILE, TILE), TILE)
        total_ref[rows, :] = dot_nt(grad_ref[rows, :], weight_ref[...])
        return carry

    lax.fori_loop(0, tiles, back, 0, unroll=True)
    for at, code in codes(range(1, bits_of(slots))):
        for out, u in ((branch_keep, code), (branch_give, code | 1)):
            for k in range(planes):
                offset = ((plane ^ k) * slots + (slot ^ u)) * seg
                out[at + (slice(k * seg, (k + 1) * seg),)] = total_ref[
                    pl.ds(pl.multiple_of(offset, seg), seg), :
                ].astype(bf16)
    model = first_ref.shape[1]
    for d in range(0, model, TILE):
        outer = dot_tn(first_ref[:, d : d + TILE], grad_ref[...])
        outer_ref[d : d + TILE, :] = outer
        scaled = jnp.sum(outer * weight_ref[d : d + TILE, :].astype(f32), axis=-1, keepdims=True)
        scaled = jnp.broadcast_to(scaled, (TILE, 128)).T
        row_ref[:, d : d + TILE] = scaled[:1] / gain_ref[:, d : d + TILE]
    wide = 3 * width
    row_ref[:, model : model + parts_ref.shape[1]] = parts_ref[...]
    gains = model + parts_ref.shape[1]
    half = planes * slots // 2
    at = 0
    for _, code in codes(range(bits_of(planes))):
        for u in range(slots):
            offset = ((plane ^ code) * slots + (slot ^ u)) * rows_each
            out = joined_keep if at < half else joined_give
            out[at % half] = outer_ref[
                pl.ds(pl.multiple_of(offset, rows_each), rows_each), :
            ].astype(bf16)
            at += 1
    outer_ref[:rows_each, :] = jnp.zeros((rows_each, wide), f32)
    for r in range(-(-gains // wide)):
        end = min((r + 1) * wide, gains)
        outer_ref[r : r + 1, : end - r * wide] = row_ref[:, r * wide : end]
    joined_give[half] = outer_ref[:rows_each, :].astype(bf16)


def backward_call(
    place, first, joined, factor, weight, gain, parts, pieces, shares, planes
):
    slots = len(pieces)
    tokens = pieces[0].shape[0] * 2
    heads, length = joined.shape[0] // 3, joined.shape[1]
    width = weight.shape[0]
    rows_each = width // (planes * slots)
    kernel = functools.partial(
        backward_kernel, planes=planes, slots=slots, seg=tokens // planes, heads=heads,
        rows_each=rows_each,
    )
    pairs = (2,) * (bits_of(slots) - 1)
    wide = 3 * heads * HEAD
    row = -(-(width + parts.shape[1]) // 128) * 128
    return pl.pallas_call(
        kernel,
        out_shape=(
            jax.ShapeDtypeStruct((planes * slots // 2, rows_each, wide), bf16),
            jax.ShapeDtypeStruct((planes * slots // 2 + 1, rows_each, wide), bf16),
            jax.ShapeDtypeStruct(pairs + (tokens, width), bf16),
            jax.ShapeDtypeStruct(pairs + (tokens, width), bf16),
        ),
        in_specs=[pl.BlockSpec(memory_space=pltpu.SMEM)]
        + [vmem_spec()] * (6 + slots + len(shares)),
        out_specs=(vmem_spec(),) * 4,
        scratch_shapes=[
            pltpu.VMEM((length, wide), bf16),
            pltpu.VMEM((length, heads * HEAD), bf16),
            pltpu.VMEM((HEAD, length), f32),
            pltpu.VMEM((HEAD, length), f32),
            pltpu.VMEM((length, width), f32),
            pltpu.VMEM((width, wide), f32),
            pltpu.VMEM((1, row), f32),
        ],
        compiler_params=params(BACKWARD_MIB * length // 1024),
        cost_estimate=cost(10 << 30, 10 << 20),
        name="attention_backward",
    )(place, first, joined, factor, weight, gain, parts, *pieces, *shares)


def widen_kernel(*refs, slots, planes, groups, width, spread, block):
    place_ref = refs[0]
    pieces = refs[1 : 1 + slots]
    inputs = refs[1 + slots : 1 + slots + planes]
    refs = refs[1 + slots + planes :]
    mixed_gain_ref, second_gain_ref, hidden_gain_ref, merge_ref, expand_ref = refs[:5]
    (
        mixed_ref, middle_ref, second_ref, hidden_ref, hidden_give_ref, normal_ref, slope_ref,
        held_ref, mixed_rate_ref, hidden_rate_ref,
    ) = refs[5:15]
    (gelu_ref,) = refs[15:]
    steps = spread // WIDE

    slot = place_ref[1]
    piece = width // groups
    tokens = planes * inputs[0].shape[0]
    half = tokens // 2
    for u in range(slots):
        for side in range(2):
            held_ref[slot ^ u, side * half : (side + 1) * half, :] = pieces[u][
                :, side * piece : (side + 1) * piece
            ].astype(f32)
    mean = sum(jnp.sum(held_ref[g], axis=-1, keepdims=True) for g in range(groups)) * (1.0 / width)
    square = 0.0
    for g in range(groups):
        centred = held_ref[g] - mean
        held_ref[g] = centred
        square = square + jnp.sum(centred * centred, axis=-1, keepdims=True)
    mixed_rate = lax.rsqrt(square * (1.0 / width) + norm_epsilon)
    mixed_rate_ref[...] = mixed_rate
    middle = jnp.concatenate([block[...] for block in inputs], axis=0).astype(f32)
    for g in range(groups):
        normal = held_ref[g] * mixed_rate
        held_ref[g] = normal
        mixed = (normal * mixed_gain_ref[g]).astype(bf16)
        mixed_ref[:, g * piece : (g + 1) * piece] = mixed
        middle = middle + dot(mixed, merge_ref[g * piece : (g + 1) * piece, :])
    middle_ref[...] = middle
    second_normal, _ = normalized(middle)
    second = (second_normal * second_gain_ref[...]).astype(bf16)
    second_ref[...] = second
    total = jnp.zeros((tokens, 1), f32)

    def widen(step, total):
        at = columns_at(step)
        value = dot(second, expand_ref[:, at])
        share = 0.5 * (1.0 + lax.erf(value * 0.7071067811865476))
        gelu = value * share
        gelu_ref[:, at] = gelu
        slope = share + value * (0.3989422804014327 * jnp.exp(-0.5 * value * value))
        slope_ref[:, at] = slope.astype(bf16)
        return total + jnp.sum(gelu, axis=-1, keepdims=True)

    total = lax.fori_loop(0, steps, widen, total)
    mean = total * (1.0 / spread)
    total = jnp.zeros((tokens, 1), f32)
    for step in range(steps):
        centred = gelu_ref[:, step * WIDE : (step + 1) * WIDE] - mean
        total = total + jnp.sum(centred * centred, axis=-1, keepdims=True)
    rate = lax.rsqrt(total * (1.0 / spread) + norm_epsilon)
    hidden_rate_ref[...] = rate
    core = slot % 2
    for at in range(0, spread, 2 * BAND):
        ours, theirs = [], []
        for start in range(at, at + 2 * BAND, 2 * block):
            low = slice(start, start + block)
            high = slice(start + block, start + 2 * block)
            parts = []
            for part in (low, high):
                normal = (gelu_ref[:, part] - mean) * rate
                normal_ref[:, part] = normal.astype(bf16)
                parts.append((normal * hidden_gain_ref[:, part]).astype(bf16))
            ours.append(parts[0])
            theirs.append(parts[1])
        even, odd = jnp.concatenate(ours, axis=1), jnp.concatenate(theirs, axis=1)
        half_at = slice(at // 2, at // 2 + BAND)
        hidden_ref[:, half_at] = jnp.where(core == 0, even, odd)
        hidden_give_ref[:, half_at] = jnp.where(core == 0, odd, even)


def widen_call(
    place, pieces, inputs, mixed_gain, second_gain, hidden_gain, merge, expand
):
    slots = len(pieces)
    tokens = len(inputs) * inputs[0].shape[0]
    piece = pieces[0].shape[1] // 2
    width, spread = expand.shape
    groups = width // piece

    def low(*shape):
        return jax.ShapeDtypeStruct(shape, bf16)

    def full(*shape):
        return jax.ShapeDtypeStruct(shape, f32)

    return pl.pallas_call(
        functools.partial(
            widen_kernel, slots=slots, planes=len(inputs), groups=groups, width=width,
            spread=spread, block=spread // (slots * len(inputs)),
        ),
        out_shape=(
            low(tokens, width),
            full(tokens, width),
            low(tokens, width),
            low(tokens, spread // 2),
            low(tokens, spread // 2),
            low(tokens, spread),
            low(tokens, spread),
            full(slots, tokens, piece),
            full(tokens, 1),
            full(tokens, 1),
        ),
        in_specs=[pl.BlockSpec(memory_space=pltpu.SMEM)]
        + [vmem_spec()] * (5 + slots + len(inputs)),
        out_specs=(vmem_spec(),) * 10,
        scratch_shapes=[
            pltpu.VMEM((tokens, spread), f32),
        ],
        compiler_params=params(WIDEN_MIB),
        cost_estimate=cost(6 << 30, 6 << 20),
        name="widen",
    )(
        place, *pieces, *inputs, mixed_gain, second_gain, hidden_gain, merge, expand,
    )


def branch_kernel(place_ref, lengths_ref, *refs, slots):
    blocks, branch_ref = refs[:-1], refs[-1]
    seg = blocks[0].shape[0]
    limit = document_ends(lengths_ref, place_ref[0])[-1]
    for k, block in enumerate(blocks):
        offset = ((place_ref[0] ^ k) * slots + place_ref[1]) * seg
        valid = offset + lax.broadcasted_iota(jnp.int32, (seg, 1), 0) < limit
        branch_ref[k * seg : (k + 1) * seg, :] = jnp.where(
            valid, block[...], jnp.zeros((), bf16)
        )


def branch_call(place, lengths, blocks, slots):
    seg, width = blocks[0].shape
    return pl.pallas_call(
        functools.partial(branch_kernel, slots=slots),
        out_shape=jax.ShapeDtypeStruct((len(blocks) * seg, width), bf16),
        in_specs=[pl.BlockSpec(memory_space=pltpu.SMEM)] * 2 + [vmem_spec()] * len(blocks),
        out_specs=vmem_spec(),
        compiler_params=params(4),
        name="branch",
    )(place, lengths, *blocks)


def turn_kernel(*refs, slots, planes, groups, width, spread):
    (
        place_ref, branch_ref, normal_ref, slope_ref, middle_ref, held_ref,
        mixed_rate_ref, hidden_rate_ref,
        mixed_gain_ref, second_gain_ref, hidden_gain_ref, merge_ref, shrink_ref, expand_ref,
    ) = refs[:14]
    expanded_ref, mix_ref, grad_ref, parts_ref = refs[14:18]
    away = refs[18 : 18 + slots]
    results = refs[18 + slots : 18 + slots + planes]
    weighted_ref, sent_ref = refs[18 + slots + planes :]
    steps = spread // WIDE

    slot = place_ref[1]
    piece = width // groups
    tokens = middle_ref.shape[0]
    half = tokens // 2
    branch = branch_ref[...]
    result = middle_ref[...]
    weighted_sum = jnp.zeros((tokens, 1), f32)
    inner_sum = jnp.zeros((tokens, 1), f32)
    for step in range(steps):
        at = slice(step * WIDE, (step + 1) * WIDE)
        normal = normal_ref[:, at].astype(f32)
        hidden = (normal * hidden_gain_ref[:, at]).astype(bf16)
        result = result + dot(hidden, shrink_ref[at, :])
        grad_hidden = dot_nt(branch, shrink_ref[at, :])
        start = 2 * width + step * WIDE
        parts_ref[:, start : start + WIDE] = jnp.sum(grad_hidden * normal, axis=0, keepdims=True)
        weighted = grad_hidden * hidden_gain_ref[:, at]
        weighted_ref[:, at] = weighted
        weighted_sum = weighted_sum + jnp.sum(weighted, axis=-1, keepdims=True)
        inner_sum = inner_sum + jnp.sum(weighted * normal, axis=-1, keepdims=True)
    seg = tokens // planes
    for k in range(planes):
        results[k][...] = result[k * seg : (k + 1) * seg, :].astype(bf16)
    weighted_mean = weighted_sum * (1.0 / spread)
    inner_mean = inner_sum * (1.0 / spread)
    rate = hidden_rate_ref[...]
    grad_second = jnp.zeros((tokens, width), f32)
    for step in range(steps):
        at = slice(step * WIDE, (step + 1) * WIDE)
        grad = rate * (
            weighted_ref[:, at] - weighted_mean - normal_ref[:, at].astype(f32) * inner_mean
        )
        expanded = (grad * slope_ref[:, at].astype(f32)).astype(bf16)
        expanded_ref[:, at] = expanded
        grad_second = grad_second + dot_nt(expanded, expand_ref[:, at])
    second_normal, second_rate = normalized(middle_ref[...])
    parts_ref[:, width : 2 * width] = jnp.sum(grad_second * second_normal, axis=0, keepdims=True)
    grad_middle = branch.astype(f32) + norm_back(
        second_normal, second_rate, grad_second * second_gain_ref[...]
    )
    grad_ref[...] = grad_middle
    mix = grad_middle.astype(bf16)
    mix_ref[...] = mix
    grads = []
    weighted_sum = 0.0
    inner_sum = 0.0
    for g in range(groups):
        grad_mixed = dot_nt(mix, merge_ref[g * piece : (g + 1) * piece, :])
        parts_ref[:, g * piece : (g + 1) * piece] = jnp.sum(
            grad_mixed * held_ref[g], axis=0, keepdims=True
        )
        weighted = grad_mixed * mixed_gain_ref[g]
        grads.append(weighted)
        weighted_sum = weighted_sum + jnp.sum(weighted, axis=-1, keepdims=True)
        inner_sum = inner_sum + jnp.sum(weighted * held_ref[g], axis=-1, keepdims=True)
    weighted_mean = weighted_sum * (1.0 / width)
    inner_mean = inner_sum * (1.0 / width)
    for g in range(slots):
        if g < groups:
            sent_ref[g] = mixed_rate_ref[...] * (
                grads[g] - weighted_mean - held_ref[g] * inner_mean
            )
        else:
            sent_ref[g] = jnp.zeros(sent_ref.shape[1:], f32)
    for u in range(slots):
        for side in range(2):
            away[u][:, side * piece : (side + 1) * piece] = sent_ref[
                slot ^ u, side * half : (side + 1) * half, :
            ].astype(bf16)


def turn_call(
    place, branch, normal, slope, middle, held, mixed_rate, hidden_rate,
    mixed_gain, second_gain, hidden_gain, merge, shrink, expand, planes,
):
    slots, tokens, piece = held.shape
    width, spread = expand.shape
    groups = width // piece

    def low(*shape):
        return jax.ShapeDtypeStruct(shape, bf16)

    def full(*shape):
        return jax.ShapeDtypeStruct(shape, f32)

    outs = pl.pallas_call(
        functools.partial(
            turn_kernel, slots=slots, planes=planes, groups=groups, width=width, spread=spread
        ),
        out_shape=(
            low(tokens, spread),
            low(tokens, width),
            full(tokens, width),
            full(1, 2 * width + spread),
        )
        + (low(tokens // 2, 2 * piece),) * slots
        + (low(tokens // planes, width),) * planes,
        in_specs=[pl.BlockSpec(memory_space=pltpu.SMEM)] + [vmem_spec()] * 13,
        out_specs=(vmem_spec(),) * (4 + slots + planes),
        scratch_shapes=[
            pltpu.VMEM((tokens, spread), f32),
            pltpu.VMEM((slots, tokens, piece), f32),
        ],
        compiler_params=params(TURN_MIB),
        cost_estimate=cost(9 << 30, 8 << 20),
        name="turn",
    )(
        place, branch, normal, slope, middle, held, mixed_rate, hidden_rate,
        mixed_gain, second_gain, hidden_gain, merge, shrink, expand,
    )
    return outs[:4], outs[4 : 4 + slots], outs[4 + slots :]


def cut_out(outs, total_ref, place_ref, bands, steps, rows_each, axis, cut):
    whole_ref, firsts = outs[0], outs[1:]
    far_rank, side = place_ref[2] // 2, place_ref[3]
    for at, code in codes(steps):
        other, far = code & 1, code >> 1
        offset = pl.multiple_of((far_rank ^ far) * rows_each, rows_each)
        parts = []
        for first, wide in bands:
            column = pl.multiple_of(first + (side ^ other) * wide, 128)
            parts.append(
                total_ref[pl.ds(offset, rows_each), pl.ds(column, wide)].astype(bf16)
            )
        value = parts[0] if len(parts) == 1 else jnp.concatenate(parts, axis=1)
        whole_ref[at] = value
        for chain, first_ref in enumerate(firsts):
            if at[chain] == 1:
                band = slice(0, cut) if chain == 0 else slice(cut, None)
                first_ref[at[:chain] + at[chain + 1 :]] = (
                    value[band] if axis == 0 else value[:, band]
                )


def shrink_kernel(
    place_ref, hidden_ref, branch_ref, hidden_got_ref, branch_got_ref, *refs, cutting
):
    total_ref = refs[-1]
    spread, _ = total_ref.shape
    branch = jnp.concatenate([branch_ref[...], branch_got_ref[...]], axis=0)

    def multiply(step, carry):
        at = columns_at(step)
        hidden = jnp.concatenate([hidden_ref[:, at], hidden_got_ref[:, at]], axis=0)
        total_ref[at, :] = dot_tn(hidden, branch)
        return carry

    lax.fori_loop(0, spread // WIDE, multiply, 0)
    cut_out(refs[:-1], total_ref, place_ref, **cutting)


def expand_kernel(
    place_ref, second_ref, mixed_ref, second_got_ref, mixed_got_ref,
    expanded_ref, mix_ref, expanded_got_ref, mix_got_ref, *refs, cutting,
):
    turned_ref, total_ref = refs[-2:]
    tokens, spread = expanded_ref.shape
    width = second_ref.shape[1]
    core = place_ref[2] % 2
    rows_each = cutting["rows_each"]

    def left(own_ref, got_ref):
        turned_ref[:, :tokens] = own_ref[...].astype(f32).T
        turned_ref[:, tokens:] = got_ref[...].astype(f32).T
        rows = [
            turned_ref[pl.ds(pl.multiple_of((2 * i + core) * rows_each, rows_each), rows_each), :]
            for i in range(width // (2 * rows_each))
        ]
        return jnp.concatenate(rows, axis=0).astype(bf16)

    second = left(second_ref, second_got_ref)
    for at in range(0, spread, WIDE):
        band = slice(at, at + WIDE)
        total_ref[:, band] = dot(
            second, jnp.concatenate([expanded_ref[:, band], expanded_got_ref[:, band]], axis=0)
        )
    mixed = left(mixed_ref, mixed_got_ref)
    total_ref[:, spread:] = dot(
        mixed, jnp.concatenate([mix_ref[...], mix_got_ref[...]], axis=0)
    )
    cut_out(refs[:-2], total_ref, place_ref, **cutting)


def outer_call(kernel, place, operands, rows, columns, bands, steps, size, axis, cut, scratch, name):
    rows_each = rows // size
    shape = (rows_each, columns // 2)
    low = (cut, shape[1]) if axis == 0 else (shape[0], cut)
    high = (shape[0] - cut, shape[1]) if axis == 0 else (shape[0], shape[1] - cut)
    pairs = (2,) * (len(steps) - 1)
    return pl.pallas_call(
        functools.partial(
            kernel,
            cutting=dict(bands=bands, steps=steps, rows_each=rows_each, axis=axis, cut=cut),
        ),
        out_shape=(
            jax.ShapeDtypeStruct((2,) + pairs + shape, bf16),
            jax.ShapeDtypeStruct(pairs + low, bf16),
            jax.ShapeDtypeStruct(pairs + high, bf16),
        ),
        in_specs=[pl.BlockSpec(memory_space=pltpu.SMEM)] + [vmem_spec()] * len(operands),
        out_specs=(vmem_spec(),) * 3,
        scratch_shapes=scratch + [pltpu.VMEM((rows // 2, columns), f32)],
        compiler_params=params(OUTER_MIB),
        cost_estimate=cost(2 << 30, 10 << 20),
        name=name,
    )(place, *operands)


def settle_kernel(place_ref, *refs):
    out = refs[-1]
    for k, ref in enumerate(refs[:-1]):
        out[place_ref[0] ^ k] = ref[...]


def settle_call(place, blocks):
    return pl.pallas_call(
        settle_kernel,
        out_shape=jax.ShapeDtypeStruct((len(blocks),) + blocks[0].shape, blocks[0].dtype),
        in_specs=[pl.BlockSpec(memory_space=pltpu.SMEM)] + [vmem_spec()] * len(blocks),
        out_specs=vmem_spec(),
        compiler_params=params(8),
        name="settle",
    )(place, *blocks)


def joined_slots_kernel(*refs, held):
    sources, outs = refs[:held], refs[held:]
    last = len(outs)
    for u, out in enumerate(outs):
        out[0] = sum(ref[u].astype(f32) for ref in sources).astype(bf16)
        out[1] = sum(ref[last].astype(f32) for ref in sources).astype(bf16)


def joined_slots_call(held, slots):
    _, rows, wide = held[0].shape
    return pl.pallas_call(
        functools.partial(joined_slots_kernel, held=len(held)),
        out_shape=(jax.ShapeDtypeStruct((2, rows, wide), bf16),) * slots,
        in_specs=[vmem_spec()] * len(held),
        out_specs=(vmem_spec(),) * slots,
        compiler_params=params(4),
        name="joined_slots",
    )(*held)


def heads_kernel(place_ref, *refs, groups, gains):
    joined_out, gains_out, held_ref = refs[-3:]
    pieces = refs[:-3]
    sums = []
    for u, ref in enumerate(pieces):
        held_ref[place_ref[1] ^ u] = ref[0].astype(f32)
        sums.append(ref[1].astype(f32))
    piece = pieces[0].shape[2] // 3
    for part in range(3):
        for g in range(groups):
            start = (part * groups + g) * piece
            joined_out[:, start : start + piece] = held_ref[
                g, :, part * piece : (part + 1) * piece
            ]
    while len(sums) > 1:
        sums = [sums[i] + sums[i + 1] for i in range(0, len(sums), 2)]
    wide = 3 * piece
    for r in range(-(-gains // wide)):
        end = min((r + 1) * wide, gains)
        gains_out[:, r * wide : end] = sums[0][r : r + 1, : end - r * wide]


def heads_call(place, blocks, width, gains):
    _, rows, wide = blocks[0].shape
    return pl.pallas_call(
        functools.partial(heads_kernel, groups=3 * width // wide, gains=gains),
        out_shape=(
            jax.ShapeDtypeStruct((rows, 3 * width), f32),
            jax.ShapeDtypeStruct((1, gains), f32),
        ),
        in_specs=[pl.BlockSpec(memory_space=pltpu.SMEM)] + [vmem_spec()] * len(blocks),
        out_specs=(vmem_spec(),) * 2,
        scratch_shapes=[pltpu.VMEM((len(blocks), rows, wide), f32)],
        compiler_params=params(8),
        name="heads_side_by_side",
    )(place, *blocks)


def input_kernel(*refs, planes, parts):
    inputs = refs[:planes]
    refs = refs[planes:]
    grad_ref, gain_ref = refs[:2]
    grad = sum(ref[at].astype(f32) for ref, at in zip(refs[2 : 2 + len(parts)], parts))
    outs = refs[2 + len(parts) :]
    normal, rate = normalized(
        jnp.concatenate([block[...] for block in inputs], axis=0).astype(f32)
    )
    value = grad_ref[...] + norm_back(normal, rate, grad * gain_ref[...])
    seg = value.shape[0] // planes
    for k in range(planes):
        outs[k][...] = value[k * seg : (k + 1) * seg, :].astype(bf16)


def input_call(inputs, grad_middle, gain, held, parts):
    planes = len(inputs)
    tokens, width = grad_middle.shape
    return pl.pallas_call(
        functools.partial(input_kernel, planes=planes, parts=parts),
        out_shape=(jax.ShapeDtypeStruct((tokens // planes, width), bf16),) * planes,
        in_specs=[vmem_spec()] * (2 + planes + len(held)),
        out_specs=(vmem_spec(),) * planes,
        compiler_params=params(16),
        name="input_back",
    )(*inputs, grad_middle, gain, *held)


def swap(value, axis, bits):
    size = lax.axis_size(axis)
    return lax.ppermute(value, axis, [(i, i ^ bits) for i in range(size)])


def pick(value, index, axis=0):
    return lax.dynamic_index_in_dim(value, index, axis, keepdims=False)


def in_hbm(*values):
    return [pltpu.with_memory_space_constraint(value, pltpu.HBM) for value in values]


def bits_of(size):
    return size.bit_length() - 1


def sums_kernel(*refs, listed, together):
    outs = refs[-1:] if together else refs[-len(listed) :]
    start = 0
    for i, terms in enumerate(listed):
        value = sum(refs[j][at].astype(f32) for j, at in terms).astype(bf16)
        if together:
            end = start + value.shape[together]
            outs[0][(..., slice(start, end)) + (slice(None),) * (-1 - together)] = value
            start = end
        else:
            outs[i][...] = value


def sums_call(sums, name, together=0):
    arrays, listed, shapes = [], [], []
    for terms in sums:
        entry = []
        for array, at in terms:
            where = [i for i, held in enumerate(arrays) if held is array]
            if not where:
                arrays.append(array)
                where = [len(arrays) - 1]
            entry.append((where[0], at))
        listed.append(entry)
        shapes.append(jax.eval_shape(lambda v, at=terms[0][1]: v[at], terms[0][0]).shape)
    if together:
        shape = list(shapes[0])
        shape[together] = sum(shape[together] for shape in shapes)
        shapes = [tuple(shape)]
    outs = pl.pallas_call(
        functools.partial(sums_kernel, listed=listed, together=together),
        out_shape=tuple(jax.ShapeDtypeStruct(shape, bf16) for shape in shapes),
        in_specs=[vmem_spec()] * len(arrays),
        out_specs=(vmem_spec(),) * len(shapes),
        compiler_params=params(4),
        name=name,
    )(*arrays)
    return outs[0] if together or len(shapes) == 1 else outs


class Halves:
    def __init__(self):
        self.entries = []
        self.chosen = {}

    def hold(self, array, names, bands=()):
        self.entries.append((array, names, dict(bands)))

    def terms(self, choice=()):
        chosen = dict(self.chosen)
        chosen.update(choice)
        return [
            (
                array,
                tuple(chosen[n] if n in chosen else bands.get(n, slice(None)) for n in names),
            )
            for array, names, bands in self.entries
        ]

    def receive(self, name, array, bands=()):
        self.chosen[name] = 0
        names = [n for n in self.entries[0][1] if n not in self.chosen]
        self.hold(array, names, bands)


def sides_kernel(place_ref, own_ref, other_ref, *outs):
    first = place_ref[3] == 0
    own, other = own_ref[...].astype(f32), other_ref[...].astype(f32)
    low, high = jnp.where(first, own, other), jnp.where(first, other, own)
    start = 0
    for out in outs:
        wide = out.shape[1] // 2
        out[:, :wide] = low[:, start : start + wide]
        out[:, wide:] = high[:, start : start + wide]
        start += wide


def sides_call(place, own, other, widths, name):
    rows = own.shape[0]
    return pl.pallas_call(
        sides_kernel,
        out_shape=tuple(jax.ShapeDtypeStruct((rows, wide), f32) for wide in widths),
        in_specs=[pl.BlockSpec(memory_space=pltpu.SMEM)] + [vmem_spec()] * 2,
        out_specs=(vmem_spec(),) * len(widths),
        compiler_params=params(8),
        name=name,
    )(place, own, other)


def per_device(
    layer_input, cotangent, doc_lengths, joined_weight, merge_weight, expand_weight,
    shrink_weight, first_gain, mixed_gain, second_gain, hidden_gain,
):
    _, planes, seg, width = layer_input.shape
    size = lax.axis_size("blk")
    slots = size // planes
    batches = lax.axis_size("batch")
    rank = lax.axis_index("blk")
    group_rank = lax.axis_index("batch")
    plane = rank // slots
    slot = rank % slots
    head_count = width // HEAD
    heads = -(-head_count // slots)
    groups = head_count // heads
    piece = heads * HEAD
    tokens = planes * seg
    length = slots * tokens
    side = group_rank % 2
    place = jnp.stack([plane, slot, rank, side]).astype(jnp.int32)

    def to_planes(blocks):
        return [pick(blocks, plane)] + [
            swap(pick(blocks, plane ^ k), "blk", k * slots) for k in range(1, planes)
        ]

    def all_slots(value):
        held = {0: value}
        for bit in reversed(range(bits_of(slots))):
            held.update({u | 1 << bit: swap(v, "blk", 1 << bit) for u, v in held.items()})
        return [held[u] for u in range(slots)]

    def over_slots(blocks):
        return [blocks[0]] + [swap(blocks[u], "blk", u) for u in range(1, slots)]

    spread = expand_weight.shape[1]
    first_arrived = to_planes(layer_input[0])
    own_start = jnp.minimum(slot, groups - 1) * piece
    own_weight = jnp.concatenate(
        [
            lax.dynamic_slice_in_dim(joined_weight, part * width + own_start, piece, 1)
            for part in range(3)
        ],
        axis=1,
    )
    lengths = doc_lengths[0]
    gain_row = first_gain.reshape(1, width)
    mixed_gain = mixed_gain.reshape(groups, 1, piece)
    second_gain = second_gain.reshape(1, width)
    hidden_gain = hidden_gain.reshape(1, spread)
    (
        first_arrived[1], place, lengths, gain_row, mixed_gain, second_gain, hidden_gain, own_weight,
    ) = lax.optimization_barrier(
        (
            first_arrived[1], place, lengths, gain_row, mixed_gain, second_gain, hidden_gain,
            own_weight,
        )
    )
    pieces = [all_slots(block) for block in first_arrived]
    (first, joined, factor), sent, shares = forward_call(
        place, lengths, gain_row, own_weight, pieces
    )
    sent, cotangent = lax.optimization_barrier((sent, cotangent))
    cotangent_blocks = to_planes(cotangent[0])
    (
        mixed, middle, second, hidden, hidden_give, normal, slope, held, mixed_rate, hidden_rate,
    ) = widen_call(
        place, over_slots(sent), first_arrived, mixed_gain, second_gain, hidden_gain, merge_weight,
        expand_weight,
    )
    hidden_give, cotangent_blocks = lax.optimization_barrier((hidden_give, cotangent_blocks))
    branch = branch_call(place, lengths, cotangent_blocks, slots)

    row_bits = list(range(1, bits_of(slots)))
    plane_bits = list(range(bits_of(slots), bits_of(size)))
    names = ["side"] + row_bits + plane_bits + ["rows", "columns"]
    steps = [0] + row_bits + plane_bits
    orders = (["side"] + row_bits, row_bits + ["side"])
    stages = len(orders[0])

    def cross(name, value):
        return swap(value, "batch", 1) if name == "side" else swap(value, "blk", 1 << name)

    def chains(axis, cut, whole):
        pair = [Halves(), Halves()]
        for chain, band in zip(pair, (slice(0, cut), slice(cut, None))):
            chain.hold(whole, names, {axis: band})
        return pair

    def sends(pair, at):
        return sums_call(
            [chain.terms({order[at]: 1}) for chain, order in zip(pair, orders)], "next_halves"
        )

    def crossed(at, values):
        return [cross(order[at], value) for order, value in zip(orders, values)]

    def arrive(pair, at, values):
        for chain, order, value in zip(pair, orders, values):
            chain.receive(order[at], value)

    def plane_depart(pair, bit, axis):
        together = -2 if axis == "rows" else -1
        return cross(
            bit, sums_call([chain.terms({bit: 1}) for chain in pair], "plane_halves", together)
        )

    def plane_arrive(pair, bit, axis, both):
        cut = pair[0].entries[0][2][axis].stop
        for chain, band in zip(pair, (slice(0, cut), slice(cut, None))):
            chain.receive(bit, both, {axis: band})

    def closed(pair, axis):
        together = -2 if axis == "rows" else -1
        value = sums_call([chain.terms() for chain in pair], "last_halves", together)
        for bit in range(1, bits_of(batches)):
            value = sums_call([[(value, ...), (swap(value, "batch", 1 << bit), ...)]], "groups")
        return value, swap(value, "batch", 1)

    cut = spread // size // 2
    shrink_whole, *shrink_firsts = outer_call(
        shrink_kernel, place,
        [hidden, branch, swap(hidden_give, "blk", 1), swap(branch, "blk", 1)],
        spread, width, ((0, width // 2),), steps, size, 0, cut, [], "shrink_outer",
    )
    shrink_sent = crossed(0, shrink_firsts)
    second_got, mixed_got = swap(second, "blk", 1), swap(mixed, "blk", 1)
    (expanded, mix, grad_middle, parts), away, results = turn_call(
        place, branch, normal, slope, middle, held, mixed_rate, hidden_rate,
        mixed_gain, second_gain, hidden_gain, merge_weight, shrink_weight, expand_weight, planes,
    )
    shrink_sent, second_got, mixed_got, expanded, mix = lax.optimization_barrier(
        (shrink_sent, second_got, mixed_got, expanded, mix)
    )
    shrink_chains = chains("rows", cut, shrink_whole)
    arrive(shrink_chains, 0, shrink_sent)

    returned = over_slots(away)
    expanded_got, mix_got = swap(expanded, "blk", 1), swap(mix, "blk", 1)
    returned, expanded_got, mix_got = lax.optimization_barrier((returned, expanded_got, mix_got))
    cut = ((spread + width) // 4 + 127) // 128 * 128
    expand_whole, *expand_firsts = outer_call(
        expand_kernel, place,
        [second, mixed, second_got, mixed_got, expanded, mix, expanded_got, mix_got],
        width, spread + width, ((0, spread // 2), (spread, width // 2)), steps, size, 1, cut,
        [pltpu.VMEM((width, 2 * tokens), f32)], "expand_outer",
    )
    for at in range(1, stages):
        shrink_sent = crossed(at, sends(shrink_chains, at))
        if at < stages - 1:
            arrive(shrink_chains, at, shrink_sent)
    expand_firsts, results = lax.optimization_barrier((expand_firsts, results))
    result_blocks = [results[0]] + [
        swap(results[k], "blk", k * slots) for k in range(1, planes)
    ]
    returned, expand_firsts, shrink_sent = lax.optimization_barrier(
        (returned, expand_firsts, shrink_sent)
    )
    arrive(shrink_chains, stages - 1, shrink_sent)
    expand_sent = crossed(0, expand_firsts)
    shrink_both = plane_depart(shrink_chains, plane_bits[0], "rows")
    joined_keep, joined_give, branch_keep, branch_give = backward_call(
        place, first, joined, factor, own_weight, gain_row, parts, returned, shares, planes
    )
    (
        joined_give, branch_give, shrink_both, expand_sent, result_blocks,
    ) = lax.optimization_barrier(
        (joined_give, branch_give, shrink_both, expand_sent, result_blocks)
    )
    plane_arrive(shrink_chains, plane_bits[0], "rows", shrink_both)
    expand_chains = chains("columns", cut, expand_whole)
    arrive(expand_chains, 0, expand_sent)

    joined_got = swap(joined_give, "blk", 1 << plane_bits[0])
    branch_got = swap(branch_give, "blk", 1)
    for at in range(1, stages):
        expand_sent = crossed(at, sends(expand_chains, at))
        if at < stages - 1:
            arrive(expand_chains, at, expand_sent)
    for bit in plane_bits[1:]:
        shrink_both = plane_depart(shrink_chains, bit, "rows")
        if bit != plane_bits[-1]:
            plane_arrive(shrink_chains, bit, "rows", shrink_both)
    branch_held, prefixes = [branch_keep, branch_got], [(), ()]
    for bit in row_bits:
        give = sums_call(
            [[(v, p + (1,)) for v, p in zip(branch_held, prefixes)]], "branch_halves"
        )
        prefixes = [p + (0,) for p in prefixes] + [()]
        branch_held.append(swap(give, "blk", 1 << bit))
    joined_got, branch_held[-1], expand_sent, shrink_both = lax.optimization_barrier(
        (joined_got, branch_held[-1], expand_sent, shrink_both)
    )
    arrive(expand_chains, stages - 1, expand_sent)
    plane_arrive(shrink_chains, plane_bits[-1], "rows", shrink_both)

    expand_both = plane_depart(expand_chains, plane_bits[0], "columns")
    joined_terms = [(joined_keep, 0), (joined_got, 0)]
    blocks = planes * slots // 2
    gain_terms = [(joined_give, blocks), (joined_got, blocks)]
    for bit in plane_bits[1:]:
        blocks //= 2
        joined_give = sums_call(
            [
                [(v, slice(start + blocks, start + 2 * blocks)) for v, start in joined_terms],
                [(v, slice(at, at + 1)) for v, at in gain_terms],
            ],
            "joined_halves", -3,
        )
        joined_got = swap(joined_give, "blk", 1 << bit)
        joined_terms.append((joined_got, 0))
        gain_terms = [(joined_give, blocks), (joined_got, blocks)]
    input_blocks = input_call(
        first_arrived, grad_middle, gain_row, branch_held, prefixes
    )
    input_blocks = [input_blocks[0]] + [
        swap(input_blocks[k], "blk", k * slots) for k in range(1, planes)
    ]
    joined_last = sums_call(
        [
            [(v, slice(start, start + slots)) for v, start in joined_terms],
            [(v, slice(at, at + 1)) for v, at in gain_terms],
        ],
        "joined_last", -3,
    )
    held = [joined_last]
    for bit in range(bits_of(batches)):
        if len(held) > 1:
            held = [sums_call([[(v, ...) for v in held]], "joined_groups")]
        held.append(swap(held[0], "batch", 1 << bit))
    joined_sent = joined_slots_call(held, slots)
    joined_grad, gain_grads = heads_call(
        place,
        [joined_sent[0]] + [swap(joined_sent[u], "blk", u) for u in range(1, slots)],
        width, 3 * width + spread,
    )
    shrink_grad, = sides_call(place, *closed(shrink_chains, "rows"), (width,), "shrink_sides")
    plane_arrive(expand_chains, plane_bits[0], "columns", expand_both)
    for bit in plane_bits[1:]:
        expand_both = plane_depart(expand_chains, bit, "columns")
        plane_arrive(expand_chains, bit, "columns", expand_both)
    expand_grad, merge_grad = sides_call(
        place, *closed(expand_chains, "columns"), (spread, width), "expand_sides"
    )
    layer_result = settle_call(place, result_blocks).reshape(layer_input.shape)
    input_grad = settle_call(place, input_blocks).reshape(layer_input.shape)
    gain_grads = gain_grads[0]
    return (
        layer_result, input_grad, joined_grad, merge_grad, expand_grad,
        shrink_grad, gain_grads[:width], gain_grads[width : 2 * width],
        gain_grads[2 * width : 3 * width], gain_grads[3 * width :],
    )


def solution(mesh):
    rows = P("batch", None, "blk", None)
    return jax.shard_map(
        per_device,
        mesh=mesh,
        in_specs=(rows, rows, P("batch", None, None)) + (P(),) * 8,
        out_specs=(rows, rows) + (P("blk", None),) * 4 + (P(),) * 4,
        check_vma=False,
    )
```
